32 devices in a mesh: dp: 8 (over y, x, core), pipe: 4 (over z).
Axes of the slice: x: 2, y: 2, z: 4, core: 2. Of those that a mesh axis runs over, the one named last changes fastest.
Arguments:
- hidden_in: bfloat16 [32, 256, 512], P(('dp', 'pipe')), may hold values from -6 to 6
- segment_ids: int32 [32, 256], P(('dp', 'pipe')), may hold values from 0 to 3, as said below
- task_ids: int32 [32, 4], P(('dp', 'pipe')), may hold values from 0 to 3
- labels: int32 [32, 4], P(('dp', 'pipe')), may hold values from 0 to 2
- cotangent: bfloat16 [32, 256, 512], P(('dp', 'pipe')), may hold values from -6 to 6
- qkv_weight: bfloat16 [4, 512, 1536], P('pipe'), may hold values from -0.25 to 0.25
- qv_bias: float32 [4, 1024], P('pipe'), may hold values from -1.5 to 1.5
- out_weight: bfloat16 [4, 512, 512], P('pipe'), may hold values from -0.75 to 0.75
- out_bias: float32 [4, 512], P('pipe'), may hold values from -1.5 to 1.5
- norm1_gain: float32 [4, 512], P('pipe'), may hold values from 0.5 to 1.5
- norm1_bias: float32 [4, 512], P('pipe'), may hold values from -1.5 to 1.5
- ffn_in_weight: bfloat16 [4, 512, 2048], P('pipe'), may hold values from -0.25 to 0.25
- ffn_in_bias: float32 [4, 2048], P('pipe'), may hold values from -1.5 to 1.5
- ffn_out_weight: bfloat16 [4, 2048, 512], P('pipe'), may hold values from -0.125 to 0.125
- ffn_out_bias: float32 [4, 512], P('pipe'), may hold values from -1.5 to 1.5
- norm2_gain: float32 [4, 512], P('pipe'), may hold values from 0.5 to 1.5
- norm2_bias: float32 [4, 512], P('pipe'), may hold values from -1.5 to 1.5
- head_weight: float32 [4, 512, 3], replicated, may hold values from -0.5 to 0.5
- head_bias: float32 [4, 3], replicated, may hold values from -4 to 4
Outputs:
- hidden_out: bfloat16 [32, 256, 512], P(('dp', 'pipe'))
- task_loss: float32 [32, 4], P(('dp', 'pipe'))
- hidden_grad: bfloat16 [32, 256, 512], P(('dp', 'pipe'))
- qkv_weight_grad: float32 [4, 512, 1536], P('pipe')
- qv_bias_grad: float32 [4, 1024], P('pipe')
- out_weight_grad: float32 [4, 512, 512], P('pipe')
- out_bias_grad: float32 [4, 512], P('pipe')
- norm1_gain_grad: float32 [4, 512], P('pipe')
- norm1_bias_grad: float32 [4, 512], P('pipe')
- ffn_in_weight_grad: float32 [4, 512, 2048], P('pipe')
- ffn_in_bias_grad: float32 [4, 2048], P('pipe')
- ffn_out_weight_grad: float32 [4, 2048, 512], P('pipe')
- ffn_out_bias_grad: float32 [4, 512], P('pipe')
- norm2_gain_grad: float32 [4, 512], P('pipe')
- norm2_bias_grad: float32 [4, 512], P('pipe')
- head_weight_grad: float32 [4, 512, 3], replicated
- head_bias_grad: float32 [4, 3], replicated
The draws below stay inside these ranges and needn't reach their ends.
Inputs may be any that keep to these rules, and one draw needn't show every extreme that they name: `segment_ids`: in each row the pair numbers start at 0 and never fall, each pair has one or more positions; a row holds 1 to 4 pairs, row 0 a single pair of 256 positions and row 1 exactly 4 pairs.
All inputs are finite; a program needn't handle non-finite values.
Results may differ from the reference program's by a relative error of at most 0.02.
Values may be sent and summed in bfloat16 or wider, within the bound.
No kernel may reach another device: no remote copies, remote signals or barrier semaphores. Data moves between devices by JAX's collectives and lax.ppermute only.
A program may use at most 192 MiB of HBM per device.

```python
import math
import jax
import jax.numpy as jnp
from jax import lax

D = 512
HEADS = 8
HD = 64
FF = 2048
SLOT = 256
SEGS = 4
TASKS = 4
CLASSES = 3
LAYERS = 4
ROWS = 32


def shuffled_cuts(row_key):
    return jax.random.permutation(row_key, SLOT - 1) + 1


def draw_segment_ids(key, part):
    key = jax.random.fold_in(key, 11)
    count_key, order_key = jax.random.split(key)
    counts = jax.random.randint(count_key, (ROWS,), 1, SEGS + 1)
    row_numbers = jnp.arange(ROWS)
    counts = jnp.where(row_numbers == 0, 1, jnp.where(row_numbers == 1, SEGS, counts))
    row_keys = jax.random.split(order_key, ROWS)
    orders = jax.vmap(shuffled_cuts)(row_keys)
    cuts = orders[:, :SEGS - 1]
    used = jnp.arange(SEGS - 1)[None, :] < counts[:, None] - 1
    positions = jnp.arange(SLOT)
    passed = (cuts[:, :, None] <= positions[None, None, :]) & used[:, :, None]
    return jnp.sum(passed.astype(jnp.int32), axis=1).astype(jnp.int32)


def place_ends(drawn, rng, least, largest):
    extent = drawn.shape
    index_at = [jax.random.randint(jax.random.fold_in(rng, axis), (), 0, extent[axis]) for axis in range(len(extent))]
    drawn = drawn.at[tuple(index_at)].set(least)
    longest = extent.index(max(extent))
    index_at[longest] = (index_at[longest] + 1) % extent[longest]
    return drawn.at[tuple(index_at)].set(largest)


def level_of(rng, extent, shards, low, largest):
    def one(dim, blocks):
        steps = jax.random.uniform(jax.random.fold_in(jax.random.fold_in(rng, 6), dim), (blocks,), jnp.float32, low / len(shards), largest / len(shards))
        return jnp.repeat(jnp.exp(steps), extent[dim] // blocks).reshape((-1,) + (1,) * (len(extent) - dim - 1))

    level = one(*shards[0])
    for cut in shards[1:]:
        level = level * one(*cut)
    return level


def bell_draw(key, dims, scale, most, cuts=(), held_as=jnp.bfloat16):
    loudness = level_of(key, dims, cuts, -0.22, 0.18) if cuts else 1.0
    array = jax.random.normal(key, dims, jnp.float32) * scale * loudness
    return jnp.minimum(jnp.maximum(array, -most), most).astype(held_as)


def setup_inputs(seed: int = 0) -> dict:
    key_of = jax.random.split(jax.random.key(seed), 20)
    return {
        "hidden_in": bell_draw(key_of[0], (ROWS, SLOT, D), 1.0, 6.0, ((0, 32),)),
        "segment_ids": draw_segment_ids(jax.random.fold_in(key_of[19], 71), 0),
        "task_ids": place_ends(jax.random.randint(key_of[2], (ROWS, SEGS), 0, TASKS), jax.random.fold_in(key_of[2], 1), 0, TASKS - 1).astype(jnp.int32),
        "labels": place_ends(jax.random.randint(key_of[3], (ROWS, SEGS), 0, CLASSES), jax.random.fold_in(key_of[3], 1), 0, CLASSES - 1).astype(jnp.int32),
        "cotangent": bell_draw(key_of[4], (ROWS, SLOT, D), 1.0, 6.0, ((0, 32),)),
        "qkv_weight": bell_draw(key_of[5], (LAYERS, D, 3 * D), D ** -0.5, 0.25, ((0, 4),)),
        "qv_bias": bell_draw(key_of[6], (LAYERS, 2 * D), 0.3, 1.5, ((0, 4),), jnp.float32),
        "out_weight": bell_draw(key_of[7], (LAYERS, D, D), (D // 8) ** -0.5, 0.75, ((0, 4),)),
        "out_bias": bell_draw(key_of[8], (LAYERS, D), 0.3, 1.5, ((0, 4),), jnp.float32),
        "norm1_gain": jnp.clip(1.0 + 0.1 * jax.random.normal(key_of[9], (LAYERS, D), jnp.float32), 0.5, 1.5),
        "norm1_bias": bell_draw(key_of[10], (LAYERS, D), 0.3, 1.5, ((0, 4),), jnp.float32),
        "ffn_in_weight": bell_draw(key_of[11], (LAYERS, D, FF), D ** -0.5, 0.25, ((0, 4),)),
        "ffn_in_bias": bell_draw(key_of[12], (LAYERS, FF), 0.3, 1.5, ((0, 4),), jnp.float32),
        "ffn_out_weight": bell_draw(key_of[13], (LAYERS, FF, D), FF ** -0.5, 0.125, ((0, 4),)),
        "ffn_out_bias": bell_draw(key_of[14], (LAYERS, D), 0.3, 1.5, ((0, 4),), jnp.float32),
        "norm2_gain": jnp.clip(1.0 + 0.1 * jax.random.normal(key_of[15], (LAYERS, D), jnp.float32), 0.5, 1.5),
        "norm2_bias": bell_draw(key_of[16], (LAYERS, D), 0.3, 1.5, ((0, 4),), jnp.float32),
        "head_weight": bell_draw(key_of[17], (TASKS, D, CLASSES), (D // 4) ** -0.5, 0.5, (), jnp.float32),
        "head_bias": bell_draw(key_of[18], (TASKS, CLASSES), 1.0, 4.0, (), jnp.float32),
    }


HIGH = lax.Precision.HIGHEST
EPS = 1e-12
NEG = -1000000000.0

@jax.custom_vjp
def low(v):
    return lax.optimization_barrier(v.astype(jnp.bfloat16)).astype(jnp.float32)

@jax.custom_vjp
def low_back(v):
    return v

def low_keep(v):
    return (low(v), None)

def low_pass(kept, grad):
    return (grad,)

def back_keep(v):
    return (v, None)

def back_low(kept, grad):
    return (low(grad),)
low.defvjp(low_keep, low_pass)
low_back.defvjp(back_keep, back_low)

def norm_rows(values, gain, shift):
    centre = values - lax.optimization_barrier(jnp.mean(values, axis=-1, keepdims=True))
    spread = lax.optimization_barrier(jnp.mean(centre * centre, axis=-1, keepdims=True))
    return centre * lax.rsqrt(spread + EPS) * gain + shift

def gelu_exact(values):
    return jax.nn.gelu(values, approximate=False)

def task_losses(seg_rows, task_rows, label_rows, final_rows, head_w, head_b):
    seg_count = task_rows.shape[1]
    task_count, class_count = head_b.shape
    previous = jnp.concatenate([jnp.full_like(seg_rows[:, :1], -1), seg_rows[:, :-1]], axis=1)
    starts = seg_rows != previous
    numbers = lax.broadcasted_iota(jnp.int32, (1, seg_count, 1), 1)
    cls_pick = ((seg_rows[:, None, :] == numbers) & starts[:, None, :]).astype(jnp.float32)
    live_segs = lax.optimization_barrier(jnp.max(cls_pick, axis=2))
    cls_rows = jnp.einsum('rgs,rsd->rgd', cls_pick, final_rows, precision=HIGH)
    all_logits = jnp.einsum('rgd,tdc->rgtc', cls_rows, head_w, precision=HIGH) + head_b
    chosen = (task_rows[..., None] == lax.broadcasted_iota(jnp.int32, (1, 1, task_count), 2)).astype(jnp.float32)
    logits = lax.optimization_barrier(jnp.sum(all_logits * chosen[..., None], axis=2))
    row_top = lax.optimization_barrier(jnp.max(logits, axis=-1, keepdims=True))
    log_total = row_top[..., 0] + jnp.log(lax.optimization_barrier(jnp.sum(jnp.exp(logits - row_top), axis=-1)))
    label_hot = (label_rows[..., None] == lax.broadcasted_iota(jnp.int32, (1, 1, class_count), 2)).astype(jnp.float32)
    right_logit = lax.optimization_barrier(jnp.sum(logits * label_hot, axis=-1))
    return live_segs * (log_total - right_logit)

def layer_forward(activations, seg_row, weights):
    qkv_w, qv_b, out_w, out_b, gain_one, shift_one, in_w, in_b, down_w, down_b, gain_two, shift_two = weights
    seq_len = activations.shape[0]
    mixed_proj = jnp.dot(activations, qkv_w, precision=HIGH)
    queries = low(low_back(mixed_proj[:, :D] + qv_b[:D])).reshape(seq_len, HEADS, HD)
    key_rows = low(low_back(mixed_proj[:, D:2 * D])).reshape(seq_len, HEADS, HD)
    values = low(low_back(mixed_proj[:, 2 * D:] + qv_b[D:])).reshape(seq_len, HEADS, HD)
    raw_scores = low_back(jnp.einsum('qhd,khd->hqk', queries, key_rows, precision=HIGH))
    allowed = seg_row[:, None] == seg_row[None, :]
    scores = jnp.where(allowed[None], raw_scores * (1.0 / math.sqrt(HD)), NEG)
    row_top = lax.optimization_barrier(jnp.max(scores, axis=-1, keepdims=True))
    expo = jnp.exp(scores - row_top)
    attn_probs = expo / lax.optimization_barrier(jnp.sum(expo, axis=-1, keepdims=True))
    context = jnp.einsum('hqk,khd->qhd', low(attn_probs), values, precision=HIGH).reshape(seq_len, D)
    context = low(low_back(context))
    resid = activations + low_back(jnp.dot(context, out_w, precision=HIGH) + out_b)
    normed = norm_rows(resid, gain_one, shift_one)
    hidden_pre = low_back(jnp.dot(low(normed), in_w, precision=HIGH) + in_b)
    hidden_low = low(gelu_exact(hidden_pre))
    summed = normed + low_back(jnp.dot(hidden_low, down_w, precision=HIGH) + down_b)
    return norm_rows(summed, gain_two, shift_two)

def reference(hidden_in, segment_ids, task_ids, labels, cotangent, qkv_weight, qv_bias, out_weight, out_bias, norm1_gain, norm1_bias, ffn_in_weight, ffn_in_bias, ffn_out_weight, ffn_out_bias, norm2_gain, norm2_bias, head_weight, head_bias):
    params = tuple((weight_item.astype(jnp.float32) for weight_item in (qkv_weight, qv_bias, out_weight, out_bias, norm1_gain, norm1_bias, ffn_in_weight, ffn_in_bias, ffn_out_weight, ffn_out_bias, norm2_gain, norm2_bias)))
    heads = (head_weight.astype(jnp.float32), head_bias.astype(jnp.float32))
    hidden_full = hidden_in.astype(jnp.float32)
    cot_full = cotangent.astype(jnp.float32)

    def objective_sum(layer_params, head_params, hidden_rows):

        def one_row(row_args):
            activations, seg_row, task_row, label_row, cot_row = row_args
            activations = low_back(activations)
            for layer_index in range(LAYERS):
                weights = tuple((weight_item[layer_index] for weight_item in layer_params))
                activations = low_back(low(layer_forward(activations, seg_row, weights)))
            losses = task_losses(seg_row[None], task_row[None], label_row[None], activations[None], head_params[0], head_params[1])[0]
            return (jnp.sum(cot_row * activations) + jnp.sum(losses), (activations, losses))
        row_values, (row_outs, row_losses) = lax.map(jax.checkpoint(one_row), (hidden_rows, segment_ids, task_ids, labels, cot_full))
        return (jnp.sum(row_values), (row_outs, row_losses))
    _, back_fn, (row_outs, row_losses) = jax.vjp(objective_sum, params, heads, hidden_full, has_aux=True)
    grad_params, grad_heads, grad_hidden = back_fn(jnp.ones((), jnp.float32))
    return (row_outs.astype(jnp.bfloat16), row_losses, grad_hidden.astype(jnp.bfloat16), grad_params[0], grad_params[1], grad_params[2], grad_params[3], grad_params[4], grad_params[5], grad_params[6], grad_params[7], grad_params[8], grad_params[9], grad_params[10], grad_params[11], grad_heads[0], grad_heads[1])
```

```python
from functools import partial

import jax
import jax.numpy as jnp
from jax import lax
from jax.experimental import pallas as pl
from jax.experimental.pallas import tpu as pltpu
from jax.sharding import PartitionSpec as P

HEADS = 8
EPS = 1e-12
NEG = -1000000000.0
EXTRA = 16
SMALL = 32
BLOCK = 512
F32 = jnp.float32
BF16 = jnp.bfloat16
VMEM = pl.BlockSpec(memory_space=pltpu.VMEM)
SMEM = pl.BlockSpec(memory_space=pltpu.SMEM)
ANY = pl.BlockSpec(memory_space=pl.ANY)
MIB = 1024 * 1024
QV_B, OUT_B, GAIN_ONE, SHIFT_ONE, IN_B, DOWN_B, GAIN_TWO, SHIFT_TWO = 0, 2, 3, 4, 5, 9, 10, 11


def mm(a, b):
    return lax.dot_general(a, b, (((1,), (0,)), ((), ())), preferred_element_type=F32)


def mm_nt(a, b):
    return lax.dot_general(a, b, (((1,), (1,)), ((), ())), preferred_element_type=F32)


def mm_tn(a, b):
    return lax.dot_general(a, b, (((0,), (0,)), ((), ())), preferred_element_type=F32)


def lane_masks(width):
    lanes = lax.broadcasted_iota(jnp.int32, (1, 2 * width), 1)
    return (lanes < width).astype(BF16), (lanes >= width).astype(BF16)


def segment_onehot(meta, count, seq_len):
    numbers = lax.broadcasted_iota(jnp.int32, (count, seq_len), 0).astype(F32)
    return (meta[0:1, :seq_len].astype(F32) == numbers).astype(F32)


def norm_stats(values):
    centre = values - jnp.mean(values, axis=-1, keepdims=True)
    spread = jnp.mean(centre * centre, axis=-1, keepdims=True)
    scale = lax.rsqrt(spread + EPS)
    return centre * scale, scale


def norm_back(grad, unit, scale, gain):
    scaled = grad * gain
    mean_one = jnp.mean(scaled, axis=-1, keepdims=True)
    mean_two = jnp.mean(scaled * unit, axis=-1, keepdims=True)
    return scale * (scaled - mean_one - unit * mean_two)


def column_sum(values):
    return jnp.sum(values.astype(F32), axis=0, keepdims=True)


def load_kernel(
    x_hbm, qkv_hbm, out_hbm, in_hbm, down_hbm, seg_ref, qv_b, out_b, gain_one, shift_one, in_b, down_b, gain_two, shift_two, head_ref,
    block_ref, qkv_ref, out_ref, in_ref, down_ref, vec_ref, head_w_ref, sems,
):
    seq_len = x_hbm.shape[1]
    width = x_hbm.shape[2]
    pairs = (
        (x_hbm.at[0], block_ref.at[:seq_len]), (qkv_hbm.at[0], qkv_ref), (out_hbm.at[0], out_ref), (in_hbm.at[0], in_ref),
        (down_hbm.at[0], down_ref),
    )
    copies = [pltpu.make_async_copy(src, dst, sems.at[i]) for i, (src, dst) in enumerate(pairs)]
    for copy in copies:
        copy.start()
    block_ref[seq_len:, :] = jnp.zeros((EXTRA, width), BF16)
    block_ref[seq_len:, :seq_len] = jnp.broadcast_to(seg_ref[...].astype(F32).astype(BF16), (EXTRA, seq_len))
    row = 0
    for vector in (qv_b, out_b, gain_one, shift_one, in_b, down_b, gain_two, shift_two):
        for part in range(vector.shape[1] // width):
            vec_ref[row : row + 1, :] = vector[:, part * width : (part + 1) * width]
            row += 1
    classes, tasks, _ = head_ref.shape
    head_w_ref[...] = jnp.zeros_like(head_w_ref)
    for c in range(classes):
        head_w_ref[c * tasks : (c + 1) * tasks, :] = head_ref[c]
    for copy in copies:
        copy.wait()


def forward_kernel(tick, stages, carry, fresh, info, x_ref, *refs):
    refs = list(refs)
    home_ref = refs.pop(0) if carry else None
    qkv_w, out_w, in_w, down_w, vec = refs[:5]
    refs = refs[5:]
    if not fresh:
        refs = refs[10:]
    y_ref, keep_ref, qkv_ref, probs_ref, context_ref, unit_one_ref, normed_ref, hidden_ref, slope_ref, unit_two_ref, scales_ref = refs
    seq_len = x_ref.shape[0] - EXTRA
    width = x_ref.shape[1]
    head_dim = width // HEADS
    place = tick - 2 * info[0]
    active = (place >= 0) & (place < stages)

    if carry:

        @pl.when(jnp.logical_not(active))
        def _():
            y_ref[...] = home_ref[...]

    @pl.when(active)
    def _():
        meta = x_ref[seq_len:, :]
        y_ref[seq_len:, :] = meta
        x = x_ref[:seq_len, :]
        keep_ref[...] = x
        onehot = segment_onehot(meta, EXTRA, seq_len).astype(BF16)
        allowed = mm_tn(onehot, onehot) > 0.5
        q = (mm(x, qkv_w[:, :width]) + vec[QV_B : QV_B + 1]).astype(BF16)
        k = mm(x, qkv_w[:, width : 2 * width]).astype(BF16)
        v = (mm(x, qkv_w[:, 2 * width :]) + vec[QV_B + 1 : QV_B + 2]).astype(BF16)
        qkv_ref[:, :width] = q
        qkv_ref[:, width : 2 * width] = k
        qkv_ref[:, 2 * width :] = v
        v_t = v.T
        mask_a, mask_b = lane_masks(head_dim)
        factor = head_dim**-0.5
        context_parts = []
        for pair in range(HEADS // 2):
            cols = slice(pair * 2 * head_dim, (pair + 1) * 2 * head_dim)
            for head, mask in ((2 * pair, mask_a), (2 * pair + 1, mask_b)):
                scores = mm_nt(k[:, cols], q[:, cols] * (mask * factor).astype(BF16))
                scores = jnp.where(allowed, scores, NEG)
                expo = jnp.exp(scores - jnp.max(scores, axis=0, keepdims=True))
                probs = (expo * (1.0 / jnp.sum(expo, axis=0, keepdims=True))).astype(BF16)
                probs_ref[:, head * seq_len : (head + 1) * seq_len] = probs
                context_parts.append(mm(v_t[head * head_dim : (head + 1) * head_dim, :], probs))
        context = jnp.concatenate(context_parts, axis=0).T.astype(BF16)
        context_ref[...] = context
        resid = x.astype(F32) + mm(context, out_w[...]) + vec[OUT_B : OUT_B + 1]
        unit_one, scale_one = norm_stats(resid)
        unit_one_ref[...] = unit_one
        normed = unit_one * vec[GAIN_ONE : GAIN_ONE + 1] + vec[SHIFT_ONE : SHIFT_ONE + 1]
        normed_low = normed.astype(BF16)
        normed_ref[...] = normed_low
        summed = normed + vec[DOWN_B : DOWN_B + 1]
        for part in range(in_w.shape[1] // BLOCK):
            cols = slice(part * BLOCK, (part + 1) * BLOCK)
            pre = mm(normed_low, in_w[:, cols]) + vec[IN_B + part : IN_B + part + 1]
            gate = 0.5 + 0.5 * lax.erf(pre * (0.5**0.5))
            slope_ref[:, cols] = (gate + pre * (jnp.exp(-0.5 * pre * pre) * 0.3989422804014327)).astype(BF16)
            hidden = (pre * gate).astype(BF16)
            hidden_ref[:, cols] = hidden
            summed = summed + mm(hidden, down_w[cols, :])
        unit_two, scale_two = norm_stats(summed)
        unit_two_ref[...] = unit_two
        y_ref[:seq_len, :] = (unit_two * vec[GAIN_TWO : GAIN_TWO + 1] + vec[SHIFT_TWO : SHIFT_TWO + 1]).astype(BF16)
        scales_ref[:, 0:128] = jnp.broadcast_to(scale_one, (seq_len, 128))
        scales_ref[:, 128:256] = jnp.broadcast_to(scale_two, (seq_len, 128))


def head_kernel(info, task_ref, label_ref, head_b_ref, *refs):
    stages = len(refs) - 6
    y_refs = refs[:stages]
    cot_ref, head_w, g_ref, final_ref, loss_ref, picked = refs[stages:]
    for s in range(stages):

        @pl.when(info[0] == s)
        def _(s=s):
            picked[...] = y_refs[s][...]

    seq_len, width = final_ref.shape
    task_count, class_count = head_b_ref.shape
    seg_count = task_ref.shape[1]
    high = lax.Precision.HIGHEST
    y = picked[:seq_len, :]
    final_ref[...] = y
    meta = picked[seq_len:, :]
    segs = 8
    onehot = segment_onehot(meta, segs, seq_len)
    row = meta[0:1, :seq_len].astype(F32)
    lanes = lax.broadcasted_iota(jnp.int32, (1, seq_len), 1)
    previous = jnp.where(lanes == 0, -1.0, pltpu.roll(row, 1, 1))
    pick = onehot * (row != previous).astype(F32)
    live = jnp.max(pick, axis=1, keepdims=True)
    cls = mm(pick.astype(BF16), y)
    logits = lax.dot_general(cls, head_w[...], (((1,), (1,)), ((), ())), precision=high, preferred_element_type=F32)
    slots = lax.broadcasted_iota(jnp.int32, (1, logits.shape[1]), 1)
    bias = jnp.zeros((1, logits.shape[1]), F32)
    for t in range(task_count):
        for c in range(class_count):
            bias = jnp.where(slots == c * task_count + t, head_b_ref[t, c], bias)
    logits = logits + bias
    numbers = lax.broadcasted_iota(jnp.int32, (segs, 1), 0)
    task = jnp.zeros((segs, 1), jnp.int32)
    label = jnp.zeros((segs, 1), jnp.int32)
    for s in range(seg_count):
        task = jnp.where(numbers == s, task_ref[0, s], task)
        label = jnp.where(numbers == s, label_ref[0, s], label)
    mine = jnp.zeros(logits.shape, jnp.bool_)
    for c in range(class_count):
        mine = mine | (slots == task + c * task_count)
    label_hot = slots == task + label * task_count
    masked = jnp.where(mine, logits, -jnp.inf)
    top = jnp.max(masked, axis=1, keepdims=True)
    expo = jnp.exp(masked - top)
    total = jnp.sum(expo, axis=1, keepdims=True)
    right = jnp.sum(jnp.where(label_hot, logits, 0.0), axis=1, keepdims=True)
    loss = live * (top + jnp.log(total) - right)
    wide = lax.broadcasted_iota(jnp.int32, (segs, 128), 1)
    loss_row = jnp.sum(jnp.where(wide == numbers, loss, 0.0), axis=0, keepdims=True)
    loss_ref[...] = loss_row[:, :seg_count]
    d_logits = live * (expo / total - label_hot.astype(F32))
    d_cls = lax.dot_general(d_logits, head_w[...], (((1,), (0,)), ((), ())), precision=high, preferred_element_type=F32)
    d_final = lax.dot_general(pick, d_cls, (((0,), (0,)), ((), ())), precision=high, preferred_element_type=F32)
    g_ref[:seq_len, :] = (cot_ref[...].astype(F32) + d_final).astype(BF16)
    g_w = lax.dot_general(d_logits, cls, (((0,), (0,)), ((), ())), precision=high, preferred_element_type=F32)
    g_b = jnp.concatenate([column_sum(d_logits)] * (width // logits.shape[1]), axis=1)
    rows = lax.broadcasted_iota(jnp.int32, (EXTRA, 1), 0)
    count = task_count * class_count
    g_ref[seq_len:, :] = jnp.where(rows < count, g_w[:EXTRA], jnp.where(rows == count, g_b, 0.0)).astype(BF16)


def backward_kernel(tick, stages, carry, fresh_proj, fresh_sums, info, g_ref, *refs):
    refs = list(refs)
    home_ref = refs.pop(0) if carry else None
    qkv_w, out_w, in_w, down_w, vec = refs[:5]
    qkv_ref, slope_ref, probs_ref, unit_one_ref, unit_two_ref, scales_ref = refs[5:11]
    refs = refs[11:]
    if not fresh_proj:
        refs = refs[2:]
    if not fresh_sums:
        refs = refs[1:]
    next_ref, d_mixed_ref, d_pre_ref, d_proj_ref, d_down_ref, sums_ref, queries = refs
    seq_len = g_ref.shape[0] - EXTRA
    width = g_ref.shape[1]
    head_dim = width // HEADS
    place = tick - 2 * info[0]
    active = (place >= 0) & (place < stages)

    if carry:

        @pl.when(jnp.logical_not(active))
        def _():
            next_ref[...] = home_ref[...]

    if fresh_sums:
        sums_ref[...] = jnp.zeros_like(sums_ref)

    @pl.when(active)
    def _():
        extra = g_ref[seq_len:, :]
        next_ref[seq_len:, :] = extra
        sums_ref[SMALL - EXTRA :, :] += extra.astype(F32)

        def add(row, value):
            sums_ref[row : row + 1, :] += value

        grad = g_ref[:seq_len, :].astype(F32)
        scale_one = scales_ref[:, 0:1]
        scale_two = scales_ref[:, 128:129]
        unit_two = unit_two_ref[...]
        add(GAIN_TWO, column_sum(grad * unit_two))
        add(SHIFT_TWO, column_sum(grad))
        d_summed = norm_back(grad, unit_two, scale_two, vec[GAIN_TWO : GAIN_TWO + 1])
        d_down = d_summed.astype(BF16)
        d_down_ref[...] = d_down
        add(DOWN_B, column_sum(d_down))
        d_normed = d_summed
        for part in range(in_w.shape[1] // BLOCK):
            cols = slice(part * BLOCK, (part + 1) * BLOCK)
            d_pre = (mm_nt(d_down, down_w[cols, :]) * slope_ref[:, cols].astype(F32)).astype(BF16)
            d_pre_ref[:, cols] = d_pre
            add(IN_B + part, column_sum(d_pre))
            d_normed = d_normed + mm_nt(d_pre, in_w[:, cols])
        unit_one = unit_one_ref[...]
        add(GAIN_ONE, column_sum(d_normed * unit_one))
        add(SHIFT_ONE, column_sum(d_normed))
        d_resid = norm_back(d_normed, unit_one, scale_one, vec[GAIN_ONE : GAIN_ONE + 1])
        d_proj = d_resid.astype(BF16)
        d_proj_ref[...] = d_proj
        add(OUT_B, column_sum(d_proj))
        d_context = mm_nt(d_proj, out_w[...]).astype(BF16)
        factor = head_dim**-0.5
        mask_a, mask_b = lane_masks(head_dim)
        queries[...] = qkv_ref[:, :width]
        keys = qkv_ref[:, width : 2 * width]
        k_t = (keys * jnp.asarray(factor, BF16)).T
        d_query_parts = []
        for pair in range(HEADS // 2):
            cols = slice(pair * 2 * head_dim, (pair + 1) * 2 * head_dim)
            q_cols = queries[:, cols]
            v_cols = qkv_ref[:, slice(cols.start + 2 * width, cols.stop + 2 * width)]
            d_values = 0.0
            d_keys = 0.0
            for head, mask in ((2 * pair, mask_a), (2 * pair + 1, mask_b)):
                d_context_head = d_context[:, cols] * mask
                probs = probs_ref[:, head * seq_len : (head + 1) * seq_len]
                d_probs = mm_nt(v_cols, d_context_head)
                probs_wide = probs.astype(F32)
                weighted = probs_wide * d_probs
                d_scores = (weighted - probs_wide * jnp.sum(weighted, axis=0, keepdims=True)).astype(BF16)
                d_values = d_values + mm(probs, d_context_head)
                d_keys = d_keys + mm(d_scores, q_cols * (mask * factor).astype(BF16))
                d_query_parts.append(mm(k_t[head * head_dim : (head + 1) * head_dim, :], d_scores))
            d_mixed_ref[:, slice(cols.start + width, cols.stop + width)] = d_keys.astype(BF16)
            d_mixed_ref[:, slice(cols.start + 2 * width, cols.stop + 2 * width)] = d_values.astype(BF16)
        d_queries = jnp.concatenate(d_query_parts, axis=0).T.astype(BF16)
        d_mixed_ref[:, :width] = d_queries
        add(QV_B, column_sum(d_queries))
        add(QV_B + 1, column_sum(d_mixed_ref[:, 2 * width :]))
        d_input = d_resid + mm_nt(d_mixed_ref[...], qkv_w[...])
        next_ref[:seq_len, :] = d_input.astype(BF16)


def half_of(info, theirs):
    return 1 - info[1] if theirs else info[1]


def ffn_weight_kernel(theirs, pad, info, *refs):
    slots = (len(refs) - 2) // 4
    normed, hidden, d_pre, d_down = (refs[i * slots : (i + 1) * slots] for i in range(4))
    sums_ref, out_ref = refs[4 * slots :]
    half = half_of(info, theirs)
    width = normed[0].shape[1]
    span = hidden[0].shape[1] // 2
    for part in range(span // BLOCK):
        cols = pl.ds(pl.multiple_of(half * span + part * BLOCK, BLOCK), BLOCK)
        total = sum(mm_tn(hidden[s][:, cols], d_down[s][...]) for s in range(slots))
        out_ref[part * BLOCK : (part + 1) * BLOCK, :] = total.astype(BF16)
        total = sum(mm_tn(normed[s][...], d_pre[s][:, cols]) for s in range(slots))
        start = span + part * width
        out_ref[start : start + width, :] = total.astype(BF16)
    start = 2 * span * width // BLOCK
    out_ref[start : start + pad, :] = jnp.zeros((pad, width), BF16)
    share = SMALL // 2
    rows = pl.ds(pl.multiple_of(half * share, share), share)
    out_ref[start : start + share, :] = sums_ref[rows, :].astype(BF16)


def attention_weight_kernel(theirs, info, *refs):
    slots = (len(refs) - 1) // 4
    x, context, d_mixed, d_proj = (refs[i * slots : (i + 1) * slots] for i in range(4))
    out_ref = refs[4 * slots]
    half = half_of(info, theirs)
    width = x[0].shape[1]
    span = width // 2
    cols = pl.ds(pl.multiple_of(half * span, span), span)
    for part in range(3):
        total = sum(mm_tn(x[s][:, cols], d_mixed[s][:, part * width : (part + 1) * width]) for s in range(slots))
        out_ref[part * span : (part + 1) * span, :] = total.astype(BF16)
    total = sum(mm_tn(context[s][:, cols], d_proj[s][...]) for s in range(slots))
    out_ref[3 * span : 4 * span, :] = total.astype(BF16)


def split_kernel(step, info, mine_ref, came_ref, keep_ref, send_ref):
    rows = keep_ref.shape[0]
    bit = info[2 + step]
    for ref, side in ((send_ref, 1 - bit), (keep_ref, bit)):
        at = pl.ds(pl.multiple_of(side * rows, 16), rows)
        ref[...] = (mine_ref[at, :].astype(F32) + came_ref[at, :].astype(F32)).astype(BF16)


def add_kernel(mine_ref, came_ref, out_ref):
    out_ref[...] = (mine_ref[...].astype(F32) + came_ref[...].astype(F32)).astype(BF16)


def join_kernel(step, info, mine_ref, came_ref, out_ref):
    rows = mine_ref.shape[0]
    bit = info[2 + step]
    out_ref[pl.ds(pl.multiple_of(bit * rows, 16), rows), :] = mine_ref[...]
    out_ref[pl.ds(pl.multiple_of((1 - bit) * rows, 16), rows), :] = came_ref[...]


def ffn_store_kernel(theirs, info, part_ref, *refs):
    stage_ref, sems = refs[-2:]
    in_out, down_out = refs[-4:-2]
    half = half_of(info, theirs)
    width = in_out.shape[1]
    span = in_out.shape[2] // 2
    copies = []
    for part in range(span // BLOCK):
        place = pl.ds(pl.multiple_of(half * span + part * BLOCK, BLOCK), BLOCK)
        for kind in range(2):
            spot = 2 * part + kind
            if kind == 0:
                start, dst = part * BLOCK, down_out.at[0, place, :]
            else:
                start, dst = span + part * width, in_out.at[0, :, place]
            stage_ref[spot] = part_ref[start : start + BLOCK, :].astype(F32)
            copies.append(pltpu.make_async_copy(stage_ref.at[spot], dst, sems.at[spot]))
            copies[-1].start()
    for copy in copies:
        copy.wait()


def attention_store_kernel(theirs, info, part_ref, *refs):
    stage_ref, sems = refs[-2:]
    qkv_out, out_out = refs[-4:-2]
    half = half_of(info, theirs)
    width = out_out.shape[2]
    span = width // 2
    rows = pl.ds(pl.multiple_of(half * span, span), span)
    copies = []
    for part in range(4):
        dst = out_out.at[0, rows, :] if part == 3 else qkv_out.at[0, rows, part * width : (part + 1) * width]
        stage_ref[part] = part_ref[part * span : (part + 1) * span, :].astype(F32)
        copies.append(pltpu.make_async_copy(stage_ref.at[part], dst, sems.at[part]))
        copies[-1].start()
    for copy in copies:
        copy.wait()


def small_store_kernel(info, mine_ref, came_ref, *refs):
    stages = len(refs) - 11
    grads = refs[:stages]
    qv_b, out_b, gain_one, shift_one, in_b, down_b, gain_two, shift_two, head_w, head_b, grad_ref = refs[stages:]
    share = SMALL // 2
    pad = mine_ref.shape[0] - share
    mine = mine_ref[...].astype(F32)
    came = came_ref[...].astype(F32)
    first = info[1] == 0
    low = jnp.where(first, mine, came)
    high = jnp.where(first, came, mine)
    width = low.shape[1]
    row = 0
    for vector in (qv_b, out_b, gain_one, shift_one, in_b, down_b, gain_two, shift_two):
        for part in range(vector.shape[1] // width):
            vector[:, part * width : (part + 1) * width] = low[row : row + 1, :]
            row += 1
    classes, tasks, _ = head_w.shape
    for c in range(classes):
        head_w[c] = high[c * tasks : (c + 1) * tasks, :]
    head_b[...] = high[classes * tasks : classes * tasks + 1, :128]
    seq_len = grad_ref.shape[0]
    for s in range(stages):

        @pl.when(info[0] == s)
        def _(s=s):
            grad_ref[...] = grads[s][:seq_len, :]


def shape(dims, dtype):
    return jax.ShapeDtypeStruct(dims, dtype)


def held(dims, dtype):
    return pltpu.VMEM(dims, dtype)


def near(array):
    return pltpu.with_memory_space_constraint(array, pltpu.VMEM)


def call(kernel, name, out_shape, args, in_specs, out_specs=None, aliases=None, scratch=(), flops=0, limit=16):
    single = not isinstance(out_shape, tuple)
    if out_specs is None:
        out_specs = VMEM if single else (VMEM,) * len(out_shape)
    return pl.pallas_call(
        kernel,
        out_shape=out_shape,
        in_specs=in_specs,
        out_specs=out_specs,
        scratch_shapes=scratch,
        input_output_aliases=aliases or {},
        compiler_params=pltpu.CompilerParams(vmem_limit_bytes=limit * MIB),
        cost_estimate=pl.CostEstimate(flops=flops, bytes_accessed=2 * MIB, transcendentals=0),
        name=name,
    )(*args)


def local(
    hidden_in, segment_ids, task_ids, labels, cotangent, qkv_weight, qv_bias, out_weight, out_bias, norm1_gain, norm1_bias,
    ffn_in_weight, ffn_in_bias, ffn_out_weight, ffn_out_bias, norm2_gain, norm2_bias, head_weight, head_bias,
):
    stages = lax.axis_size("pipe")
    stage = lax.axis_index("pipe")
    shards = lax.axis_size("dp")
    shard = lax.axis_index("dp")
    _, seq_len, width = hidden_in.shape
    hidden_width = ffn_in_weight.shape[2]
    task_count, _, class_count = head_weight.shape
    block = (seq_len + EXTRA, width)

    bits = shards.bit_length() - 1
    upward = list(range(1, bits))
    orders = (upward, upward[::-1])
    core = shard & 1
    sides = [jnp.where(core == 0, (shard >> orders[0][j]) & 1, (shard >> orders[1][j]) & 1) for j in range(bits - 1)]
    info = jnp.stack([stage, core] + sides).astype(jnp.int32)

    home, qkv_w, out_w, in_w, down_w, vec, head_w = call(
        load_kernel,
        "load",
        (
            held(block, BF16),
            held((width, 3 * width), BF16),
            held((width, width), BF16),
            held((width, hidden_width), BF16),
            held((hidden_width, width), BF16),
            held((16, width), F32),
            held((16, width), F32),
        ),
        (
            hidden_in, qkv_weight, out_weight, ffn_in_weight, ffn_out_weight, segment_ids, qv_bias, out_bias, norm1_gain, norm1_bias,
            ffn_in_bias, ffn_out_bias, norm2_gain, norm2_bias, head_weight.transpose(2, 0, 1),
        ),
        [ANY] * 5 + [VMEM] * 10,
        scratch=[pltpu.SemaphoreType.DMA((5,))],
    )
    weights = tuple(near(w) for w in (qkv_w, out_w, in_w, down_w, vec))

    def move(array, pairs):
        return lax.ppermute(array, "pipe", pairs)

    def route(tick):
        pairs = [(s, s + 1) for s in range(stages - 1) if 0 <= tick - 2 * s < stages]
        if tick + 2 < stages:
            pairs.append((tick + 2, 0))
        late = tick - 2 * (stages - 1)
        if 0 <= late < stages - 1:
            pairs.append((stages - 1, late))
        return pairs

    def back(tick):
        return [(b, a) for a, b in route(tick)]

    ticks = 2 * (stages - 1) + stages
    saved_shapes = (
        held((seq_len, width), BF16),
        held((seq_len, 3 * width), BF16),
        held((seq_len, HEADS * seq_len), BF16),
        held((seq_len, width), BF16),
        held((seq_len, width), F32),
        held((seq_len, width), BF16),
        held((seq_len, hidden_width), BF16),
        held((seq_len, hidden_width), BF16),
        held((seq_len, width), F32),
        held((seq_len, 256), F32),
    )
    arrived = {0: home, 1: move(home, [(1, 0)])}
    slots = [None] * stages
    last = None
    for tick in range(ticks):
        carry = 0 < tick + 2 < stages
        fresh = slots[tick % stages] is None
        args = [info, near(arrived[tick])] + ([near(home)] if carry else []) + list(weights)
        aliases = {}
        if not fresh:
            aliases = {len(args) + i: 1 + i for i in range(len(saved_shapes))}
            args += [near(a) for a in slots[tick % stages]]
        outs = call(
            partial(forward_kernel, tick, stages, carry, fresh),
            "layer_forward",
            (held(block, BF16),) + saved_shapes,
            args,
            [SMEM] + [VMEM] * (len(args) - 1),
            aliases=aliases,
            flops=4_000_000_000,
        )
        slots[tick % stages] = tuple(outs[1:])
        last = outs[0]
        if route(tick):
            arrived[tick + 2] = move(last, route(tick))
    finals = [arrived[2 * (stages - 1) + 2 + s] for s in range(stages - 1)] + [last]
    home, hidden_out, losses = call(
        head_kernel,
        "task_heads",
        (held(block, BF16), shape((seq_len, width), BF16), shape(task_ids.shape, F32)),
        [info, task_ids, labels, head_bias] + [near(f) for f in finals] + [cotangent.reshape(seq_len, width), near(head_w)],
        [SMEM] * 4 + [VMEM] * (stages + 2),
        scratch=[pltpu.VMEM(block, BF16)],
        flops=1_000_000_000,
    )

    arrived = {ticks - 1: home, ticks - 2: move(home, back(ticks - 2))}
    proj = [None] * stages
    sums = None
    results = {}
    for tick in reversed(range(ticks)):
        slot = tick % stages
        carry = tick < ticks - 1 and 0 <= tick - 2 - 2 * (stages - 1) + 0 or tick in (ticks - 1, ticks - 2)
        x, qkv, probs, context, unit_one, normed, hidden, slope, unit_two, scales = slots[slot]
        args = [info, near(arrived[tick])] + ([near(home)] if carry else []) + list(weights)
        aliases = {len(args): 1, len(args) + 1: 2}
        args += [near(a) for a in (qkv, slope, probs, unit_one, unit_two, scales)]
        fresh_proj, fresh_sums = proj[slot] is None, sums is None
        if not fresh_proj:
            aliases |= {len(args): 3, len(args) + 1: 4}
            args += [near(a) for a in proj[slot]]
        if not fresh_sums:
            aliases |= {len(args): 5}
            args += [near(sums)]
        last, d_mixed, d_pre, d_proj, d_down, sums = call(
            partial(backward_kernel, tick, stages, carry, fresh_proj, fresh_sums),
            "layer_backward",
            (
                held(block, BF16),
                held((seq_len, 3 * width), BF16),
                held((seq_len, hidden_width), BF16),
                held((seq_len, width), BF16),
                held((seq_len, width), BF16),
                held((SMALL, width), F32),
            ),
            args,
            [SMEM] + [VMEM] * (len(args) - 1),
            aliases=aliases,
            scratch=[pltpu.VMEM((seq_len, width), BF16)],
            flops=4_000_000_000,
        )
        proj[slot] = (d_proj, d_down)
        slots[slot] = (x, d_mixed, probs, context, unit_one, normed, hidden, d_pre, unit_two, scales)
        if tick >= 2:
            arrived[tick - 2] = move(last, back(tick - 2))
        if tick == 1:
            results[1] = move(last, [(0, 1)])
        if 2 <= tick < stages:
            results[tick] = arrived[tick - 2]
    results[0] = last

    def flip(bit):
        return [(i, i ^ (1 << bit)) for i in range(shards)]

    def across(step):
        return [(i, i ^ (1 << orders[i & 1][step])) for i in range(shards)]

    def swap(array, pairs):
        return lax.ppermute(array, "dp", pairs)

    def reduced(mine, theirs):
        came = swap(theirs, flip(0))
        for step in range(bits - 1):
            rows = mine.shape[0] // 2
            out = held((rows, width), BF16)
            mine, send = call(
                partial(split_kernel, step), "split_sum", (out, out), (info, near(mine), near(came)), [SMEM, VMEM, VMEM], flops=1_000_000
            )
            came = swap(send, across(step))
        mine = call(add_kernel, "last_sum", held(mine.shape, BF16), (near(mine), near(came)), [VMEM, VMEM], flops=1_000_000)
        for step in reversed(range(bits - 1)):
            came = swap(mine, across(step))
            mine = call(
                partial(join_kernel, step),
                "join",
                held((2 * mine.shape[0], width), BF16),
                (info, near(mine), near(came)),
                [SMEM, VMEM, VMEM],
                flops=1_000_000,
            )
        return mine, swap(mine, flip(0))

    chunk = 16 * shards // 2
    ffn_rows = hidden_width // 2 + hidden_width // 2 * width // BLOCK
    total_rows = -(-(ffn_rows + SMALL // 2) // chunk) * chunk
    pad = total_rows - ffn_rows
    picks = [[slots[s][i] for s in range(stages)] for i in range(10)]
    ffn_args = [near(a) for a in picks[5] + picks[6] + picks[7] + [proj[s][1] for s in range(stages)]] + [near(sums)]
    theirs, mine = (
        call(
            partial(ffn_weight_kernel, other, pad),
            "ffn_weight_gradients",
            held((total_rows, width), BF16),
            [info] + ffn_args,
            [SMEM] + [VMEM] * len(ffn_args),
            flops=6_000_000_000,
        )
        for other in (True, False)
    )
    ffn_mine, ffn_came = reduced(mine, theirs)
    att_args = [near(a) for a in picks[0] + picks[3] + picks[1] + [proj[s][0] for s in range(stages)]]
    theirs, mine = (
        call(
            partial(attention_weight_kernel, other),
            "attention_weight_gradients",
            held((2 * width, width), BF16),
            [info] + att_args,
            [SMEM] + [VMEM] * len(att_args),
            flops=3_000_000_000,
        )
        for other in (True, False)
    )
    att_mine, att_came = reduced(mine, theirs)

    def stored(kernel, name, mine, came, dims, count, tile):
        out_shape = tuple(pltpu.HBM(d, F32) for d in dims)
        scratch = [pltpu.VMEM((count,) + tile, F32), pltpu.SemaphoreType.DMA((count,))]
        first = call(partial(kernel, False), name, out_shape, (info, near(mine)), [SMEM, VMEM], (ANY, ANY), scratch=scratch, flops=1_000_000)
        return call(
            partial(kernel, True),
            name,
            out_shape,
            (info, near(came)) + tuple(first),
            [SMEM, VMEM, ANY, ANY],
            (ANY, ANY),
            aliases={2: 0, 3: 1},
            scratch=scratch,
            flops=1_000_000,
        )

    in_grad, down_grad = stored(
        ffn_store_kernel, "ffn_store", ffn_mine, ffn_came, ((1, width, hidden_width), (1, hidden_width, width)), hidden_width // BLOCK,
        (BLOCK, BLOCK),
    )
    qkv_grad, out_grad = stored(
        attention_store_kernel, "attention_store", att_mine, att_came, ((1, width, 3 * width), (1, width, width)), 4, (width // 2, width)
    )
    vectors = tuple(
        shape((1, n), F32) for n in (2 * width, width, width, width, hidden_width, width, width, width)
    )
    *vectors, head_w_grad, head_b_grad, hidden_grad = call(
        small_store_kernel,
        "small_store",
        vectors + (shape((class_count, task_count, width), F32), shape((1, 128), F32), shape((seq_len, width), BF16)),
        [info, ffn_mine[ffn_rows : ffn_rows + SMALL // 2], ffn_came[ffn_rows : ffn_rows + SMALL // 2]] + [near(results[s]) for s in range(stages)],
        [SMEM] + [VMEM] * (2 + stages),
        flops=1_000_000,
    )
    qv_grad, out_b_grad, gain_one_grad, shift_one_grad, in_b_grad, down_b_grad, gain_two_grad, shift_two_grad = vectors
    return (
        hidden_out[None],
        losses,
        hidden_grad[None],
        qkv_grad,
        qv_grad,
        out_grad,
        out_b_grad,
        gain_one_grad,
        shift_one_grad,
        in_grad,
        in_b_grad,
        down_grad,
        down_b_grad,
        gain_two_grad,
        shift_two_grad,
        head_w_grad.transpose(1, 2, 0),
        head_b_grad[0, : class_count * task_count].reshape(class_count, task_count).T,
    )


def solution(mesh):
    rows = P(("dp", "pipe"), None, None)
    ids = P(("dp", "pipe"), None)
    big = P("pipe", None, None)
    vec = P("pipe", None)
    return jax.shard_map(
        local,
        mesh=mesh,
        in_specs=(rows, ids, ids, ids, rows, big, vec, big, vec, vec, vec, big, vec, big, vec, vec, vec, P(), P()),
        out_specs=(rows, ids, rows, big, vec, big, vec, vec, vec, big, vec, big, vec, vec, vec, P(), P()),
        check_vma=False,
    )
```

```python
from functools import partial

import jax
import jax.numpy as jnp
from jax import lax
from jax.experimental import pallas as pl
from jax.experimental.pallas import tpu as pltpu
from jax.sharding import PartitionSpec as P

HEADS = 8
EPS = 1e-12
NEG = -1000000000.0
EXTRA = 16
SMALL = 32
BLOCK = 512
F32 = jnp.float32
BF16 = jnp.bfloat16
VMEM = pl.BlockSpec(memory_space=pltpu.VMEM)
ANY = pl.BlockSpec(memory_space=pl.ANY)
MIB = 1024 * 1024
PICK = 1
SPLIT = 20_000_000_000
WHOLE = 10_000_000_000
HEAVY = 10_000_000_000
J_A1 = 10_000_000_000
J_D0 = 100_000_000
J_I0 = 10_000_000_000
J_A0 = 10_000_000_000
J_D1 = 10_000_000_000
J_I1 = 10_000_000_000
STORE = 100_000_000
LIMIT = 6
QV_B, OUT_B, GAIN_ONE, SHIFT_ONE, IN_B, DOWN_B, GAIN_TWO, SHIFT_TWO = 0, 2, 3, 4, 5, 9, 10, 11


def mm(a, b):
    return lax.dot_general(a, b, (((1,), (0,)), ((), ())), preferred_element_type=F32)


def mm_nt(a, b):
    return lax.dot_general(a, b, (((1,), (1,)), ((), ())), preferred_element_type=F32)


def mm_tn(a, b):
    return lax.dot_general(a, b, (((0,), (0,)), ((), ())), preferred_element_type=F32)


def lane_masks(width):
    lanes = lax.broadcasted_iota(jnp.int32, (1, 2 * width), 1)
    return (lanes < width).astype(BF16), (lanes >= width).astype(BF16)


def segment_onehot(meta, count, seq_len):
    numbers = lax.broadcasted_iota(jnp.int32, (count, seq_len), 0).astype(F32)
    return (meta[0:1, :seq_len].astype(F32) == numbers).astype(F32)


def norm_stats(values):
    centre = values - jnp.mean(values, axis=-1, keepdims=True)
    spread = jnp.mean(centre * centre, axis=-1, keepdims=True)
    scale = lax.rsqrt(spread + EPS)
    return centre * scale, scale


def norm_back(grad, unit, scale, gain):
    scaled = grad * gain
    mean_one = jnp.mean(scaled, axis=-1, keepdims=True)
    mean_two = jnp.mean(scaled * unit, axis=-1, keepdims=True)
    return scale * (scaled - mean_one - unit * mean_two)


def column_sum(values):
    return jnp.sum(values.astype(F32), axis=0, keepdims=True)


def prepare_kernel(
    x_ref, seg_ref, qv_b, out_b, gain_one, shift_one, in_b, down_b, gain_two, shift_two, head_ref, block_ref, vec_ref, head_w_ref
):
    _, seq_len, width = x_ref.shape
    block_ref[:seq_len, :] = x_ref[0]
    block_ref[seq_len:, :] = jnp.zeros((EXTRA, width), BF16)
    block_ref[seq_len:, :seq_len] = jnp.broadcast_to(seg_ref[...].astype(F32).astype(BF16), (EXTRA, seq_len))
    row = 0
    for vector in (qv_b, out_b, gain_one, shift_one, in_b, down_b, gain_two, shift_two):
        for part in range(vector.shape[1] // width):
            vec_ref[row : row + 1, :] = vector[:, part * width : (part + 1) * width]
            row += 1
    classes, tasks, _ = head_ref.shape
    head_w_ref[...] = jnp.zeros_like(head_w_ref)
    for c in range(classes):
        head_w_ref[c * tasks : (c + 1) * tasks, :] = head_ref[c]


def forward_kernel(tick, stages, carry, fresh, info, x_ref, *refs):
    refs = list(refs)
    home_ref = refs.pop(0) if carry else None
    if tick == 0:
        vec, refs, sems = refs[4], refs[:4] + refs[5:-1], refs[-1]
        qkv_w, out_w, in_w, down_w = weights = refs[-4:]
        copies = [pltpu.make_async_copy(refs[i].at[0], weights[i], sems.at[i]) for i in range(4)]
        for copy in copies:
            copy.start()
        refs = refs[4:-4]
    else:
        copies = []
        qkv_w, out_w, in_w, down_w, vec = refs[:5]
        refs = refs[5:]

    def ready(*which):
        for i in which:
            if copies:
                copies[i].wait()

    if not fresh:
        refs = refs[10:]
    y_ref, keep_ref, qkv_ref, probs_ref, context_ref, unit_one_ref, normed_ref, hidden_ref, slope_ref, unit_two_ref, scales_ref = refs
    seq_len = x_ref.shape[0] - EXTRA
    width = x_ref.shape[1]
    head_dim = width // HEADS
    place = tick - 2 * info[0, 0]
    active = (place >= 0) & (place < stages)

    if carry:

        @pl.when(jnp.logical_not(active))
        def _():
            y_ref[...] = home_ref[...]
            ready(0, 1, 2, 3)

    @pl.when(active)
    def _():
        meta = x_ref[seq_len:, :]
        y_ref[seq_len:, :] = meta
        x = x_ref[:seq_len, :]
        keep_ref[...] = x
        onehot = segment_onehot(meta, EXTRA, seq_len).astype(BF16)
        allowed = mm_tn(onehot, onehot) > 0.5
        ready(0)
        q = (mm(x, qkv_w[:, :width]) + vec[QV_B : QV_B + 1]).astype(BF16)
        k = mm(x, qkv_w[:, width : 2 * width]).astype(BF16)
        v = (mm(x, qkv_w[:, 2 * width :]) + vec[QV_B + 1 : QV_B + 2]).astype(BF16)
        qkv_ref[:, :width] = q
        qkv_ref[:, width : 2 * width] = k
        qkv_ref[:, 2 * width :] = v
        v_t = v.T
        mask_a, mask_b = lane_masks(head_dim)
        factor = head_dim**-0.5
        context_parts = []
        for pair in range(HEADS // 2):
            cols = slice(pair * 2 * head_dim, (pair + 1) * 2 * head_dim)
            k_two = jnp.concatenate([k[:, cols] * (mask * factor).astype(BF16) for mask in (mask_a, mask_b)], axis=0)
            both = mm_nt(k_two, q[:, cols])
            for side in range(2):
                head = 2 * pair + side
                scores = jnp.where(allowed, both[side * seq_len : (side + 1) * seq_len], NEG)
                expo = jnp.exp(scores - jnp.max(scores, axis=0, keepdims=True))
                probs = (expo * (1.0 / jnp.sum(expo, axis=0, keepdims=True))).astype(BF16)
                probs_ref[head * seq_len : (head + 1) * seq_len, :] = probs
                context_parts.append(mm(v_t[head * head_dim : (head + 1) * head_dim, :], probs))
        context = jnp.concatenate(context_parts, axis=0).T.astype(BF16)
        context_ref[...] = context
        ready(1)
        resid = x.astype(F32) + mm(context, out_w[...]) + vec[OUT_B : OUT_B + 1]
        unit_one, scale_one = norm_stats(resid)
        unit_one_ref[...] = unit_one
        normed = unit_one * vec[GAIN_ONE : GAIN_ONE + 1] + vec[SHIFT_ONE : SHIFT_ONE + 1]
        normed_low = normed.astype(BF16)
        normed_ref[...] = normed_low
        summed = normed + vec[DOWN_B : DOWN_B + 1]
        ready(2, 3)
        for part in range(in_w.shape[1] // BLOCK):
            cols = slice(part * BLOCK, (part + 1) * BLOCK)
            pre = mm(normed_low, in_w[:, cols]) + vec[IN_B + part : IN_B + part + 1]
            gate = 0.5 + 0.5 * lax.erf(pre * (0.5**0.5))
            slope_ref[:, cols] = (gate + pre * (jnp.exp(-0.5 * pre * pre) * 0.3989422804014327)).astype(BF16)
            hidden = (pre * gate).astype(BF16)
            hidden_ref[:, cols] = hidden
            summed = summed + mm(hidden, down_w[cols, :])
        unit_two, scale_two = norm_stats(summed)
        unit_two_ref[...] = unit_two
        y_ref[:seq_len, :] = (unit_two * vec[GAIN_TWO : GAIN_TWO + 1] + vec[SHIFT_TWO : SHIFT_TWO + 1]).astype(BF16)
        scales_ref[:, 0:128] = jnp.broadcast_to(scale_one, (seq_len, 128))
        scales_ref[:, 128:256] = jnp.broadcast_to(scale_two, (seq_len, 128))


def head_kernel(info, task_ref, label_ref, head_b_ref, *refs):
    stages = len(refs) - 6
    y_refs = refs[:stages]
    cot_ref, head_w, g_ref, final_ref, loss_ref, picked = refs[stages:]
    for s in range(stages):

        @pl.when(info[0, 0] == s)
        def _(s=s):
            picked[...] = y_refs[s][...]

    seq_len, width = final_ref.shape
    task_count, class_count = head_b_ref.shape
    seg_count = task_ref.shape[1]
    high = lax.Precision.HIGHEST
    y = picked[:seq_len, :]
    final_ref[...] = y
    meta = picked[seq_len:, :]
    segs = 8
    onehot = segment_onehot(meta, segs, seq_len)
    row = meta[0:1, :seq_len].astype(F32)
    lanes = lax.broadcasted_iota(jnp.int32, (1, seq_len), 1)
    previous = jnp.where(lanes == 0, -1.0, pltpu.roll(row, 1, 1))
    pick = onehot * (row != previous).astype(F32)
    live = jnp.max(pick, axis=1, keepdims=True)
    cls = mm(pick.astype(BF16), y)
    logits = lax.dot_general(cls, head_w[...], (((1,), (1,)), ((), ())), precision=high, preferred_element_type=F32)
    slots = lax.broadcasted_iota(jnp.int32, (1, logits.shape[1]), 1)
    bias = jnp.zeros((1, logits.shape[1]), F32)
    for t in range(task_count):
        for c in range(class_count):
            bias = jnp.where(slots == c * task_count + t, head_b_ref[t, c], bias)
    logits = logits + bias
    numbers = lax.broadcasted_iota(jnp.int32, (segs, 1), 0)
    task = jnp.zeros((segs, 1), jnp.int32)
    label = jnp.zeros((segs, 1), jnp.int32)
    for s in range(seg_count):
        task = jnp.where(numbers == s, task_ref[0, s], task)
        label = jnp.where(numbers == s, label_ref[0, s], label)
    mine = jnp.zeros(logits.shape, jnp.bool_)
    for c in range(class_count):
        mine = mine | (slots == task + c * task_count)
    label_hot = slots == task + label * task_count
    masked = jnp.where(mine, logits, -jnp.inf)
    top = jnp.max(masked, axis=1, keepdims=True)
    expo = jnp.exp(masked - top)
    total = jnp.sum(expo, axis=1, keepdims=True)
    right = jnp.sum(jnp.where(label_hot, logits, 0.0), axis=1, keepdims=True)
    loss = live * (top + jnp.log(total) - right)
    wide = lax.broadcasted_iota(jnp.int32, (segs, 128), 1)
    loss_row = jnp.sum(jnp.where(wide == numbers, loss, 0.0), axis=0, keepdims=True)
    loss_ref[...] = loss_row[:, :seg_count]
    d_logits = live * (expo / total - label_hot.astype(F32))
    d_cls = lax.dot_general(d_logits, head_w[...], (((1,), (0,)), ((), ())), precision=high, preferred_element_type=F32)
    d_final = lax.dot_general(pick, d_cls, (((0,), (0,)), ((), ())), precision=high, preferred_element_type=F32)
    g_ref[:seq_len, :] = (cot_ref[...].astype(F32) + d_final).astype(BF16)
    g_w = lax.dot_general(d_logits, cls, (((0,), (0,)), ((), ())), precision=high, preferred_element_type=F32)
    g_b = jnp.concatenate([column_sum(d_logits)] * (width // logits.shape[1]), axis=1)
    rows = lax.broadcasted_iota(jnp.int32, (EXTRA, 1), 0)
    count = task_count * class_count
    g_ref[seq_len:, :] = jnp.where(rows < count, g_w[:EXTRA], jnp.where(rows == count, g_b, 0.0)).astype(BF16)


def adder(sums_ref):
    def add(row, value):
        sums_ref[row : row + 1, :] += value

    return add


def ffn_back(g_ref, slope_ref, unit_one_ref, unit_two_ref, scales_ref, in_w, down_w, vec, d_pre_ref, d_down_ref, sums_ref):
    seq_len = g_ref.shape[0] - EXTRA
    add = adder(sums_ref)
    sums_ref[SMALL - EXTRA :, :] += g_ref[seq_len:, :].astype(F32)
    grad = g_ref[:seq_len, :].astype(F32)
    scale_one = scales_ref[:, 0:1]
    scale_two = scales_ref[:, 128:129]
    unit_two = unit_two_ref[...]
    add(GAIN_TWO, column_sum(grad * unit_two))
    add(SHIFT_TWO, column_sum(grad))
    d_summed = norm_back(grad, unit_two, scale_two, vec[GAIN_TWO : GAIN_TWO + 1])
    d_down = d_summed.astype(BF16)
    d_down_ref[...] = d_down
    add(DOWN_B, column_sum(d_down))
    d_normed = d_summed
    for part in range(in_w.shape[1] // BLOCK):
        cols = slice(part * BLOCK, (part + 1) * BLOCK)
        d_pre = (mm_nt(d_down, down_w[cols, :]) * slope_ref[:, cols].astype(F32)).astype(BF16)
        d_pre_ref[:, cols] = d_pre
        add(IN_B + part, column_sum(d_pre))
        d_normed = d_normed + mm_nt(d_pre, in_w[:, cols])
    unit_one = unit_one_ref[...]
    add(GAIN_ONE, column_sum(d_normed * unit_one))
    add(SHIFT_ONE, column_sum(d_normed))
    return norm_back(d_normed, unit_one, scale_one, vec[GAIN_ONE : GAIN_ONE + 1])


def attention_back(d_resid, qkv_ref, probs_ref, qkv_w, out_w, next_ref, d_mixed_ref, d_proj_ref, sums_ref, queries):
    seq_len, width = d_resid.shape
    head_dim = width // HEADS
    add = adder(sums_ref)
    d_proj = d_resid.astype(BF16)
    d_proj_ref[...] = d_proj
    add(OUT_B, column_sum(d_proj))
    d_context = mm_nt(d_proj, out_w[...]).astype(BF16)
    factor = head_dim**-0.5
    mask_a, mask_b = lane_masks(head_dim)
    queries[...] = qkv_ref[:, :width]
    keys = qkv_ref[:, width : 2 * width]
    k_t = (keys * jnp.asarray(factor, BF16)).T
    d_query_parts = []
    first = lax.broadcasted_iota(jnp.int32, (seq_len, 2 * head_dim), 1) < head_dim
    for pair in range(HEADS // 2):
        cols = slice(pair * 2 * head_dim, (pair + 1) * 2 * head_dim)
        rows = slice(pair * 2 * seq_len, (pair + 1) * 2 * seq_len)
        v_cols = qkv_ref[:, slice(cols.start + 2 * width, cols.stop + 2 * width)]
        d_context_cols = d_context[:, cols]
        v_two = jnp.concatenate([v_cols * mask for mask in (mask_a, mask_b)], axis=0)
        d_probs = mm_nt(v_two, d_context_cols)
        probs = probs_ref[rows, :]
        d_values = mm(probs, d_context_cols)
        parts = []
        for side in range(2):
            half = slice(side * seq_len, (side + 1) * seq_len)
            probs_wide = probs[half].astype(F32)
            weighted = probs_wide * d_probs[half]
            d_scores = (weighted - probs_wide * jnp.sum(weighted, axis=0, keepdims=True)).astype(BF16)
            parts.append(d_scores)
            head = 2 * pair + side
            d_query_parts.append(mm(k_t[head * head_dim : (head + 1) * head_dim, :], d_scores))
        d_keys = mm(jnp.concatenate(parts, axis=0), queries[:, cols] * jnp.asarray(factor, BF16))
        d_mixed_ref[:, slice(cols.start + width, cols.stop + width)] = jnp.where(first, d_keys[:seq_len], d_keys[seq_len:]).astype(BF16)
        d_mixed_ref[:, slice(cols.start + 2 * width, cols.stop + 2 * width)] = jnp.where(
            first, d_values[:seq_len], d_values[seq_len:]
        ).astype(BF16)
    d_queries = jnp.concatenate(d_query_parts, axis=0).T.astype(BF16)
    d_mixed_ref[:, :width] = d_queries
    add(QV_B, column_sum(d_queries))
    add(QV_B + 1, column_sum(d_mixed_ref[:, 2 * width :]))
    d_input = d_resid + mm_nt(d_mixed_ref[...], qkv_w[...])
    next_ref[:seq_len, :] = d_input.astype(BF16)


def is_active(info, tick, stages):
    place = tick - 2 * info[0, 0]
    return (place >= 0) & (place < stages)


def backward_kernel(tick, stages, carry, fresh_proj, fresh_sums, info, g_ref, *refs):
    refs = list(refs)
    home_ref = refs.pop(0) if carry else None
    qkv_w, out_w, in_w, down_w, vec = refs[:5]
    qkv_ref, slope_ref, probs_ref, unit_one_ref, unit_two_ref, scales_ref = refs[5:11]
    refs = refs[11:]
    if not fresh_proj:
        refs = refs[2:]
    if not fresh_sums:
        refs = refs[1:]
    next_ref, d_mixed_ref, d_pre_ref, d_proj_ref, d_down_ref, sums_ref, queries = refs
    seq_len = g_ref.shape[0] - EXTRA
    active = is_active(info, tick, stages)

    if carry:

        @pl.when(jnp.logical_not(active))
        def _():
            next_ref[...] = home_ref[...]

    if fresh_sums:
        sums_ref[...] = jnp.zeros_like(sums_ref)

    @pl.when(active)
    def _():
        next_ref[seq_len:, :] = g_ref[seq_len:, :]
        d_resid = ffn_back(
            g_ref, slope_ref, unit_one_ref, unit_two_ref, scales_ref, in_w, down_w, vec, d_pre_ref, d_down_ref, sums_ref
        )
        attention_back(d_resid, qkv_ref, probs_ref, qkv_w, out_w, next_ref, d_mixed_ref, d_proj_ref, sums_ref, queries)


def last_ffn_kernel(
    tick, stages, info, g_ref, in_w, down_w, vec, slope_ref, unit_one_ref, unit_two_ref, scales_ref, d_down_in, sums_in,
    d_pre_ref, d_down_ref, sums_ref, d_resid_ref,
):
    @pl.when(is_active(info, tick, stages))
    def _():
        d_resid_ref[...] = ffn_back(
            g_ref, slope_ref, unit_one_ref, unit_two_ref, scales_ref, in_w, down_w, vec, d_pre_ref, d_down_ref, sums_ref
        )


def last_attention_kernel(
    tick, stages, info, d_resid_ref, qkv_w, out_w, probs_ref, qkv_ref, d_proj_in, sums_in,
    next_ref, d_mixed_ref, d_proj_ref, sums_ref, queries,
):
    @pl.when(is_active(info, tick, stages))
    def _():
        attention_back(d_resid_ref[...], qkv_ref, probs_ref, qkv_w, out_w, next_ref, d_mixed_ref, d_proj_ref, sums_ref, queries)


def half_of(info, theirs):
    return 1 - info[1, 0] if theirs else info[1, 0]


def outer(left, right, rows=None, cols=None):
    rows = slice(None) if rows is None else rows
    cols = slice(None) if cols is None else cols
    return sum(mm_tn(a[:, rows], b[:, cols]) for a, b in zip(left, right))


def down_weights(theirs, info, *refs):
    *refs, out_ref = refs
    hidden, d_down = refs[: len(refs) // 2], refs[len(refs) // 2 :]
    span = hidden[0].shape[1] // 2
    for start in range(0, span, BLOCK):
        at = pl.ds(pl.multiple_of(half_of(info, theirs) * span + start, BLOCK), BLOCK)
        out_ref[start : start + BLOCK, :] = outer(hidden, d_down, rows=at).astype(BF16)


def in_weights(theirs, info, *refs):
    *refs, out_ref = refs
    normed, d_pre = refs[: len(refs) // 2], refs[len(refs) // 2 :]
    width = normed[0].shape[1]
    span = d_pre[0].shape[1] // 2
    for part in range(span // BLOCK):
        at = pl.ds(pl.multiple_of(half_of(info, theirs) * span + part * BLOCK, BLOCK), BLOCK)
        out_ref[part * width : (part + 1) * width, :] = outer(normed, d_pre, cols=at).astype(BF16)


def attention_weights(theirs, info, *refs):
    *refs, sums_ref, out_ref = refs
    slots = len(refs) // 4
    x, context, d_mixed, d_proj = (refs[i * slots : (i + 1) * slots] for i in range(4))
    half = half_of(info, theirs)
    width = x[0].shape[1]
    span = width // 2
    at = pl.ds(pl.multiple_of(half * span, span), span)
    for part in range(3):
        cols = slice(part * width, (part + 1) * width)
        out_ref[part * span : (part + 1) * span, :] = outer(x, d_mixed, rows=at, cols=cols).astype(BF16)
    out_ref[3 * span : 4 * span, :] = outer(context, d_proj, rows=at).astype(BF16)
    out_ref[4 * span :, :] = jnp.zeros((out_ref.shape[0] - 4 * span, width), BF16)
    share = SMALL // 2
    out_ref[4 * span : 4 * span + share, :] = sums_ref[pl.ds(pl.multiple_of(half * share, share), share), :].astype(BF16)


def split_kernel(step, info, mine_ref, came_ref, keep_ref, send_ref):
    rows = keep_ref.shape[0]
    bit = info[2 + step, 0]
    for ref, side in ((send_ref, 1 - bit), (keep_ref, bit)):
        at = pl.ds(pl.multiple_of(side * rows, 16), rows)
        ref[...] = (mine_ref[at, :].astype(F32) + came_ref[at, :].astype(F32)).astype(BF16)


def add_kernel(mine_ref, came_ref, out_ref):
    out_ref[...] = (mine_ref[...].astype(F32) + came_ref[...].astype(F32)).astype(BF16)


def join_kernel(step, info, mine_ref, came_ref, out_ref):
    rows = mine_ref.shape[0]
    bit = info[2 + step, 0]
    out_ref[pl.ds(pl.multiple_of(bit * rows, 16), rows), :] = mine_ref[...]
    out_ref[pl.ds(pl.multiple_of((1 - bit) * rows, 16), rows), :] = came_ref[...]


def store_kernel(name, sides, known, info, *refs):
    parts = refs[: len(sides)]
    token, stage_ref, sems = refs[-3:]
    outs = refs[len(sides) + known : -3]
    token[...] = jnp.zeros_like(token)
    copies = []
    row = 0
    for theirs, part_ref in zip(sides, parts):
        half = half_of(info, theirs)
        width = part_ref.shape[1]
        targets = []
        if name == "down":
            span = outs[0].shape[1] // 2
            for start in range(0, span, BLOCK):
                targets.append((BLOCK, outs[0].at[0, pl.ds(pl.multiple_of(half * span + start, BLOCK), BLOCK), :]))
        elif name == "in":
            span = outs[0].shape[2] // 2
            for start in range(0, span, BLOCK):
                targets.append((width, outs[0].at[0, :, pl.ds(pl.multiple_of(half * span + start, BLOCK), BLOCK)]))
        else:
            span = width // 2
            at = pl.ds(pl.multiple_of(half * span, span), span)
            targets = [(span, outs[0].at[0, at, i * width : (i + 1) * width]) for i in range(3)] + [(span, outs[1].at[0, at, :])]
        start = 0
        for size, dst in targets:
            stage_ref[row : row + size, :] = part_ref[start : start + size, :].astype(F32)
            copies.append(pltpu.make_async_copy(stage_ref.at[row : row + size], dst, sems.at[len(copies)]))
            copies[-1].start()
            start += size
            row += size
    for copy in copies:
        copy.wait()


def small_store_kernel(
    start, info, mine_ref, came_ref, qv_b, out_b, gain_one, shift_one, in_b, down_b, gain_two, shift_two, head_w, head_b, token
):
    token[...] = jnp.zeros_like(token)
    share = SMALL // 2
    mine = mine_ref[start : start + share, :].astype(F32)
    came = came_ref[start : start + share, :].astype(F32)
    first = info[1, 0] == 0
    low = jnp.where(first, mine, came)
    high = jnp.where(first, came, mine)
    width = low.shape[1]
    row = 0
    for vector in (qv_b, out_b, gain_one, shift_one, in_b, down_b, gain_two, shift_two):
        for part in range(vector.shape[1] // width):
            vector[:, part * width : (part + 1) * width] = low[row : row + 1, :]
            row += 1
    classes, tasks, _ = head_w.shape
    for c in range(classes):
        head_w[c] = high[c * tasks : (c + 1) * tasks, :]
    line = high[classes * tasks : classes * tasks + 1, :128]
    lanes = lax.broadcasted_iota(jnp.int32, (16, 128), 1)
    spread = jnp.where(lanes % tasks == lax.broadcasted_iota(jnp.int32, (16, 128), 0), line, 0.0).astype(BF16)
    gather = (lax.broadcasted_iota(jnp.int32, (128, 128), 0) // tasks == lax.broadcasted_iota(jnp.int32, (128, 128), 1)).astype(BF16)
    head_b[...] = mm(spread, gather)[:tasks, :classes]


def relay_kernel(in_ref, out_ref):
    out_ref[...] = in_ref[...]


def pick_kernel(info, *refs):
    *grads, out_ref, token = refs
    token[...] = jnp.zeros_like(token)
    for s, grad in enumerate(grads):

        @pl.when(info[0, 0] == s)
        def _(grad=grad):
            out_ref[...] = grad[: out_ref.shape[0], :]


def shape(dims, dtype):
    return jax.ShapeDtypeStruct(dims, dtype)


def held(dims, dtype):
    return pltpu.VMEM(dims, dtype)


def near(array):
    return pltpu.with_memory_space_constraint(array, pltpu.VMEM)


def far(array):
    return pltpu.with_memory_space_constraint(array, pltpu.HBM)


def call(kernel, name, out_shape, args, in_specs, out_specs=None, aliases=None, scratch=(), flops=0, limit=LIMIT, after=()):
    single = not isinstance(out_shape, tuple)
    if out_specs is None:
        out_specs = VMEM if single else (VMEM,) * len(out_shape)
    count, extra = len(args), len(after)

    def body(*refs):
        kernel(*refs[:count], *refs[count + extra :])

    args = tuple(args) + tuple(near(a) for a in after)
    in_specs = list(in_specs) + [ANY] * extra
    return pl.pallas_call(
        body,
        out_shape=out_shape,
        in_specs=in_specs,
        out_specs=out_specs,
        scratch_shapes=scratch,
        input_output_aliases=aliases or {},
        compiler_params=pltpu.CompilerParams(vmem_limit_bytes=limit * MIB),
        cost_estimate=pl.CostEstimate(flops=flops, bytes_accessed=0, transcendentals=0),
        name=name,
    )(*args)


def piece(kernel, args, specs, out_shape, out_specs=None, aliases=None, scratch=()):
    return kernel, tuple(args), list(specs), tuple(out_shape), out_specs or (VMEM,) * len(out_shape), aliases or {}, list(scratch)


def fused(name, pieces, **rest):
    counts = [(len(args), len(outs), len(scratch)) for _, args, _, outs, _, _, scratch in pieces]
    sums = [sum(c[i] for c in counts) for i in range(3)]

    def kernel(*refs):
        ins, outs, scratch = refs[: sums[0]], refs[sums[0] : sums[0] + sums[1]], refs[sums[0] + sums[1] :]
        for (part, *_), (a, b, c) in zip(pieces, counts):
            part(*ins[:a], *outs[:b], *scratch[:c])
            ins, outs, scratch = ins[a:], outs[b:], scratch[c:]

    aliases = {}
    a = b = 0
    for (_, _, _, _, _, own, _), count in zip(pieces, counts):
        aliases |= {a + i: b + o for i, o in own.items()}
        a, b = a + count[0], b + count[1]
    results = call(
        kernel,
        name,
        sum((p[3] for p in pieces), ()),
        sum((p[1] for p in pieces), ()),
        sum((p[2] for p in pieces), []),
        sum((tuple(p[4]) for p in pieces), ()),
        aliases=aliases,
        scratch=sum((p[6] for p in pieces), []),
        **rest,
    )
    split = []
    for count in counts:
        split.append(results[: count[1]])
        results = results[count[1] :]
    return split


def local(
    hidden_in, segment_ids, task_ids, labels, cotangent, qkv_weight, qv_bias, out_weight, out_bias, norm1_gain, norm1_bias,
    ffn_in_weight, ffn_in_bias, ffn_out_weight, ffn_out_bias, norm2_gain, norm2_bias, head_weight, head_bias,
):
    stages = lax.axis_size("pipe")
    stage = lax.axis_index("pipe")
    shards = lax.axis_size("dp")
    shard = lax.axis_index("dp")
    _, seq_len, width = hidden_in.shape
    hidden_width = ffn_in_weight.shape[2]
    task_count, _, class_count = head_weight.shape
    block = (seq_len + EXTRA, width)

    bits = shards.bit_length() - 1
    upward = list(range(1, bits))
    orders = (upward, upward[::-1])
    core = shard & 1
    sides = [jnp.where(core == 0, (shard >> orders[0][j]) & 1, (shard >> orders[1][j]) & 1) for j in range(bits - 1)]
    info = jnp.stack([stage, core] + sides + [stage] * (6 - len(sides))).astype(jnp.int32)
    info = near(jnp.broadcast_to(info[:, None], (8, 128)))

    home, vec, head_w = call(
        prepare_kernel,
        "prepare",
        (held(block, BF16), held((16, width), F32), held((16, width), F32)),
        tuple(
            far(a)
            for a in (
                hidden_in, segment_ids, qv_bias, out_bias, norm1_gain, norm1_bias, ffn_in_bias, ffn_out_bias, norm2_gain, norm2_bias,
                head_weight.transpose(2, 0, 1),
            )
        ),
        [VMEM] * 11,
    )
    weights = tuple(far(w) for w in (qkv_weight, out_weight, ffn_in_weight, ffn_out_weight)) + (near(vec),)
    weight_shapes = tuple(held(w.shape[1:], BF16) for w in weights[:4])

    def move(array, pairs):
        return lax.ppermute(array, "pipe", pairs)

    def route(tick):
        pairs = [(s, s + 1) for s in range(stages - 1) if 0 <= tick - 2 * s < stages]
        if tick + 2 < stages:
            pairs.append((tick + 2, 0))
        late = tick - 2 * (stages - 1)
        if 0 <= late < stages - 1:
            pairs.append((stages - 1, late))
        return pairs

    def back(tick):
        return [(b, a) for a, b in route(tick)]

    ticks = 2 * (stages - 1) + stages
    saved_shapes = (
        held((seq_len, width), BF16),
        held((seq_len, 3 * width), BF16),
        held((HEADS * seq_len, seq_len), BF16),
        held((seq_len, width), BF16),
        held((seq_len, width), F32),
        held((seq_len, width), BF16),
        held((seq_len, hidden_width), BF16),
        held((seq_len, hidden_width), BF16),
        held((seq_len, width), F32),
        held((seq_len, 256), F32),
    )
    arrived = {0: home, 1: move(home, [(1, 0)])}
    slots = [None] * stages
    last = None
    for tick in range(ticks):
        carry = 0 < tick + 2 < stages
        fresh = slots[tick % stages] is None
        args = [info, near(arrived[tick])] + ([near(home)] if carry else []) + list(weights)
        aliases = {}
        if not fresh:
            aliases = {len(args) + i: 1 + i for i in range(len(saved_shapes))}
            args += [near(a) for a in slots[tick % stages]]
        outs = call(
            partial(forward_kernel, tick, stages, carry, fresh),
            "layer_forward",
            (held(block, BF16),) + saved_shapes + (() if tick else weight_shapes),
            args,
            [ANY if a is w else VMEM for a in args for w in [next((w for w in weights[:4] if w is a and not tick), None)]],
            aliases=aliases,
            scratch=[] if tick else [pltpu.SemaphoreType.DMA((4,))],
            flops=4_000_000_000,
        )
        if tick == 0:
            weights = tuple(near(w) for w in outs[-4:]) + (near(vec),)
        slots[tick % stages] = tuple(outs[1:11])
        last = outs[0]
        if route(tick):
            arrived[tick + 2] = move(last, route(tick))
    finals = [arrived[2 * (stages - 1) + 2 + s] for s in range(stages - 1)] + [last]
    home, hidden_out, losses = call(
        head_kernel,
        "task_heads",
        (held(block, BF16), shape((seq_len, width), BF16), shape(task_ids.shape, F32)),
        [info, near(task_ids), near(labels), near(head_bias)] + [near(f) for f in finals] + [cotangent.reshape(seq_len, width), near(head_w)],
        [VMEM] * (stages + 6),
        scratch=[pltpu.VMEM(block, BF16)],
        flops=1_000_000_000,
    )

    arrived = {ticks - 1: home, ticks - 2: move(home, back(ticks - 2))}
    proj = [None] * stages
    sums = None
    results = {}
    for tick in reversed(range(1, ticks)):
        slot = tick % stages
        carry = tick < ticks - 1 and 0 <= tick - 2 - 2 * (stages - 1) + 0 or tick in (ticks - 1, ticks - 2)
        x, qkv, probs, context, unit_one, normed, hidden, slope, unit_two, scales = slots[slot]
        args = [info, near(arrived[tick])] + ([near(home)] if carry else []) + list(weights)
        aliases = {len(args): 1, len(args) + 1: 2}
        args += [near(a) for a in (qkv, slope, probs, unit_one, unit_two, scales)]
        fresh_proj, fresh_sums = proj[slot] is None, sums is None
        if not fresh_proj:
            aliases |= {len(args): 3, len(args) + 1: 4}
            args += [near(a) for a in proj[slot]]
        if not fresh_sums:
            aliases |= {len(args): 5}
            args += [near(sums)]
        last, d_mixed, d_pre, d_proj, d_down, sums = call(
            partial(backward_kernel, tick, stages, carry, fresh_proj, fresh_sums),
            "layer_backward",
            (
                held(block, BF16),
                held((seq_len, 3 * width), BF16),
                held((seq_len, hidden_width), BF16),
                held((seq_len, width), BF16),
                held((seq_len, width), BF16),
                held((SMALL, width), F32),
            ),
            args,
            [VMEM] + [VMEM] * (len(args) - 1),
            aliases=aliases,
            scratch=[pltpu.VMEM((seq_len, width), BF16)],
            flops=4_000_000_000,
        )
        proj[slot] = (d_proj, d_down)
        slots[slot] = (x, d_mixed, probs, context, unit_one, normed, hidden, d_pre, unit_two, scales)
        if tick >= 2:
            arrived[tick - 2] = move(last, back(tick - 2))
        if 2 <= tick < stages:
            results[tick] = arrived[tick - 2]

    def flip(bit):
        return [(i, i ^ (1 << bit)) for i in range(shards)]

    def across(step):
        return [(i, i ^ (1 << orders[i & 1][step])) for i in range(shards)]

    def swap(array, pairs):
        return lax.ppermute(array, "dp", pairs)

    second_last = last
    x, qkv, probs, context, unit_one, normed, hidden, slope, unit_two, scales = slots[0]
    qkv_w, out_w, in_w, down_w, vec = weights
    args = [info, near(arrived[0]), in_w, down_w, vec] + [near(a) for a in (slope, unit_one, unit_two, scales, proj[0][1], sums)]
    d_pre, d_down, sums, d_resid = call(
        partial(last_ffn_kernel, 0, stages),
        "last_ffn_backward",
        (held((seq_len, hidden_width), BF16), held((seq_len, width), BF16), held((SMALL, width), F32), held((seq_len, width), F32)),
        args,
        [VMEM] * len(args),
        aliases={5: 0, 9: 1, 10: 2},
    )
    LIGHT = 100_000_000
    tail = [d_resid]
    token = held((8, 128), F32)

    def run(name, *pieces, flops=10_000_000_000, **rest):
        split = fused(name, pieces, after=[tail[0]], flops=flops, **rest)
        tail[0] = split[-1][-1]
        return split

    unit = 16 * shards // 2
    half_hidden = hidden_width // 2
    small_start = 2 * width
    rows = {
        "down": half_hidden,
        "in": half_hidden * width // BLOCK,
        "attention": -(-(small_start + SMALL // 2) // unit) * unit,
    }
    mine, came = {}, {}

    def kept(index):
        return [near(slots[s][index]) for s in range(stages)]

    def products(p, theirs):
        if p == "down":
            kernel, arrays = down_weights, kept(6) + [near(d_down if s == 0 else proj[s][1]) for s in range(stages)]
        elif p == "in":
            kernel, arrays = in_weights, kept(5) + [near(d_pre if s == 0 else slots[s][7]) for s in range(stages)]
        else:
            kernel = attention_weights
            arrays = kept(0) + kept(3) + kept(1) + [near(proj[s][0]) for s in range(stages)] + [near(sums)]
        args = [info] + arrays
        return piece(partial(kernel, theirs), args, [VMEM] * len(args), (held((rows[p], width), BF16),))

    def split(p, step):
        out = held((mine[p].shape[0] // 2, width), BF16)
        ((mine[p], send),) = run("split_sum", flops=SPLIT, *(piece(partial(split_kernel, step), (info, near(mine[p]), near(came[p])), [VMEM] * 3, (out, out)),))
        came[p] = swap(send, across(step))

    def whole(p):
        ((mine[p],),) = run("last_sum", piece(add_kernel, (near(mine[p]), near(came[p])), [VMEM] * 2, (held(mine[p].shape, BF16),)), flops=WHOLE)
        came[p] = swap(mine[p], across(bits - 2))

    COST = {("attention", 1): J_A1, ("down", 0): J_D0, ("in", 0): J_I0, ("attention", 0): J_A0, ("down", 1): J_D1, ("in", 1): J_I1}

    def join(p, step, beside=()):
        out = held((2 * mine[p].shape[0], width), BF16)
        joined = piece(partial(join_kernel, step), (info, near(mine[p]), near(came[p])), [VMEM] * 3, (out,))
        *others, (mine[p],) = run("join", *beside, joined, flops=COST.get((p, step), HEAVY), limit=8)
        came[p] = swap(mine[p], across(step - 1) if step else flip(0))
        return others

    dims = {"down": ((1, hidden_width, width),), "in": ((1, width, hidden_width),), "attention": ((1, width, 3 * width), (1, width, width))}
    out_grads = {}

    def stored(p, sides):
        known = out_grads.get(p, ())
        parts = tuple(near(came[p] if theirs else mine[p]) for theirs in sides)
        args = (info,) + parts + tuple(far(g) for g in known)
        size = len(sides) * (2 * width if p == "attention" else rows[p])
        return piece(
            partial(store_kernel, p, sides, len(known)),
            args,
            [VMEM] * (1 + len(sides)) + [ANY] * len(known),
            tuple(pltpu.HBM(d, F32) for d in dims[p]) + (token,),
            (ANY,) * len(dims[p]) + (VMEM,),
            {1 + len(sides) + i: i for i in range(len(known))},
            [pltpu.VMEM((size, width), F32), pltpu.SemaphoreType.DMA((4 * len(sides),))],
        )

    ((theirs,),) = run("down_gradients", products("down", True), flops=LIGHT)
    came["down"] = swap(theirs, flip(0))
    (mine["down"],), (theirs,) = run("ffn_gradients", products("down", False), products("in", True), flops=LIGHT)
    came["in"] = swap(theirs, flip(0))
    split("down", 0)
    ((mine["in"],),) = run("in_gradients", products("in", False), flops=LIGHT)
    split("in", 0)
    args = [info, near(d_resid), qkv_w, out_w] + [near(a) for a in (probs, qkv, proj[0][0], sums)]
    ((last, d_mixed, d_proj, sums),) = run(
        "last_attention_backward",
        piece(
            partial(last_attention_kernel, 0, stages),
            args,
            [VMEM] * len(args),
            (held(block, BF16), held((seq_len, 3 * width), BF16), held((seq_len, width), BF16), held((SMALL, width), F32)),
            aliases={5: 1, 6: 2, 7: 3},
            scratch=[pltpu.VMEM((seq_len, width), BF16)],
        ),
        flops=LIGHT,
    )
    results[0] = last
    results[1] = second_last
    slots[0] = (x, d_mixed) + slots[0][2:]
    proj[0] = (d_proj, d_down)
    (theirs,), (mine["attention"],) = run("attention_gradients", products("attention", True), products("attention", False), flops=LIGHT)
    came["attention"] = swap(theirs, flip(0))
    split("down", 1)
    split("attention", 0)
    ((results[1],),) = run("relay", piece(relay_kernel, (near(results[1]),), [VMEM], (held(block, BF16),)))
    results[1] = move(results[1], [(0, 1)])
    pick = piece(
        pick_kernel, [info] + [near(results[s]) for s in range(stages)], [VMEM] * (1 + stages), (shape((seq_len, width), BF16), token)
    )
    moves = [partial(split, step=step) for step in range(1, bits - 1)] + [whole] + [partial(join, step=step) for step in reversed(range(bits - 1))]
    todo = {"in": moves[:-1], "down": moves[1:], "attention": moves[:-1]}
    while any(todo.values()):
        for p, steps in todo.items():
            if steps:
                steps.pop(0)(p)
                if p == "in" and len(steps) == PICK:
                    ((hidden_grad, _),) = run("pick_gradient", pick)
    (((*out_grads["down"], _)),) = join("in", 0, [stored("down", (False, True))])
    (((*out_grads["in"], _)),) = run("store", stored("in", (False,)), flops=STORE)
    join("attention", 0)
    (*out_grads["in"], _), (*out_grads["attention"], _) = run(
        "store", stored("in", (True,)), stored("attention", (False,)), limit=8, flops=HEAVY
    )
    vectors = tuple(shape((1, n), F32) for n in (2 * width, width, width, width, hidden_width, width, width, width))
    small = piece(
        partial(small_store_kernel, small_start),
        [info, near(mine["attention"]), near(came["attention"])],
        [VMEM] * 3,
        vectors + (shape((class_count, task_count, width), F32), shape((task_count, class_count), F32), token),
    )
    (*out_grads["attention"], _), (*vectors, head_w_grad, head_b_grad, _) = run("store", stored("attention", (True,)), small)
    qv_grad, out_b_grad, gain_one_grad, shift_one_grad, in_b_grad, down_b_grad, gain_two_grad, shift_two_grad = vectors
    return (
        hidden_out[None],
        losses,
        hidden_grad[None],
        out_grads["attention"][0],
        qv_grad,
        out_grads["attention"][1],
        out_b_grad,
        gain_one_grad,
        shift_one_grad,
        out_grads["in"][0],
        in_b_grad,
        out_grads["down"][0],
        down_b_grad,
        gain_two_grad,
        shift_two_grad,
        head_w_grad.transpose(1, 2, 0),
        head_b_grad,
    )


def solution(mesh):
    rows = P(("dp", "pipe"), None, None)
    ids = P(("dp", "pipe"), None)
    big = P("pipe", None, None)
    vec = P("pipe", None)
    return jax.shard_map(
        local,
        mesh=mesh,
        in_specs=(rows, ids, ids, ids, rows, big, vec, big, vec, vec, vec, big, vec, big, vec, vec, vec, P(), P()),
        out_specs=(rows, ids, rows, big, vec, big, vec, vec, vec, big, vec, big, vec, vec, vec, P(), P()),
        check_vma=False,
    )
```

```python
from functools import partial

import jax
import jax.numpy as jnp
from jax import lax
from jax.experimental import pallas as pl
from jax.experimental.pallas import tpu as pltpu
from jax.sharding import PartitionSpec as P

HEADS = 8
EPS = 1e-12
NEG = -1000000000.0
EXTRA = 16
SMALL = 32
BLOCK = 512
F32 = jnp.float32
BF16 = jnp.bfloat16
VMEM = pl.BlockSpec(memory_space=pltpu.VMEM)
ANY = pl.BlockSpec(memory_space=pl.ANY)
MIB = 1024 * 1024
PICK = 2
SPLIT = 20_000_000_000
WHOLE = 10_000_000_000
HEAVY = 10_000_000_000
J_A1 = 10_000_000_000
J_D0 = 100_000_000
J_I0 = 10_000_000_000
J_A0 = 10_000_000_000
J_D1 = 10_000_000_000
J_I1 = 10_000_000_000
STORE = 100_000_000
LIMIT = 6
QV_B, OUT_B, GAIN_ONE, SHIFT_ONE, IN_B, DOWN_B, GAIN_TWO, SHIFT_TWO = 0, 2, 3, 4, 5, 9, 10, 11


def mm(a, b):
    return lax.dot_general(a, b, (((1,), (0,)), ((), ())), preferred_element_type=F32)


def mm_nt(a, b):
    return lax.dot_general(a, b, (((1,), (1,)), ((), ())), preferred_element_type=F32)


def mm_tn(a, b):
    return lax.dot_general(a, b, (((0,), (0,)), ((), ())), preferred_element_type=F32)


def lane_masks(width):
    lanes = lax.broadcasted_iota(jnp.int32, (1, 2 * width), 1)
    return (lanes < width).astype(BF16), (lanes >= width).astype(BF16)


def segment_onehot(meta, count, seq_len):
    numbers = lax.broadcasted_iota(jnp.int32, (count, seq_len), 0).astype(F32)
    return (meta[0:1, :seq_len].astype(F32) == numbers).astype(F32)


def norm_stats(values):
    centre = values - jnp.mean(values, axis=-1, keepdims=True)
    spread = jnp.mean(centre * centre, axis=-1, keepdims=True)
    scale = lax.rsqrt(spread + EPS)
    return centre * scale, scale


def norm_back(grad, unit, scale, gain):
    scaled = grad * gain
    mean_one = jnp.mean(scaled, axis=-1, keepdims=True)
    mean_two = jnp.mean(scaled * unit, axis=-1, keepdims=True)
    return scale * (scaled - mean_one - unit * mean_two)


def column_sum(values):
    return jnp.sum(values.astype(F32), axis=0, keepdims=True)


def prepare_kernel(
    x_ref, seg_ref, qv_b, out_b, gain_one, shift_one, in_b, down_b, gain_two, shift_two, head_ref, block_ref, vec_ref, head_w_ref
):
    _, seq_len, width = x_ref.shape
    block_ref[:seq_len, :] = x_ref[0]
    block_ref[seq_len:, :] = jnp.zeros((EXTRA, width), BF16)
    block_ref[seq_len:, :seq_len] = jnp.broadcast_to(seg_ref[...].astype(F32).astype(BF16), (EXTRA, seq_len))
    row = 0
    for vector in (qv_b, out_b, gain_one, shift_one, in_b, down_b, gain_two, shift_two):
        for part in range(vector.shape[1] // width):
            vec_ref[row : row + 1, :] = vector[:, part * width : (part + 1) * width]
            row += 1
    classes, tasks, _ = head_ref.shape
    head_w_ref[...] = jnp.zeros_like(head_w_ref)
    for c in range(classes):
        head_w_ref[c * tasks : (c + 1) * tasks, :] = head_ref[c]


def forward_kernel(tick, stages, carry, fresh, info, x_ref, *refs):
    refs = list(refs)
    home_ref = refs.pop(0) if carry else None
    if tick == 0:
        vec, refs, sems = refs[4], refs[:4] + refs[5:-1], refs[-1]
        qkv_w, out_w, in_w, down_w = weights = refs[-4:]
        copies = [pltpu.make_async_copy(refs[i].at[0], weights[i], sems.at[i]) for i in range(4)]
        for copy in copies:
            copy.start()
        refs = refs[4:-4]
    else:
        copies = []
        qkv_w, out_w, in_w, down_w, vec = refs[:5]
        refs = refs[5:]

    def ready(*which):
        for i in which:
            if copies:
                copies[i].wait()

    if not fresh:
        refs = refs[10:]
    y_ref, keep_ref, qkv_ref, probs_ref, context_ref, unit_one_ref, normed_ref, hidden_ref, slope_ref, unit_two_ref, scales_ref = refs
    seq_len = x_ref.shape[0] - EXTRA
    width = x_ref.shape[1]
    head_dim = width // HEADS
    place = tick - 2 * info[0, 0]
    active = (place >= 0) & (place < stages)

    if carry:

        @pl.when(jnp.logical_not(active))
        def _():
            y_ref[...] = home_ref[...]
            ready(0, 1, 2, 3)

    @pl.when(active)
    def _():
        meta = x_ref[seq_len:, :]
        y_ref[seq_len:, :] = meta
        x = x_ref[:seq_len, :]
        keep_ref[...] = x
        onehot = segment_onehot(meta, EXTRA, seq_len).astype(BF16)
        barred = jnp.where(mm_tn(onehot, onehot) > 0.5, 0.0, NEG)
        ready(0)
        q = (mm(x, qkv_w[:, :width]) + vec[QV_B : QV_B + 1]).astype(BF16)
        k = mm(x, qkv_w[:, width : 2 * width]).astype(BF16)
        v = (mm(x, qkv_w[:, 2 * width :]) + vec[QV_B + 1 : QV_B + 2]).astype(BF16)
        qkv_ref[:, :width] = q
        qkv_ref[:, width : 2 * width] = k
        qkv_ref[:, 2 * width :] = v
        v_t = v.T
        mask_a, mask_b = lane_masks(head_dim)
        factor = head_dim**-0.5

        def raw_scores(pair):
            cols = slice(pair * 2 * head_dim, (pair + 1) * 2 * head_dim)
            k_two = jnp.concatenate([k[:, cols] * (mask * factor).astype(BF16) for mask in (mask_a, mask_b)], axis=0)
            return mm_nt(k_two, q[:, cols])

        context_parts = []
        shares = []
        ahead = raw_scores(0)
        for pair in range(HEADS // 2):
            both = ahead
            if pair + 1 < HEADS // 2:
                ahead = raw_scores(pair + 1)
            for side in range(2):
                head = 2 * pair + side
                scores = both[side * seq_len : (side + 1) * seq_len] + barred
                expo = jnp.exp(scores - jnp.max(scores, axis=0, keepdims=True))
                share = 1.0 / jnp.sum(expo, axis=0, keepdims=True)
                expo_low = expo.astype(BF16)
                probs_ref[head * seq_len : (head + 1) * seq_len, :] = expo_low
                shares.append(share)
                context_parts.append(mm(v_t[head * head_dim : (head + 1) * head_dim, :], expo_low) * share)
        context = jnp.concatenate(context_parts, axis=0).T.astype(BF16)
        scales_ref[:, 256 : 256 + HEADS] = jnp.concatenate(shares, axis=0).T
        context_ref[...] = context
        ready(1)
        resid = x.astype(F32) + mm(context, out_w[...]) + vec[OUT_B : OUT_B + 1]
        unit_one, scale_one = norm_stats(resid)
        unit_one_ref[...] = unit_one
        normed = unit_one * vec[GAIN_ONE : GAIN_ONE + 1] + vec[SHIFT_ONE : SHIFT_ONE + 1]
        normed_low = normed.astype(BF16)
        normed_ref[...] = normed_low
        summed = normed + vec[DOWN_B : DOWN_B + 1]
        ready(2, 3)
        parts = in_w.shape[1] // BLOCK
        ahead = mm(normed_low, in_w[:, :BLOCK])
        for part in range(parts):
            cols = slice(part * BLOCK, (part + 1) * BLOCK)
            pre = ahead + vec[IN_B + part : IN_B + part + 1]
            if part + 1 < parts:
                ahead = mm(normed_low, in_w[:, (part + 1) * BLOCK : (part + 2) * BLOCK])
            gate = 0.5 + 0.5 * lax.erf(pre * (0.5**0.5))
            slope_ref[:, cols] = (gate + pre * (jnp.exp(-0.5 * pre * pre) * 0.3989422804014327)).astype(BF16)
            hidden = (pre * gate).astype(BF16)
            hidden_ref[:, cols] = hidden
            summed = summed + mm(hidden, down_w[cols, :])
        unit_two, scale_two = norm_stats(summed)
        unit_two_ref[...] = unit_two
        y_ref[:seq_len, :] = (unit_two * vec[GAIN_TWO : GAIN_TWO + 1] + vec[SHIFT_TWO : SHIFT_TWO + 1]).astype(BF16)
        scales_ref[:, 0:128] = jnp.broadcast_to(scale_one, (seq_len, 128))
        scales_ref[:, 128:256] = jnp.broadcast_to(scale_two, (seq_len, 128))


def head_kernel(info, task_ref, label_ref, head_b_ref, *refs):
    stages = len(refs) - 6
    y_refs = refs[:stages]
    cot_ref, head_w, g_ref, final_ref, loss_ref, picked = refs[stages:]
    for s in range(stages):

        @pl.when(info[0, 0] == s)
        def _(s=s):
            picked[...] = y_refs[s][...]

    seq_len, width = final_ref.shape
    task_count, class_count = head_b_ref.shape
    seg_count = task_ref.shape[1]
    high = lax.Precision.HIGHEST
    y = picked[:seq_len, :]
    final_ref[...] = y
    meta = picked[seq_len:, :]
    segs = 8
    onehot = segment_onehot(meta, segs, seq_len)
    row = meta[0:1, :seq_len].astype(F32)
    lanes = lax.broadcasted_iota(jnp.int32, (1, seq_len), 1)
    previous = jnp.where(lanes == 0, -1.0, pltpu.roll(row, 1, 1))
    pick = onehot * (row != previous).astype(F32)
    live = jnp.max(pick, axis=1, keepdims=True)
    cls = mm(pick.astype(BF16), y)
    logits = lax.dot_general(cls, head_w[...], (((1,), (1,)), ((), ())), precision=high, preferred_element_type=F32)
    slots = lax.broadcasted_iota(jnp.int32, (1, logits.shape[1]), 1)
    bias = jnp.zeros((1, logits.shape[1]), F32)
    for t in range(task_count):
        for c in range(class_count):
            bias = jnp.where(slots == c * task_count + t, head_b_ref[t, c], bias)
    logits = logits + bias
    numbers = lax.broadcasted_iota(jnp.int32, (segs, 1), 0)
    task = jnp.zeros((segs, 1), jnp.int32)
    label = jnp.zeros((segs, 1), jnp.int32)
    for s in range(seg_count):
        task = jnp.where(numbers == s, task_ref[0, s], task)
        label = jnp.where(numbers == s, label_ref[0, s], label)
    mine = jnp.zeros(logits.shape, jnp.bool_)
    for c in range(class_count):
        mine = mine | (slots == task + c * task_count)
    label_hot = slots == task + label * task_count
    masked = jnp.where(mine, logits, -jnp.inf)
    top = jnp.max(masked, axis=1, keepdims=True)
    expo = jnp.exp(masked - top)
    total = jnp.sum(expo, axis=1, keepdims=True)
    right = jnp.sum(jnp.where(label_hot, logits, 0.0), axis=1, keepdims=True)
    loss = live * (top + jnp.log(total) - right)
    wide = lax.broadcasted_iota(jnp.int32, (segs, 128), 1)
    loss_row = jnp.sum(jnp.where(wide == numbers, loss, 0.0), axis=0, keepdims=True)
    loss_ref[...] = loss_row[:, :seg_count]
    d_logits = live * (expo / total - label_hot.astype(F32))
    d_cls = lax.dot_general(d_logits, head_w[...], (((1,), (0,)), ((), ())), precision=high, preferred_element_type=F32)
    d_final = lax.dot_general(pick, d_cls, (((0,), (0,)), ((), ())), precision=high, preferred_element_type=F32)
    g_ref[:seq_len, :] = (cot_ref[...].astype(F32) + d_final).astype(BF16)
    g_w = lax.dot_general(d_logits, cls, (((0,), (0,)), ((), ())), precision=high, preferred_element_type=F32)
    g_b = jnp.concatenate([column_sum(d_logits)] * (width // logits.shape[1]), axis=1)
    rows = lax.broadcasted_iota(jnp.int32, (EXTRA, 1), 0)
    count = task_count * class_count
    g_ref[seq_len:, :] = jnp.where(rows < count, g_w[:EXTRA], jnp.where(rows == count, g_b, 0.0)).astype(BF16)


def adder(sums_ref):
    def add(row, value):
        sums_ref[row : row + 1, :] += value

    return add


def ffn_back(g_ref, slope_ref, unit_one_ref, unit_two_ref, scales_ref, in_w, down_w, vec, d_pre_ref, d_down_ref, sums_ref):
    seq_len = g_ref.shape[0] - EXTRA
    add = adder(sums_ref)
    sums_ref[SMALL - EXTRA :, :] += g_ref[seq_len:, :].astype(F32)
    grad = g_ref[:seq_len, :].astype(F32)
    scale_one = scales_ref[:, 0:1]
    scale_two = scales_ref[:, 128:129]
    unit_two = unit_two_ref[...]
    add(GAIN_TWO, column_sum(grad * unit_two))
    add(SHIFT_TWO, column_sum(grad))
    d_summed = norm_back(grad, unit_two, scale_two, vec[GAIN_TWO : GAIN_TWO + 1])
    d_down = d_summed.astype(BF16)
    d_down_ref[...] = d_down
    add(DOWN_B, column_sum(d_down))
    d_normed = d_summed
    for part in range(in_w.shape[1] // BLOCK):
        cols = slice(part * BLOCK, (part + 1) * BLOCK)
        d_pre = (mm_nt(d_down, down_w[cols, :]) * slope_ref[:, cols].astype(F32)).astype(BF16)
        d_pre_ref[:, cols] = d_pre
        add(IN_B + part, column_sum(d_pre))
        d_normed = d_normed + mm_nt(d_pre, in_w[:, cols])
    unit_one = unit_one_ref[...]
    add(GAIN_ONE, column_sum(d_normed * unit_one))
    add(SHIFT_ONE, column_sum(d_normed))
    return norm_back(d_normed, unit_one, scale_one, vec[GAIN_ONE : GAIN_ONE + 1])


def attention_back(d_resid, qkv_ref, probs_ref, scales_ref, qkv_w, out_w, next_ref, d_mixed_ref, d_proj_ref, sums_ref, queries):
    seq_len, width = d_resid.shape
    head_dim = width // HEADS
    add = adder(sums_ref)
    d_proj = d_resid.astype(BF16)
    d_proj_ref[...] = d_proj
    add(OUT_B, column_sum(d_proj))
    d_context = mm_nt(d_proj, out_w[...])
    factor = head_dim**-0.5
    mask_a, mask_b = lane_masks(head_dim)
    queries[...] = qkv_ref[:, :width]
    keys = qkv_ref[:, width : 2 * width]
    k_t = (keys * jnp.asarray(factor, BF16)).T
    shares = scales_ref[:, 256 : 256 + HEADS]
    share_rows = shares.T
    d_query_parts = []
    first = lax.broadcasted_iota(jnp.int32, (seq_len, 2 * head_dim), 1) < head_dim

    def weight_gradients_of(pair):
        cols = slice(pair * 2 * head_dim, (pair + 1) * 2 * head_dim)
        v_cols = qkv_ref[:, slice(cols.start + 2 * width, cols.stop + 2 * width)]
        scale = jnp.where(first, shares[:, 2 * pair : 2 * pair + 1], shares[:, 2 * pair + 1 : 2 * pair + 2])
        scaled = (d_context[:, cols] * scale).astype(BF16)
        v_two = jnp.concatenate([v_cols * mask for mask in (mask_a, mask_b)], axis=0)
        return scaled, mm_nt(v_two, scaled)

    ahead = weight_gradients_of(0)
    for pair in range(HEADS // 2):
        scaled, d_probs = ahead
        if pair + 1 < HEADS // 2:
            ahead = weight_gradients_of(pair + 1)
        cols = slice(pair * 2 * head_dim, (pair + 1) * 2 * head_dim)
        rows = slice(pair * 2 * seq_len, (pair + 1) * 2 * seq_len)
        probs = probs_ref[rows, :]
        d_values = mm(probs, scaled)
        parts = []
        for side in range(2):
            half = slice(side * seq_len, (side + 1) * seq_len)
            head = 2 * pair + side
            probs_wide = probs[half].astype(F32)
            total = jnp.sum(probs_wide * d_probs[half], axis=0, keepdims=True) * share_rows[head : head + 1, :]
            d_scores = (probs_wide * (d_probs[half] - total)).astype(BF16)
            parts.append(d_scores)
            d_query_parts.append(mm(k_t[head * head_dim : (head + 1) * head_dim, :], d_scores))
        d_keys = mm(jnp.concatenate(parts, axis=0), queries[:, cols] * jnp.asarray(factor, BF16))
        d_mixed_ref[:, slice(cols.start + width, cols.stop + width)] = jnp.where(first, d_keys[:seq_len], d_keys[seq_len:]).astype(BF16)
        d_mixed_ref[:, slice(cols.start + 2 * width, cols.stop + 2 * width)] = jnp.where(
            first, d_values[:seq_len], d_values[seq_len:]
        ).astype(BF16)
    d_queries = jnp.concatenate(d_query_parts, axis=0).T.astype(BF16)
    d_mixed_ref[:, :width] = d_queries
    add(QV_B, column_sum(d_queries))
    add(QV_B + 1, column_sum(d_mixed_ref[:, 2 * width :]))
    d_input = d_resid + mm_nt(d_mixed_ref[...], qkv_w[...])
    next_ref[:seq_len, :] = d_input.astype(BF16)


def is_active(info, tick, stages):
    place = tick - 2 * info[0, 0]
    return (place >= 0) & (place < stages)


def backward_kernel(tick, stages, carry, fresh_proj, fresh_sums, info, g_ref, *refs):
    refs = list(refs)
    home_ref = refs.pop(0) if carry else None
    qkv_w, out_w, in_w, down_w, vec = refs[:5]
    qkv_ref, slope_ref, probs_ref, unit_one_ref, unit_two_ref, scales_ref = refs[5:11]
    refs = refs[11:]
    if not fresh_proj:
        refs = refs[2:]
    if not fresh_sums:
        refs = refs[1:]
    next_ref, d_mixed_ref, d_pre_ref, d_proj_ref, d_down_ref, sums_ref, queries = refs
    seq_len = g_ref.shape[0] - EXTRA
    active = is_active(info, tick, stages)

    if carry:

        @pl.when(jnp.logical_not(active))
        def _():
            next_ref[...] = home_ref[...]

    if fresh_sums:
        sums_ref[...] = jnp.zeros_like(sums_ref)

    @pl.when(active)
    def _():
        next_ref[seq_len:, :] = g_ref[seq_len:, :]
        d_resid = ffn_back(
            g_ref, slope_ref, unit_one_ref, unit_two_ref, scales_ref, in_w, down_w, vec, d_pre_ref, d_down_ref, sums_ref
        )
        attention_back(d_resid, qkv_ref, probs_ref, scales_ref, qkv_w, out_w, next_ref, d_mixed_ref, d_proj_ref, sums_ref, queries)


def last_ffn_kernel(
    tick, stages, info, g_ref, in_w, down_w, vec, slope_ref, unit_one_ref, unit_two_ref, scales_ref, d_down_in, sums_in,
    d_pre_ref, d_down_ref, sums_ref, d_resid_ref,
):
    @pl.when(is_active(info, tick, stages))
    def _():
        d_resid_ref[...] = ffn_back(
            g_ref, slope_ref, unit_one_ref, unit_two_ref, scales_ref, in_w, down_w, vec, d_pre_ref, d_down_ref, sums_ref
        )


def last_attention_kernel(
    tick, stages, info, d_resid_ref, qkv_w, out_w, probs_ref, scales_ref, qkv_ref, d_proj_in, sums_in,
    next_ref, d_mixed_ref, d_proj_ref, sums_ref, queries,
):
    @pl.when(is_active(info, tick, stages))
    def _():
        attention_back(d_resid_ref[...], qkv_ref, probs_ref, scales_ref, qkv_w, out_w, next_ref, d_mixed_ref, d_proj_ref, sums_ref, queries)


def half_of(info, theirs):
    return 1 - info[1, 0] if theirs else info[1, 0]


def outer(left, right, rows=None, cols=None):
    rows = slice(None) if rows is None else rows
    cols = slice(None) if cols is None else cols
    return sum(mm_tn(a[:, rows], b[:, cols]) for a, b in zip(left, right))


def down_weights(theirs, info, *refs):
    *refs, out_ref = refs
    hidden, d_down = refs[: len(refs) // 2], refs[len(refs) // 2 :]
    span = hidden[0].shape[1] // 2
    for start in range(0, span, BLOCK):
        at = pl.ds(pl.multiple_of(half_of(info, theirs) * span + start, BLOCK), BLOCK)
        out_ref[start : start + BLOCK, :] = outer(hidden, d_down, rows=at).astype(BF16)


def in_weights(theirs, info, *refs):
    *refs, out_ref = refs
    normed, d_pre = refs[: len(refs) // 2], refs[len(refs) // 2 :]
    width = normed[0].shape[1]
    span = d_pre[0].shape[1] // 2
    for part in range(span // BLOCK):
        at = pl.ds(pl.multiple_of(half_of(info, theirs) * span + part * BLOCK, BLOCK), BLOCK)
        out_ref[part * width : (part + 1) * width, :] = outer(normed, d_pre, cols=at).astype(BF16)


def attention_weights(theirs, info, *refs):
    *refs, sums_ref, out_ref = refs
    slots = len(refs) // 4
    x, context, d_mixed, d_proj = (refs[i * slots : (i + 1) * slots] for i in range(4))
    half = half_of(info, theirs)
    width = x[0].shape[1]
    span = width // 2
    at = pl.ds(pl.multiple_of(half * span, span), span)
    for part in range(3):
        cols = slice(part * width, (part + 1) * width)
        out_ref[part * span : (part + 1) * span, :] = outer(x, d_mixed, rows=at, cols=cols).astype(BF16)
    out_ref[3 * span : 4 * span, :] = outer(context, d_proj, rows=at).astype(BF16)
    out_ref[4 * span :, :] = jnp.zeros((out_ref.shape[0] - 4 * span, width), BF16)
    share = SMALL // 2
    out_ref[4 * span : 4 * span + share, :] = sums_ref[pl.ds(pl.multiple_of(half * share, share), share), :].astype(BF16)


def split_kernel(step, info, mine_ref, came_ref, keep_ref, send_ref):
    rows = keep_ref.shape[0]
    bit = info[2 + step, 0]
    for ref, side in ((send_ref, 1 - bit), (keep_ref, bit)):
        at = pl.ds(pl.multiple_of(side * rows, 16), rows)
        ref[...] = (mine_ref[at, :].astype(F32) + came_ref[at, :].astype(F32)).astype(BF16)


def add_kernel(mine_ref, came_ref, out_ref):
    out_ref[...] = (mine_ref[...].astype(F32) + came_ref[...].astype(F32)).astype(BF16)


def join_kernel(step, info, mine_ref, came_ref, out_ref):
    rows = mine_ref.shape[0]
    bit = info[2 + step, 0]
    out_ref[pl.ds(pl.multiple_of(bit * rows, 16), rows), :] = mine_ref[...]
    out_ref[pl.ds(pl.multiple_of((1 - bit) * rows, 16), rows), :] = came_ref[...]


def store_kernel(name, sides, known, info, *refs):
    parts = refs[: len(sides)]
    token, stage_ref, sems = refs[-3:]
    outs = refs[len(sides) + known : -3]
    token[...] = jnp.zeros_like(token)
    copies = []
    row = 0
    for theirs, part_ref in zip(sides, parts):
        half = half_of(info, theirs)
        width = part_ref.shape[1]
        targets = []
        if name == "down":
            span = outs[0].shape[1] // 2
            for start in range(0, span, BLOCK):
                targets.append((BLOCK, outs[0].at[0, pl.ds(pl.multiple_of(half * span + start, BLOCK), BLOCK), :]))
        elif name == "in":
            span = outs[0].shape[2] // 2
            for start in range(0, span, BLOCK):
                targets.append((width, outs[0].at[0, :, pl.ds(pl.multiple_of(half * span + start, BLOCK), BLOCK)]))
        else:
            span = width // 2
            at = pl.ds(pl.multiple_of(half * span, span), span)
            targets = [(span, outs[0].at[0, at, i * width : (i + 1) * width]) for i in range(3)] + [(span, outs[1].at[0, at, :])]
        start = 0
        for size, dst in targets:
            stage_ref[row : row + size, :] = part_ref[start : start + size, :].astype(F32)
            copies.append(pltpu.make_async_copy(stage_ref.at[row : row + size], dst, sems.at[len(copies)]))
            copies[-1].start()
            start += size
            row += size
    for copy in copies:
        copy.wait()


def small_store_kernel(
    start, info, mine_ref, came_ref, qv_b, out_b, gain_one, shift_one, in_b, down_b, gain_two, shift_two, head_w, head_b, token
):
    token[...] = jnp.zeros_like(token)
    share = SMALL // 2
    mine = mine_ref[start : start + share, :].astype(F32)
    came = came_ref[start : start + share, :].astype(F32)
    first = info[1, 0] == 0
    low = jnp.where(first, mine, came)
    high = jnp.where(first, came, mine)
    width = low.shape[1]
    row = 0
    for vector in (qv_b, out_b, gain_one, shift_one, in_b, down_b, gain_two, shift_two):
        for part in range(vector.shape[1] // width):
            vector[:, part * width : (part + 1) * width] = low[row : row + 1, :]
            row += 1
    classes, tasks, _ = head_w.shape
    for c in range(classes):
        head_w[c] = high[c * tasks : (c + 1) * tasks, :]
    line = high[classes * tasks : classes * tasks + 1, :128]
    lanes = lax.broadcasted_iota(jnp.int32, (16, 128), 1)
    spread = jnp.where(lanes % tasks == lax.broadcasted_iota(jnp.int32, (16, 128), 0), line, 0.0).astype(BF16)
    gather = (lax.broadcasted_iota(jnp.int32, (128, 128), 0) // tasks == lax.broadcasted_iota(jnp.int32, (128, 128), 1)).astype(BF16)
    head_b[...] = mm(spread, gather)[:tasks, :classes]


def relay_kernel(in_ref, out_ref):
    out_ref[...] = in_ref[...]


def pick_kernel(info, *refs):
    *grads, out_ref, token = refs
    token[...] = jnp.zeros_like(token)
    for s, grad in enumerate(grads):

        @pl.when(info[0, 0] == s)
        def _(grad=grad):
            out_ref[...] = grad[: out_ref.shape[0], :]


def shape(dims, dtype):
    return jax.ShapeDtypeStruct(dims, dtype)


def held(dims, dtype):
    return pltpu.VMEM(dims, dtype)


def near(array):
    return pltpu.with_memory_space_constraint(array, pltpu.VMEM)


def far(array):
    return pltpu.with_memory_space_constraint(array, pltpu.HBM)


def call(kernel, name, out_shape, args, in_specs, out_specs=None, aliases=None, scratch=(), flops=0, limit=LIMIT, after=()):
    single = not isinstance(out_shape, tuple)
    if out_specs is None:
        out_specs = VMEM if single else (VMEM,) * len(out_shape)
    count, extra = len(args), len(after)

    def body(*refs):
        kernel(*refs[:count], *refs[count + extra :])

    args = tuple(args) + tuple(near(a) for a in after)
    in_specs = list(in_specs) + [ANY] * extra
    return pl.pallas_call(
        body,
        out_shape=out_shape,
        in_specs=in_specs,
        out_specs=out_specs,
        scratch_shapes=scratch,
        input_output_aliases=aliases or {},
        compiler_params=pltpu.CompilerParams(vmem_limit_bytes=limit * MIB),
        cost_estimate=pl.CostEstimate(flops=flops, bytes_accessed=0, transcendentals=0),
        name=name,
    )(*args)


def piece(kernel, args, specs, out_shape, out_specs=None, aliases=None, scratch=()):
    return kernel, tuple(args), list(specs), tuple(out_shape), out_specs or (VMEM,) * len(out_shape), aliases or {}, list(scratch)


def fused(name, pieces, **rest):
    counts = [(len(args), len(outs), len(scratch)) for _, args, _, outs, _, _, scratch in pieces]
    sums = [sum(c[i] for c in counts) for i in range(3)]

    def kernel(*refs):
        ins, outs, scratch = refs[: sums[0]], refs[sums[0] : sums[0] + sums[1]], refs[sums[0] + sums[1] :]
        for (part, *_), (a, b, c) in zip(pieces, counts):
            part(*ins[:a], *outs[:b], *scratch[:c])
            ins, outs, scratch = ins[a:], outs[b:], scratch[c:]

    aliases = {}
    a = b = 0
    for (_, _, _, _, _, own, _), count in zip(pieces, counts):
        aliases |= {a + i: b + o for i, o in own.items()}
        a, b = a + count[0], b + count[1]
    results = call(
        kernel,
        name,
        sum((p[3] for p in pieces), ()),
        sum((p[1] for p in pieces), ()),
        sum((p[2] for p in pieces), []),
        sum((tuple(p[4]) for p in pieces), ()),
        aliases=aliases,
        scratch=sum((p[6] for p in pieces), []),
        **rest,
    )
    split = []
    for count in counts:
        split.append(results[: count[1]])
        results = results[count[1] :]
    return split


def local(
    hidden_in, segment_ids, task_ids, labels, cotangent, qkv_weight, qv_bias, out_weight, out_bias, norm1_gain, norm1_bias,
    ffn_in_weight, ffn_in_bias, ffn_out_weight, ffn_out_bias, norm2_gain, norm2_bias, head_weight, head_bias,
):
    stages = lax.axis_size("pipe")
    stage = lax.axis_index("pipe")
    shards = lax.axis_size("dp")
    shard = lax.axis_index("dp")
    _, seq_len, width = hidden_in.shape
    hidden_width = ffn_in_weight.shape[2]
    task_count, _, class_count = head_weight.shape
    block = (seq_len + EXTRA, width)

    bits = shards.bit_length() - 1
    upward = list(range(1, bits))
    orders = (upward, upward[::-1])
    core = shard & 1
    sides = [jnp.where(core == 0, (shard >> orders[0][j]) & 1, (shard >> orders[1][j]) & 1) for j in range(bits - 1)]
    info = jnp.stack([stage, core] + sides + [stage] * (6 - len(sides))).astype(jnp.int32)
    info = near(jnp.broadcast_to(info[:, None], (8, 128)))

    home, vec, head_w = call(
        prepare_kernel,
        "prepare",
        (held(block, BF16), held((16, width), F32), held((16, width), F32)),
        tuple(
            far(a)
            for a in (
                hidden_in, segment_ids, qv_bias, out_bias, norm1_gain, norm1_bias, ffn_in_bias, ffn_out_bias, norm2_gain, norm2_bias,
                head_weight.transpose(2, 0, 1),
            )
        ),
        [VMEM] * 11,
    )
    weights = tuple(far(w) for w in (qkv_weight, out_weight, ffn_in_weight, ffn_out_weight)) + (near(vec),)
    weight_shapes = tuple(held(w.shape[1:], BF16) for w in weights[:4])

    def move(array, pairs):
        return lax.ppermute(array, "pipe", pairs)

    def route(tick):
        pairs = [(s, s + 1) for s in range(stages - 1) if 0 <= tick - 2 * s < stages]
        if tick + 2 < stages:
            pairs.append((tick + 2, 0))
        late = tick - 2 * (stages - 1)
        if 0 <= late < stages - 1:
            pairs.append((stages - 1, late))
        return pairs

    def back(tick):
        return [(b, a) for a, b in route(tick)]

    ticks = 2 * (stages - 1) + stages
    saved_shapes = (
        held((seq_len, width), BF16),
        held((seq_len, 3 * width), BF16),
        held((HEADS * seq_len, seq_len), BF16),
        held((seq_len, width), BF16),
        held((seq_len, width), F32),
        held((seq_len, width), BF16),
        held((seq_len, hidden_width), BF16),
        held((seq_len, hidden_width), BF16),
        held((seq_len, width), F32),
        held((seq_len, 384), F32),
    )
    arrived = {0: home, 1: move(home, [(1, 0)])}
    slots = [None] * stages
    last = None
    for tick in range(ticks):
        carry = 0 < tick + 2 < stages
        fresh = slots[tick % stages] is None
        args = [info, near(arrived[tick])] + ([near(home)] if carry else []) + list(weights)
        aliases = {}
        if not fresh:
            aliases = {len(args) + i: 1 + i for i in range(len(saved_shapes))}
            args += [near(a) for a in slots[tick % stages]]
        outs = call(
            partial(forward_kernel, tick, stages, carry, fresh),
            "layer_forward",
            (held(block, BF16),) + saved_shapes + (() if tick else weight_shapes),
            args,
            [ANY if a is w else VMEM for a in args for w in [next((w for w in weights[:4] if w is a and not tick), None)]],
            aliases=aliases,
            scratch=[] if tick else [pltpu.SemaphoreType.DMA((4,))],
            flops=4_000_000_000,
        )
        if tick == 0:
            weights = tuple(near(w) for w in outs[-4:]) + (near(vec),)
        slots[tick % stages] = tuple(outs[1:11])
        last = outs[0]
        if route(tick):
            arrived[tick + 2] = move(last, route(tick))
    finals = [arrived[2 * (stages - 1) + 2 + s] for s in range(stages - 1)] + [last]
    home, hidden_out, losses = call(
        head_kernel,
        "task_heads",
        (held(block, BF16), shape((seq_len, width), BF16), shape(task_ids.shape, F32)),
        [info, near(task_ids), near(labels), near(head_bias)] + [near(f) for f in finals] + [cotangent.reshape(seq_len, width), near(head_w)],
        [VMEM] * (stages + 6),
        scratch=[pltpu.VMEM(block, BF16)],
        flops=1_000_000_000,
    )

    arrived = {ticks - 1: home, ticks - 2: move(home, back(ticks - 2))}
    proj = [None] * stages
    sums = None
    results = {}
    for tick in reversed(range(1, ticks)):
        slot = tick % stages
        carry = tick < ticks - 1 and 0 <= tick - 2 - 2 * (stages - 1) + 0 or tick in (ticks - 1, ticks - 2)
        x, qkv, probs, context, unit_one, normed, hidden, slope, unit_two, scales = slots[slot]
        args = [info, near(arrived[tick])] + ([near(home)] if carry else []) + list(weights)
        aliases = {len(args): 1, len(args) + 1: 2}
        args += [near(a) for a in (qkv, slope, probs, unit_one, unit_two, scales)]
        fresh_proj, fresh_sums = proj[slot] is None, sums is None
        if not fresh_proj:
            aliases |= {len(args): 3, len(args) + 1: 4}
            args += [near(a) for a in proj[slot]]
        if not fresh_sums:
            aliases |= {len(args): 5}
            args += [near(sums)]
        last, d_mixed, d_pre, d_proj, d_down, sums = call(
            partial(backward_kernel, tick, stages, carry, fresh_proj, fresh_sums),
            "layer_backward",
            (
                held(block, BF16),
                held((seq_len, 3 * width), BF16),
                held((seq_len, hidden_width), BF16),
                held((seq_len, width), BF16),
                held((seq_len, width), BF16),
                held((SMALL, width), F32),
            ),
            args,
            [VMEM] + [VMEM] * (len(args) - 1),
            aliases=aliases,
            scratch=[pltpu.VMEM((seq_len, width), BF16)],
            flops=4_000_000_000,
        )
        proj[slot] = (d_proj, d_down)
        slots[slot] = (x, d_mixed, probs, context, unit_one, normed, hidden, d_pre, unit_two, scales)
        if tick >= 2:
            arrived[tick - 2] = move(last, back(tick - 2))
        if 2 <= tick < stages:
            results[tick] = arrived[tick - 2]

    def flip(bit):
        return [(i, i ^ (1 << bit)) for i in range(shards)]

    def across(step):
        return [(i, i ^ (1 << orders[i & 1][step])) for i in range(shards)]

    def swap(array, pairs):
        return lax.ppermute(array, "dp", pairs)

    second_last = last
    x, qkv, probs, context, unit_one, normed, hidden, slope, unit_two, scales = slots[0]
    qkv_w, out_w, in_w, down_w, vec = weights
    args = [info, near(arrived[0]), in_w, down_w, vec] + [near(a) for a in (slope, unit_one, unit_two, scales, proj[0][1], sums)]
    d_pre, d_down, sums, d_resid = call(
        partial(last_ffn_kernel, 0, stages),
        "last_ffn_backward",
        (held((seq_len, hidden_width), BF16), held((seq_len, width), BF16), held((SMALL, width), F32), held((seq_len, width), F32)),
        args,
        [VMEM] * len(args),
        aliases={5: 0, 9: 1, 10: 2},
    )
    LIGHT = 100_000_000
    tail = [d_resid]
    token = held((8, 128), F32)

    def run(name, *pieces, flops=10_000_000_000, **rest):
        split = fused(name, pieces, after=[tail[0]], flops=flops, **rest)
        tail[0] = split[-1][-1]
        return split

    unit = 16 * shards // 2
    half_hidden = hidden_width // 2
    small_start = 2 * width
    rows = {
        "down": half_hidden,
        "in": half_hidden * width // BLOCK,
        "attention": -(-(small_start + SMALL // 2) // unit) * unit,
    }
    mine, came = {}, {}

    def kept(index):
        return [near(slots[s][index]) for s in range(stages)]

    def products(p, theirs):
        if p == "down":
            kernel, arrays = down_weights, kept(6) + [near(d_down if s == 0 else proj[s][1]) for s in range(stages)]
        elif p == "in":
            kernel, arrays = in_weights, kept(5) + [near(d_pre if s == 0 else slots[s][7]) for s in range(stages)]
        else:
            kernel = attention_weights
            arrays = kept(0) + kept(3) + kept(1) + [near(proj[s][0]) for s in range(stages)] + [near(sums)]
        args = [info] + arrays
        return piece(partial(kernel, theirs), args, [VMEM] * len(args), (held((rows[p], width), BF16),))

    def split(p, step):
        out = held((mine[p].shape[0] // 2, width), BF16)
        ((mine[p], send),) = run("split_sum", flops=SPLIT, *(piece(partial(split_kernel, step), (info, near(mine[p]), near(came[p])), [VMEM] * 3, (out, out)),))
        came[p] = swap(send, across(step))

    def whole(p):
        ((mine[p],),) = run("last_sum", piece(add_kernel, (near(mine[p]), near(came[p])), [VMEM] * 2, (held(mine[p].shape, BF16),)), flops=WHOLE)
        came[p] = swap(mine[p], across(bits - 2))

    COST = {("attention", 1): J_A1, ("down", 0): J_D0, ("in", 0): J_I0, ("attention", 0): J_A0, ("down", 1): J_D1, ("in", 1): J_I1}

    def join(p, step, beside=()):
        out = held((2 * mine[p].shape[0], width), BF16)
        joined = piece(partial(join_kernel, step), (info, near(mine[p]), near(came[p])), [VMEM] * 3, (out,))
        *others, (mine[p],) = run("join", *beside, joined, flops=COST.get((p, step), HEAVY), limit=8)
        came[p] = swap(mine[p], across(step - 1) if step else flip(0))
        return others

    dims = {"down": ((1, hidden_width, width),), "in": ((1, width, hidden_width),), "attention": ((1, width, 3 * width), (1, width, width))}
    out_grads = {}

    def stored(p, sides):
        known = out_grads.get(p, ())
        parts = tuple(near(came[p] if theirs else mine[p]) for theirs in sides)
        args = (info,) + parts + tuple(far(g) for g in known)
        size = len(sides) * (2 * width if p == "attention" else rows[p])
        return piece(
            partial(store_kernel, p, sides, len(known)),
            args,
            [VMEM] * (1 + len(sides)) + [ANY] * len(known),
            tuple(pltpu.HBM(d, F32) for d in dims[p]) + (token,),
            (ANY,) * len(dims[p]) + (VMEM,),
            {1 + len(sides) + i: i for i in range(len(known))},
            [pltpu.VMEM((size, width), F32), pltpu.SemaphoreType.DMA((4 * len(sides),))],
        )

    ((theirs,),) = run("down_gradients", products("down", True), flops=LIGHT)
    came["down"] = swap(theirs, flip(0))
    (mine["down"],), (theirs,) = run("ffn_gradients", products("down", False), products("in", True), flops=LIGHT)
    came["in"] = swap(theirs, flip(0))
    split("down", 0)
    ((mine["in"],),) = run("in_gradients", products("in", False), flops=LIGHT)
    split("in", 0)
    args = [info, near(d_resid), qkv_w, out_w] + [near(a) for a in (probs, scales, qkv, proj[0][0], sums)]
    ((last, d_mixed, d_proj, sums),) = run(
        "last_attention_backward",
        piece(
            partial(last_attention_kernel, 0, stages),
            args,
            [VMEM] * len(args),
            (held(block, BF16), held((seq_len, 3 * width), BF16), held((seq_len, width), BF16), held((SMALL, width), F32)),
            aliases={6: 1, 7: 2, 8: 3},
            scratch=[pltpu.VMEM((seq_len, width), BF16)],
        ),
        flops=LIGHT,
    )
    results[0] = last
    results[1] = second_last
    slots[0] = (x, d_mixed) + slots[0][2:]
    proj[0] = (d_proj, d_down)
    (theirs,), (mine["attention"],) = run("attention_gradients", products("attention", True), products("attention", False), flops=LIGHT)
    came["attention"] = swap(theirs, flip(0))
    split("down", 1)
    split("attention", 0)
    ((results[1],),) = run("relay", piece(relay_kernel, (near(results[1]),), [VMEM], (held(block, BF16),)))
    results[1] = move(results[1], [(0, 1)])
    pick = piece(
        pick_kernel, [info] + [near(results[s]) for s in range(stages)], [VMEM] * (1 + stages), (shape((seq_len, width), BF16), token)
    )
    moves = [partial(split, step=step) for step in range(1, bits - 1)] + [whole] + [partial(join, step=step) for step in reversed(range(bits - 1))]
    todo = {"in": moves[:-1], "down": moves[1:], "attention": moves[:-1]}
    while any(todo.values()):
        for p, steps in todo.items():
            if steps:
                steps.pop(0)(p)
                if p == "in" and len(steps) == PICK:
                    ((hidden_grad, _),) = run("pick_gradient", pick)
    (((*out_grads["down"], _)),) = join("in", 0, [stored("down", (False, True))])
    (((*out_grads["in"], _)),) = run("store", stored("in", (False,)), flops=STORE)
    join("attention", 0)
    (*out_grads["in"], _), (*out_grads["attention"], _) = run(
        "store", stored("in", (True,)), stored("attention", (False,)), limit=8, flops=HEAVY
    )
    vectors = tuple(shape((1, n), F32) for n in (2 * width, width, width, width, hidden_width, width, width, width))
    small = piece(
        partial(small_store_kernel, small_start),
        [info, near(mine["attention"]), near(came["attention"])],
        [VMEM] * 3,
        vectors + (shape((class_count, task_count, width), F32), shape((task_count, class_count), F32), token),
    )
    (*out_grads["attention"], _), (*vectors, head_w_grad, head_b_grad, _) = run("store", stored("attention", (True,)), small)
    qv_grad, out_b_grad, gain_one_grad, shift_one_grad, in_b_grad, down_b_grad, gain_two_grad, shift_two_grad = vectors
    return (
        hidden_out[None],
        losses,
        hidden_grad[None],
        out_grads["attention"][0],
        qv_grad,
        out_grads["attention"][1],
        out_b_grad,
        gain_one_grad,
        shift_one_grad,
        out_grads["in"][0],
        in_b_grad,
        out_grads["down"][0],
        down_b_grad,
        gain_two_grad,
        shift_two_grad,
        head_w_grad.transpose(1, 2, 0),
        head_b_grad,
    )


def solution(mesh):
    rows = P(("dp", "pipe"), None, None)
    ids = P(("dp", "pipe"), None)
    big = P("pipe", None, None)
    vec = P("pipe", None)
    return jax.shard_map(
        local,
        mesh=mesh,
        in_specs=(rows, ids, ids, ids, rows, big, vec, big, vec, vec, vec, big, vec, big, vec, vec, vec, P(), P()),
        out_specs=(rows, ids, rows, big, vec, big, vec, vec, vec, big, vec, big, vec, vec, vec, P(), P()),
        check_vma=False,
    )
```

```python
from functools import partial

import jax
import jax.numpy as jnp
from jax import lax
from jax.experimental import pallas as pl
from jax.experimental.pallas import tpu as pltpu
from jax.sharding import PartitionSpec as P

HEADS = 8
EPS = 1e-12
NEG = -1000000000.0
SEGS = 4
EXTRA = 16
SMALL = 32
BLOCK = 512
F32 = jnp.float32
BF16 = jnp.bfloat16
VMEM = pl.BlockSpec(memory_space=pltpu.VMEM)
ANY = pl.BlockSpec(memory_space=pl.ANY)
MIB = 1024 * 1024
HEADF = 100_000_000
PASSED = {
    0: {2: "home"}, 1: {1: "cot", 3: "home"}, 2: {2: "cot"}, 3: {2: "came"}, 4: {0: "cot"}, 6: {1: "came"}, 8: {2: "came"},
}
ADDED = {1: [(1, 2)], 2: [(2, 3)], 3: [(2, 3)], 4: [(0, 1)], 6: [(1, 2)], 8: [(2, 3)]}
PICK = 2
SPLIT = 20_000_000_000
WHOLE = 10_000_000_000
HEAVY = 10_000_000_000
J_A1 = 10_000_000_000
J_D0 = 100_000_000
J_I0 = 10_000_000_000
J_A0 = 10_000_000_000
J_D1 = 10_000_000_000
J_I1 = 10_000_000_000
STORE = 100_000_000
LIMIT = 6
QV_B, OUT_B, GAIN_ONE, SHIFT_ONE, IN_B, DOWN_B, GAIN_TWO, SHIFT_TWO = 0, 2, 3, 4, 5, 9, 10, 11


def mm(a, b):
    return lax.dot_general(a, b, (((1,), (0,)), ((), ())), preferred_element_type=F32)


def mm_nt(a, b):
    return lax.dot_general(a, b, (((1,), (1,)), ((), ())), preferred_element_type=F32)


def mm_tn(a, b):
    return lax.dot_general(a, b, (((0,), (0,)), ((), ())), preferred_element_type=F32)


def lane_masks(width):
    lanes = lax.broadcasted_iota(jnp.int32, (1, 2 * width), 1)
    return (lanes < width).astype(BF16), (lanes >= width).astype(BF16)


def segment_onehot(meta, count, seq_len):
    numbers = lax.broadcasted_iota(jnp.int32, (count, seq_len), 0).astype(F32)
    return (meta[0:1, :seq_len].astype(F32) == numbers).astype(F32)


def norm_stats(values):
    centre = values - jnp.mean(values, axis=-1, keepdims=True)
    spread = jnp.mean(centre * centre, axis=-1, keepdims=True)
    scale = lax.rsqrt(spread + EPS)
    return centre * scale, scale


def norm_back(grad, unit, scale, gain):
    scaled = grad * gain
    mean_one = jnp.mean(scaled, axis=-1, keepdims=True)
    mean_two = jnp.mean(scaled * unit, axis=-1, keepdims=True)
    return scale * (scaled - mean_one - unit * mean_two)


def column_sum(values):
    return jnp.sum(values.astype(F32), axis=0, keepdims=True)


def prepare_kernel(
    x_ref, cot_ref, seg_ref, task_ref, label_ref, qv_b, out_b, gain_one, shift_one, in_b, down_b, gain_two, shift_two, head_ref,
    block_ref, cot_block_ref, vec_ref, head_w_ref,
):
    _, seq_len, width = x_ref.shape
    block_ref[:seq_len, :] = x_ref[0]
    segs = task_ref.shape[1]
    lanes = lax.broadcasted_iota(jnp.int32, (1, width), 1)
    tags = jnp.zeros((1, width), jnp.int32)
    for s in range(segs):
        tags = jnp.where(lanes == seq_len + s, task_ref[0, s], tags)
        tags = jnp.where(lanes == seq_len + segs + s, label_ref[0, s], tags)
    block_ref[seq_len:, :] = jnp.broadcast_to(tags.astype(F32).astype(BF16), (EXTRA, width))
    block_ref[seq_len:, :seq_len] = jnp.broadcast_to(seg_ref[...].astype(F32).astype(BF16), (EXTRA, seq_len))
    cot_block_ref[:seq_len, :] = cot_ref[0]
    cot_block_ref[seq_len:, :] = jnp.zeros((EXTRA, width), BF16)

    row = 0
    for vector in (qv_b, out_b, gain_one, shift_one, in_b, down_b, gain_two, shift_two):
        for part in range(vector.shape[1] // width):
            vec_ref[row : row + 1, :] = vector[:, part * width : (part + 1) * width]
            row += 1
    classes, tasks, _ = head_ref.shape
    head_w_ref[...] = jnp.zeros_like(head_w_ref)
    for c in range(classes):
        head_w_ref[c * tasks : (c + 1) * tasks, :] = head_ref[c]


def forward_kernel(tick, stages, carry, fresh, info, x_ref, *refs):
    refs = list(refs)
    home_ref, cot_ref = (refs.pop(0), refs.pop(0)) if carry else (None, None)
    if tick == 0:
        vec, refs, sems = refs[4], refs[:4] + refs[5:-1], refs[-1]
        qkv_w, out_w, in_w, down_w = weights = refs[-4:]
        copies = [pltpu.make_async_copy(refs[i].at[0], weights[i], sems.at[i]) for i in range(4)]
        for copy in copies:
            copy.start()
        refs = refs[4:-4]
    else:
        copies = []
        qkv_w, out_w, in_w, down_w, vec = refs[:5]
        refs = refs[5:]

    def ready(*which):
        for i in which:
            if copies:
                copies[i].wait()

    if not fresh:
        refs = refs[10:]
    y_ref, keep_ref, qkv_ref, probs_ref, context_ref, unit_one_ref, normed_ref, hidden_ref, slope_ref, unit_two_ref, scales_ref = refs
    seq_len = x_ref.shape[0] - EXTRA
    width = x_ref.shape[1]
    head_dim = width // HEADS
    place = tick - 2 * info[0, 0]
    active = (place >= 0) & (place < stages)

    for stage, what in PASSED.get(tick, {}).items():

        @pl.when(info[0, 0] == stage)
        def _(what=what):
            y_ref[...] = {"home": home_ref, "cot": cot_ref, "came": x_ref}[what][...]

    if tick == 0:

        @pl.when(jnp.logical_not(active))
        def _():
            ready(0, 1, 2, 3)

    @pl.when(active)
    def _():
        meta = x_ref[seq_len:, :]
        y_ref[seq_len:, :] = meta
        x = x_ref[:seq_len, :]
        keep_ref[...] = x
        onehot = segment_onehot(meta, EXTRA, seq_len).astype(BF16)
        barred = jnp.where(mm_tn(onehot, onehot) > 0.5, 0.0, NEG)
        ready(0)
        q = (mm(x, qkv_w[:, :width]) + vec[QV_B : QV_B + 1]).astype(BF16)
        k = mm(x, qkv_w[:, width : 2 * width]).astype(BF16)
        v = (mm(x, qkv_w[:, 2 * width :]) + vec[QV_B + 1 : QV_B + 2]).astype(BF16)
        qkv_ref[:, :width] = q
        qkv_ref[:, width : 2 * width] = k
        qkv_ref[:, 2 * width :] = v
        v_t = v.T
        mask_a, mask_b = lane_masks(head_dim)
        factor = head_dim**-0.5

        def raw_scores(pair):
            cols = slice(pair * 2 * head_dim, (pair + 1) * 2 * head_dim)
            k_two = jnp.concatenate([k[:, cols] * (mask * factor).astype(BF16) for mask in (mask_a, mask_b)], axis=0)
            return mm_nt(k_two, q[:, cols])

        context_parts = []
        shares = []
        ahead = raw_scores(0)
        for pair in range(HEADS // 2):
            both = ahead
            if pair + 1 < HEADS // 2:
                ahead = raw_scores(pair + 1)
            for side in range(2):
                head = 2 * pair + side
                scores = both[side * seq_len : (side + 1) * seq_len] + barred
                expo = jnp.exp(scores - jnp.max(scores, axis=0, keepdims=True))
                share = 1.0 / jnp.sum(expo, axis=0, keepdims=True)
                expo_low = expo.astype(BF16)
                probs_ref[head * seq_len : (head + 1) * seq_len, :] = expo_low
                shares.append(share)
                context_parts.append(mm(v_t[head * head_dim : (head + 1) * head_dim, :], expo_low) * share)
        context = jnp.concatenate(context_parts, axis=0).T.astype(BF16)
        scales_ref[:, 256 : 256 + HEADS] = jnp.concatenate(shares, axis=0).T
        context_ref[...] = context
        ready(1)
        resid = x.astype(F32) + mm(context, out_w[...]) + vec[OUT_B : OUT_B + 1]
        unit_one, scale_one = norm_stats(resid)
        unit_one_ref[...] = unit_one
        normed = unit_one * vec[GAIN_ONE : GAIN_ONE + 1] + vec[SHIFT_ONE : SHIFT_ONE + 1]
        normed_low = normed.astype(BF16)
        normed_ref[...] = normed_low
        summed = normed + vec[DOWN_B : DOWN_B + 1]
        ready(2, 3)
        parts = in_w.shape[1] // BLOCK
        ahead = mm(normed_low, in_w[:, :BLOCK])
        for part in range(parts):
            cols = slice(part * BLOCK, (part + 1) * BLOCK)
            pre = ahead + vec[IN_B + part : IN_B + part + 1]
            if part + 1 < parts:
                ahead = mm(normed_low, in_w[:, (part + 1) * BLOCK : (part + 2) * BLOCK])
            gate = 0.5 + 0.5 * lax.erf(pre * (0.5**0.5))
            slope_ref[:, cols] = (gate + pre * (jnp.exp(-0.5 * pre * pre) * 0.3989422804014327)).astype(BF16)
            hidden = (pre * gate).astype(BF16)
            hidden_ref[:, cols] = hidden
            summed = summed + mm(hidden, down_w[cols, :])
        unit_two, scale_two = norm_stats(summed)
        unit_two_ref[...] = unit_two
        y_ref[:seq_len, :] = (unit_two * vec[GAIN_TWO : GAIN_TWO + 1] + vec[SHIFT_TWO : SHIFT_TWO + 1]).astype(BF16)
        scales_ref[:, 0:128] = jnp.broadcast_to(scale_one, (seq_len, 128))
        scales_ref[:, 128:256] = jnp.broadcast_to(scale_two, (seq_len, 128))


def head_parts(y, meta, cot, head_w, head_b_ref):
    seq_len, width = y.shape
    task_count, class_count = head_b_ref.shape
    high = lax.Precision.HIGHEST
    segs = 8
    onehot = segment_onehot(meta, segs, seq_len)
    row = meta[0:1, :seq_len].astype(F32)
    lanes = lax.broadcasted_iota(jnp.int32, (1, seq_len), 1)
    previous = jnp.where(lanes == 0, -1.0, pltpu.roll(row, 1, 1))
    pick = onehot * (row != previous).astype(F32)
    live = jnp.max(pick, axis=1, keepdims=True)
    cls = mm(pick.astype(BF16), y)
    logits = lax.dot_general(cls, head_w[...], (((1,), (1,)), ((), ())), precision=high, preferred_element_type=F32)
    slots = lax.broadcasted_iota(jnp.int32, (1, logits.shape[1]), 1)
    bias = jnp.zeros((1, logits.shape[1]), F32)
    for t in range(task_count):
        for c in range(class_count):
            bias = jnp.where(slots == c * task_count + t, head_b_ref[t, c], bias)
    logits = logits + bias
    tags = meta[0:1, :].astype(F32)
    spots = lax.broadcasted_iota(jnp.int32, (segs, width), 1) - lax.broadcasted_iota(jnp.int32, (segs, width), 0)
    task = jnp.sum(jnp.where(spots == seq_len, tags, 0.0), axis=1, keepdims=True).astype(jnp.int32)
    label = jnp.sum(jnp.where(spots == seq_len + SEGS, tags, 0.0), axis=1, keepdims=True).astype(jnp.int32)
    mine = jnp.zeros(logits.shape, jnp.bool_)
    for c in range(class_count):
        mine = mine | (slots == task + c * task_count)
    label_hot = slots == task + label * task_count
    masked = jnp.where(mine, logits, -jnp.inf)
    top = jnp.max(masked, axis=1, keepdims=True)
    expo = jnp.exp(masked - top)
    total = jnp.sum(expo, axis=1, keepdims=True)
    right = jnp.sum(jnp.where(label_hot, logits, 0.0), axis=1, keepdims=True)
    loss = live * (top + jnp.log(total) - right)
    d_logits = live * (expo / total - label_hot.astype(F32))
    d_cls = lax.dot_general(d_logits, head_w[...], (((1,), (0,)), ((), ())), precision=high, preferred_element_type=F32)
    upper = d_cls.astype(BF16)
    lower = (d_cls - upper.astype(F32)).astype(BF16)
    ones = pick.astype(BF16)
    d_final = mm_tn(jnp.concatenate([ones, ones], axis=0), jnp.concatenate([upper, lower], axis=0))
    grad = (cot.astype(F32) + d_final).astype(BF16)
    g_w = lax.dot_general(d_logits, cls, (((0,), (0,)), ((), ())), precision=high, preferred_element_type=F32)
    g_b = jnp.concatenate([column_sum(d_logits)] * (width // logits.shape[1]), axis=1)
    rows = lax.broadcasted_iota(jnp.int32, (EXTRA, 1), 0)
    count = task_count * class_count
    heads = jnp.where(rows < count, g_w[:EXTRA], jnp.where(rows == count, g_b, 0.0)).astype(BF16)
    return loss, grad, heads


def row_head_kernel(stages, info, y_ref, cot_ref, head_b_ref, head_w, g_ref):
    seq_len = y_ref.shape[0] - EXTRA

    @pl.when(info[0, 0] == stages - 1)
    def _():
        _, grad, heads = head_parts(y_ref[:seq_len, :], y_ref[seq_len:, :], cot_ref[:seq_len, :], head_w, head_b_ref)
        g_ref[:seq_len, :] = grad
        g_ref[seq_len:, :] = heads


def loss_kernel(stages, info, head_b_ref, *refs):
    y_refs = refs[:stages]
    cot_ref, head_w, final_ref, loss_ref, picked = refs[stages:]
    for s in range(stages):

        @pl.when(info[0, 0] == s)
        def _(s=s):
            picked[...] = y_refs[s][...]

    seq_len, _ = final_ref.shape
    y = picked[:seq_len, :]
    final_ref[...] = y
    loss, _, _ = head_parts(y, picked[seq_len:, :], cot_ref[:seq_len, :], head_w, head_b_ref)
    segs = loss.shape[0]
    wide = lax.broadcasted_iota(jnp.int32, (segs, 128), 1)
    numbers = lax.broadcasted_iota(jnp.int32, (segs, 1), 0)
    loss_ref[...] = jnp.sum(jnp.where(wide == numbers, loss, 0.0), axis=0, keepdims=True)[:, : loss_ref.shape[1]]


def adder(sums_ref):
    def add(row, value):
        sums_ref[row : row + 1, :] += value

    return add


def ffn_back(g_ref, slope_ref, unit_one_ref, unit_two_ref, scales_ref, in_w, down_w, vec, d_pre_ref, d_down_ref, sums_ref):
    seq_len = g_ref.shape[0] - EXTRA
    add = adder(sums_ref)
    sums_ref[SMALL - EXTRA :, :] += g_ref[seq_len:, :].astype(F32)
    grad = g_ref[:seq_len, :].astype(F32)
    scale_one = scales_ref[:, 0:1]
    scale_two = scales_ref[:, 128:129]
    unit_two = unit_two_ref[...]
    add(GAIN_TWO, column_sum(grad * unit_two))
    add(SHIFT_TWO, column_sum(grad))
    d_summed = norm_back(grad, unit_two, scale_two, vec[GAIN_TWO : GAIN_TWO + 1])
    d_down = d_summed.astype(BF16)
    d_down_ref[...] = d_down
    add(DOWN_B, column_sum(d_down))
    d_normed = d_summed
    for part in range(in_w.shape[1] // BLOCK):
        cols = slice(part * BLOCK, (part + 1) * BLOCK)
        d_pre = (mm_nt(d_down, down_w[cols, :]) * slope_ref[:, cols].astype(F32)).astype(BF16)
        d_pre_ref[:, cols] = d_pre
        add(IN_B + part, column_sum(d_pre))
        d_normed = d_normed + mm_nt(d_pre, in_w[:, cols])
    unit_one = unit_one_ref[...]
    add(GAIN_ONE, column_sum(d_normed * unit_one))
    add(SHIFT_ONE, column_sum(d_normed))
    return norm_back(d_normed, unit_one, scale_one, vec[GAIN_ONE : GAIN_ONE + 1])


def attention_back(d_resid, qkv_ref, probs_ref, scales_ref, qkv_w, out_w, next_ref, d_mixed_ref, d_proj_ref, sums_ref, queries):
    seq_len, width = d_resid.shape
    head_dim = width // HEADS
    add = adder(sums_ref)
    d_proj = d_resid.astype(BF16)
    d_proj_ref[...] = d_proj
    add(OUT_B, column_sum(d_proj))
    d_context = mm_nt(d_proj, out_w[...])
    factor = head_dim**-0.5
    mask_a, mask_b = lane_masks(head_dim)
    queries[...] = qkv_ref[:, :width]
    keys = qkv_ref[:, width : 2 * width]
    k_t = (keys * jnp.asarray(factor, BF16)).T
    shares = scales_ref[:, 256 : 256 + HEADS]
    share_rows = shares.T
    d_query_parts = []
    first = lax.broadcasted_iota(jnp.int32, (seq_len, 2 * head_dim), 1) < head_dim

    def weight_gradients_of(pair):
        cols = slice(pair * 2 * head_dim, (pair + 1) * 2 * head_dim)
        v_cols = qkv_ref[:, slice(cols.start + 2 * width, cols.stop + 2 * width)]
        scale = jnp.where(first, shares[:, 2 * pair : 2 * pair + 1], shares[:, 2 * pair + 1 : 2 * pair + 2])
        scaled = (d_context[:, cols] * scale).astype(BF16)
        v_two = jnp.concatenate([v_cols * mask for mask in (mask_a, mask_b)], axis=0)
        return scaled, mm_nt(v_two, scaled)

    ahead = weight_gradients_of(0)
    for pair in range(HEADS // 2):
        scaled, d_probs = ahead
        if pair + 1 < HEADS // 2:
            ahead = weight_gradients_of(pair + 1)
        cols = slice(pair * 2 * head_dim, (pair + 1) * 2 * head_dim)
        rows = slice(pair * 2 * seq_len, (pair + 1) * 2 * seq_len)
        probs = probs_ref[rows, :]
        d_values = mm(probs, scaled)
        parts = []
        for side in range(2):
            half = slice(side * seq_len, (side + 1) * seq_len)
            head = 2 * pair + side
            probs_wide = probs[half].astype(F32)
            total = jnp.sum(probs_wide * d_probs[half], axis=0, keepdims=True) * share_rows[head : head + 1, :]
            d_scores = (probs_wide * (d_probs[half] - total)).astype(BF16)
            parts.append(d_scores)
            d_query_parts.append(mm(k_t[head * head_dim : (head + 1) * head_dim, :], d_scores))
        d_keys = mm(jnp.concatenate(parts, axis=0), queries[:, cols] * jnp.asarray(factor, BF16))
        d_mixed_ref[:, slice(cols.start + width, cols.stop + width)] = jnp.where(first, d_keys[:seq_len], d_keys[seq_len:]).astype(BF16)
        d_mixed_ref[:, slice(cols.start + 2 * width, cols.stop + 2 * width)] = jnp.where(
            first, d_values[:seq_len], d_values[seq_len:]
        ).astype(BF16)
    d_queries = jnp.concatenate(d_query_parts, axis=0).T.astype(BF16)
    d_mixed_ref[:, :width] = d_queries
    add(QV_B, column_sum(d_queries))
    add(QV_B + 1, column_sum(d_mixed_ref[:, 2 * width :]))
    d_input = d_resid + mm_nt(d_mixed_ref[...], qkv_w[...])
    next_ref[:seq_len, :] = d_input.astype(BF16)


def is_active(info, tick, stages):
    place = tick - 2 * info[0, 0]
    return (place >= 0) & (place < stages)


def backward_kernel(tick, stages, own, fresh_proj, fresh_sums, info, g_ref, *refs):
    refs = list(refs)
    own_ref = refs.pop(0) if own else None
    qkv_w, out_w, in_w, down_w, vec = refs[:5]
    qkv_ref, slope_ref, probs_ref, unit_one_ref, unit_two_ref, scales_ref = refs[5:11]
    refs = refs[11:]
    if not fresh_proj:
        refs = refs[2:]
    if not fresh_sums:
        refs = refs[1:]
    next_ref, d_mixed_ref, d_pre_ref, d_proj_ref, d_down_ref, sums_ref, queries, picked = refs
    seq_len = g_ref.shape[0] - EXTRA
    active = is_active(info, tick, stages)

    if own:

        @pl.when(info[0, 0] == stages - 1)
        def _():
            picked[...] = own_ref[...]

        @pl.when(info[0, 0] != stages - 1)
        def _():
            picked[...] = g_ref[...]

        g_ref = picked
    if fresh_sums:
        sums_ref[...] = jnp.zeros_like(sums_ref)

    @pl.when(active)
    def _():
        next_ref[seq_len:, :] = g_ref[seq_len:, :]
        d_resid = ffn_back(
            g_ref, slope_ref, unit_one_ref, unit_two_ref, scales_ref, in_w, down_w, vec, d_pre_ref, d_down_ref, sums_ref
        )
        attention_back(d_resid, qkv_ref, probs_ref, scales_ref, qkv_w, out_w, next_ref, d_mixed_ref, d_proj_ref, sums_ref, queries)


def last_ffn_kernel(
    tick, stages, info, g_ref, in_w, down_w, vec, slope_ref, unit_one_ref, unit_two_ref, scales_ref, d_down_in, sums_in,
    d_pre_ref, d_down_ref, sums_ref, d_resid_ref,
):
    @pl.when(is_active(info, tick, stages))
    def _():
        d_resid_ref[...] = ffn_back(
            g_ref, slope_ref, unit_one_ref, unit_two_ref, scales_ref, in_w, down_w, vec, d_pre_ref, d_down_ref, sums_ref
        )


def last_attention_kernel(
    tick, stages, info, d_resid_ref, qkv_w, out_w, probs_ref, scales_ref, qkv_ref, d_proj_in, sums_in,
    next_ref, d_mixed_ref, d_proj_ref, sums_ref, queries,
):
    @pl.when(is_active(info, tick, stages))
    def _():
        attention_back(d_resid_ref[...], qkv_ref, probs_ref, scales_ref, qkv_w, out_w, next_ref, d_mixed_ref, d_proj_ref, sums_ref, queries)


def half_of(info, theirs):
    return 1 - info[1, 0] if theirs else info[1, 0]


def outer(left, right, rows=None, cols=None):
    rows = slice(None) if rows is None else rows
    cols = slice(None) if cols is None else cols
    return sum(mm_tn(a[:, rows], b[:, cols]) for a, b in zip(left, right))


def down_weights(theirs, info, *refs):
    *refs, out_ref = refs
    hidden, d_down = refs[: len(refs) // 2], refs[len(refs) // 2 :]
    span = hidden[0].shape[1] // 2
    for start in range(0, span, BLOCK):
        at = pl.ds(pl.multiple_of(half_of(info, theirs) * span + start, BLOCK), BLOCK)
        out_ref[start : start + BLOCK, :] = outer(hidden, d_down, rows=at).astype(BF16)


def in_weights(theirs, info, *refs):
    *refs, out_ref = refs
    normed, d_pre = refs[: len(refs) // 2], refs[len(refs) // 2 :]
    width = normed[0].shape[1]
    span = d_pre[0].shape[1] // 2
    for part in range(span // BLOCK):
        at = pl.ds(pl.multiple_of(half_of(info, theirs) * span + part * BLOCK, BLOCK), BLOCK)
        out_ref[part * width : (part + 1) * width, :] = outer(normed, d_pre, cols=at).astype(BF16)


def attention_weights(theirs, info, *refs):
    *refs, sums_ref, out_ref = refs
    slots = len(refs) // 4
    x, context, d_mixed, d_proj = (refs[i * slots : (i + 1) * slots] for i in range(4))
    half = half_of(info, theirs)
    width = x[0].shape[1]
    span = width // 2
    at = pl.ds(pl.multiple_of(half * span, span), span)
    for part in range(3):
        cols = slice(part * width, (part + 1) * width)
        out_ref[part * span : (part + 1) * span, :] = outer(x, d_mixed, rows=at, cols=cols).astype(BF16)
    out_ref[3 * span : 4 * span, :] = outer(context, d_proj, rows=at).astype(BF16)
    out_ref[4 * span :, :] = jnp.zeros((out_ref.shape[0] - 4 * span, width), BF16)
    share = SMALL // 2
    out_ref[4 * span : 4 * span + share, :] = sums_ref[pl.ds(pl.multiple_of(half * share, share), share), :].astype(BF16)


def split_kernel(step, info, mine_ref, came_ref, keep_ref, send_ref):
    rows = keep_ref.shape[0]
    bit = info[2 + step, 0]
    for ref, side in ((send_ref, 1 - bit), (keep_ref, bit)):
        at = pl.ds(pl.multiple_of(side * rows, 16), rows)
        ref[...] = (mine_ref[at, :].astype(F32) + came_ref[at, :].astype(F32)).astype(BF16)


def add_kernel(mine_ref, came_ref, out_ref):
    out_ref[...] = (mine_ref[...].astype(F32) + came_ref[...].astype(F32)).astype(BF16)


def join_kernel(step, info, mine_ref, came_ref, out_ref):
    rows = mine_ref.shape[0]
    bit = info[2 + step, 0]
    out_ref[pl.ds(pl.multiple_of(bit * rows, 16), rows), :] = mine_ref[...]
    out_ref[pl.ds(pl.multiple_of((1 - bit) * rows, 16), rows), :] = came_ref[...]


def store_kernel(name, sides, known, info, *refs):
    parts = refs[: len(sides)]
    token, stage_ref, sems = refs[-3:]
    outs = refs[len(sides) + known : -3]
    token[...] = jnp.zeros_like(token)
    copies = []
    row = 0
    for theirs, part_ref in zip(sides, parts):
        half = half_of(info, theirs)
        width = part_ref.shape[1]
        targets = []
        if name == "down":
            span = outs[0].shape[1] // 2
            for start in range(0, span, BLOCK):
                targets.append((BLOCK, outs[0].at[0, pl.ds(pl.multiple_of(half * span + start, BLOCK), BLOCK), :]))
        elif name == "in":
            span = outs[0].shape[2] // 2
            for start in range(0, span, BLOCK):
                targets.append((width, outs[0].at[0, :, pl.ds(pl.multiple_of(half * span + start, BLOCK), BLOCK)]))
        else:
            span = width // 2
            at = pl.ds(pl.multiple_of(half * span, span), span)
            targets = [(span, outs[0].at[0, at, i * width : (i + 1) * width]) for i in range(3)] + [(span, outs[1].at[0, at, :])]
        start = 0
        for size, dst in targets:
            stage_ref[row : row + size, :] = part_ref[start : start + size, :].astype(F32)
            copies.append(pltpu.make_async_copy(stage_ref.at[row : row + size], dst, sems.at[len(copies)]))
            copies[-1].start()
            start += size
            row += size
    for copy in copies:
        copy.wait()


def small_store_kernel(
    start, info, mine_ref, came_ref, qv_b, out_b, gain_one, shift_one, in_b, down_b, gain_two, shift_two, head_w, head_b, token
):
    token[...] = jnp.zeros_like(token)
    share = SMALL // 2
    mine = mine_ref[start : start + share, :].astype(F32)
    came = came_ref[start : start + share, :].astype(F32)
    first = info[1, 0] == 0
    low = jnp.where(first, mine, came)
    high = jnp.where(first, came, mine)
    width = low.shape[1]
    row = 0
    for vector in (qv_b, out_b, gain_one, shift_one, in_b, down_b, gain_two, shift_two):
        for part in range(vector.shape[1] // width):
            vector[:, part * width : (part + 1) * width] = low[row : row + 1, :]
            row += 1
    classes, tasks, _ = head_w.shape
    for c in range(classes):
        head_w[c] = high[c * tasks : (c + 1) * tasks, :]
    line = high[classes * tasks : classes * tasks + 1, :128]
    lanes = lax.broadcasted_iota(jnp.int32, (16, 128), 1)
    spread = jnp.where(lanes % tasks == lax.broadcasted_iota(jnp.int32, (16, 128), 0), line, 0.0).astype(BF16)
    gather = (lax.broadcasted_iota(jnp.int32, (128, 128), 0) // tasks == lax.broadcasted_iota(jnp.int32, (128, 128), 1)).astype(BF16)
    head_b[...] = mm(spread, gather)[:tasks, :classes]


def relay_kernel(in_ref, out_ref):
    out_ref[...] = in_ref[...]


def pick_kernel(info, *refs):
    *grads, out_ref, token = refs
    token[...] = jnp.zeros_like(token)
    for s, grad in enumerate(grads):

        @pl.when(info[0, 0] == s)
        def _(grad=grad):
            out_ref[...] = grad[: out_ref.shape[0], :]


def shape(dims, dtype):
    return jax.ShapeDtypeStruct(dims, dtype)


def held(dims, dtype):
    return pltpu.VMEM(dims, dtype)


def near(array):
    return pltpu.with_memory_space_constraint(array, pltpu.VMEM)


def far(array):
    return pltpu.with_memory_space_constraint(array, pltpu.HBM)


def call(kernel, name, out_shape, args, in_specs, out_specs=None, aliases=None, scratch=(), flops=0, limit=LIMIT, after=()):
    single = not isinstance(out_shape, tuple)
    if out_specs is None:
        out_specs = VMEM if single else (VMEM,) * len(out_shape)
    count, extra = len(args), len(after)

    def body(*refs):
        kernel(*refs[:count], *refs[count + extra :])

    args = tuple(args) + tuple(near(a) for a in after)
    in_specs = list(in_specs) + [ANY] * extra
    return pl.pallas_call(
        body,
        out_shape=out_shape,
        in_specs=in_specs,
        out_specs=out_specs,
        scratch_shapes=scratch,
        input_output_aliases=aliases or {},
        compiler_params=pltpu.CompilerParams(vmem_limit_bytes=limit * MIB),
        cost_estimate=pl.CostEstimate(flops=flops, bytes_accessed=0, transcendentals=0),
        name=name,
    )(*args)


def piece(kernel, args, specs, out_shape, out_specs=None, aliases=None, scratch=()):
    return kernel, tuple(args), list(specs), tuple(out_shape), out_specs or (VMEM,) * len(out_shape), aliases or {}, list(scratch)


def fused(name, pieces, **rest):
    counts = [(len(args), len(outs), len(scratch)) for _, args, _, outs, _, _, scratch in pieces]
    sums = [sum(c[i] for c in counts) for i in range(3)]

    def kernel(*refs):
        ins, outs, scratch = refs[: sums[0]], refs[sums[0] : sums[0] + sums[1]], refs[sums[0] + sums[1] :]
        for (part, *_), (a, b, c) in zip(pieces, counts):
            part(*ins[:a], *outs[:b], *scratch[:c])
            ins, outs, scratch = ins[a:], outs[b:], scratch[c:]

    aliases = {}
    a = b = 0
    for (_, _, _, _, _, own, _), count in zip(pieces, counts):
        aliases |= {a + i: b + o for i, o in own.items()}
        a, b = a + count[0], b + count[1]
    results = call(
        kernel,
        name,
        sum((p[3] for p in pieces), ()),
        sum((p[1] for p in pieces), ()),
        sum((p[2] for p in pieces), []),
        sum((tuple(p[4]) for p in pieces), ()),
        aliases=aliases,
        scratch=sum((p[6] for p in pieces), []),
        **rest,
    )
    split = []
    for count in counts:
        split.append(results[: count[1]])
        results = results[count[1] :]
    return split


def local(
    hidden_in, segment_ids, task_ids, labels, cotangent, qkv_weight, qv_bias, out_weight, out_bias, norm1_gain, norm1_bias,
    ffn_in_weight, ffn_in_bias, ffn_out_weight, ffn_out_bias, norm2_gain, norm2_bias, head_weight, head_bias,
):
    stages = lax.axis_size("pipe")
    stage = lax.axis_index("pipe")
    shards = lax.axis_size("dp")
    shard = lax.axis_index("dp")
    _, seq_len, width = hidden_in.shape
    hidden_width = ffn_in_weight.shape[2]
    task_count, _, class_count = head_weight.shape
    block = (seq_len + EXTRA, width)

    bits = shards.bit_length() - 1
    upward = list(range(1, bits))
    orders = (upward, upward[::-1])
    core = shard & 1
    sides = [jnp.where(core == 0, (shard >> orders[0][j]) & 1, (shard >> orders[1][j]) & 1) for j in range(bits - 1)]
    info = jnp.stack([stage, core] + sides + [stage] * (6 - len(sides))).astype(jnp.int32)
    info = near(jnp.broadcast_to(info[:, None], (8, 128)))

    home, cot_block, vec, head_w = call(
        prepare_kernel,
        "prepare",
        (held(block, BF16), held(block, BF16), held((16, width), F32), held((16, width), F32)),
        tuple(
            far(a)
            for a in (
                hidden_in, cotangent, segment_ids, task_ids, labels, qv_bias, out_bias, norm1_gain, norm1_bias, ffn_in_bias, ffn_out_bias,
                norm2_gain, norm2_bias, head_weight.transpose(2, 0, 1),
            )
        ),
        [VMEM] * 14,
    )
    head_b = near(head_bias)
    weights = tuple(far(w) for w in (qkv_weight, out_weight, ffn_in_weight, ffn_out_weight)) + (near(vec),)
    weight_shapes = tuple(held(w.shape[1:], BF16) for w in weights[:4])

    def move(array, pairs):
        return lax.ppermute(array, "pipe", pairs)

    def route(tick):
        pairs = [(s, s + 1) for s in range(stages - 1) if 0 <= tick - 2 * s < stages]
        if tick + 2 < stages:
            pairs.append((tick + 2, 0))
        pairs += ADDED.get(tick, [])
        late = tick - 2 * (stages - 1)
        if 0 <= late < stages - 1:
            pairs.append((stages - 1, late))
        return pairs

    def back(tick):
        pairs = [(s + 1, s) for s in range(stages - 1) if 0 <= tick - 2 * s < stages]
        if tick + 2 < stages:
            pairs.append((0, tick + 2))
        return pairs

    ticks = 2 * (stages - 1) + stages
    saved_shapes = (
        held((seq_len, width), BF16),
        held((seq_len, 3 * width), BF16),
        held((HEADS * seq_len, seq_len), BF16),
        held((seq_len, width), BF16),
        held((seq_len, width), F32),
        held((seq_len, width), BF16),
        held((seq_len, hidden_width), BF16),
        held((seq_len, hidden_width), BF16),
        held((seq_len, width), F32),
        held((seq_len, 384), F32),
    )
    arrived = {0: home, 1: move(home, [(1, 0)])}
    slots = [None] * stages
    last = None
    own_heads, final_blocks = {}, {}

    def row_heads(final, cots, after=()):
        return call(
            partial(row_head_kernel, stages),
            "row_heads",
            held(block, BF16),
            [info, near(final), near(cots), head_b, near(head_w)],
            [VMEM] * 5,
            flops=HEADF,
            after=after,
        )

    for tick in range(ticks):
        carry = any(what != "came" for what in PASSED.get(tick, {}).values())
        fresh = slots[tick % stages] is None
        args = [info, near(arrived[tick])] + ([near(home), near(cot_block)] if carry else []) + list(weights)
        aliases = {}
        if not fresh:
            aliases = {len(args) + i: 1 + i for i in range(len(saved_shapes))}
            args += [near(a) for a in slots[tick % stages]]
        outs = call(
            partial(forward_kernel, tick, stages, carry, fresh),
            "layer_forward",
            (held(block, BF16),) + saved_shapes + (() if tick else weight_shapes),
            args,
            [ANY if a is w else VMEM for a in args for w in [next((w for w in weights[:4] if w is a and not tick), None)]],
            aliases=aliases,
            scratch=[] if tick else [pltpu.SemaphoreType.DMA((4,))],
            flops=4_000_000_000,
        )
        if tick == 0:
            weights = tuple(near(w) for w in outs[-4:]) + (near(vec),)
        slots[tick % stages] = tuple(outs[1:11])
        last = outs[0]
        if route(tick):
            arrived[tick + 2] = move(last, route(tick))
        if tick >= 2 * (stages - 1):
            final_blocks[tick] = last
    finals = [arrived[2 * (stages - 1) + 2 + s] for s in range(stages - 1)] + [last]
    own_heads[ticks - 1] = row_heads(last, cot_block)

    cots = {8: arrived[4], 7: arrived[5], 6: arrived[10]}
    arrived = {ticks - 1: own_heads[ticks - 1]}
    proj = [None] * stages
    sums = None
    results = {}
    for tick in reversed(range(1, ticks)):
        slot = tick % stages
        if tick in cots:
            own_heads[tick] = row_heads(final_blocks[tick], cots[tick], [last])
            arrived.setdefault(tick, own_heads[tick])
        own = tick in own_heads and tick < ticks - 2
        x, qkv, probs, context, unit_one, normed, hidden, slope, unit_two, scales = slots[slot]
        args = [info, near(arrived[tick])] + ([near(own_heads[tick])] if own else []) + list(weights)
        aliases = {len(args): 1, len(args) + 1: 2}
        args += [near(a) for a in (qkv, slope, probs, unit_one, unit_two, scales)]
        fresh_proj, fresh_sums = proj[slot] is None, sums is None
        if not fresh_proj:
            aliases |= {len(args): 3, len(args) + 1: 4}
            args += [near(a) for a in proj[slot]]
        if not fresh_sums:
            aliases |= {len(args): 5}
            args += [near(sums)]
        last, d_mixed, d_pre, d_proj, d_down, sums = call(
            partial(backward_kernel, tick, stages, own, fresh_proj, fresh_sums),
            "layer_backward",
            (
                held(block, BF16),
                held((seq_len, 3 * width), BF16),
                held((seq_len, hidden_width), BF16),
                held((seq_len, width), BF16),
                held((seq_len, width), BF16),
                held((SMALL, width), F32),
            ),
            args,
            [VMEM] + [VMEM] * (len(args) - 1),
            aliases=aliases,
            scratch=[pltpu.VMEM((seq_len, width), BF16), pltpu.VMEM(block, BF16)],
            flops=4_000_000_000,
        )
        proj[slot] = (d_proj, d_down)
        slots[slot] = (x, d_mixed, probs, context, unit_one, normed, hidden, d_pre, unit_two, scales)
        if tick >= 2:
            arrived[tick - 2] = move(last, back(tick - 2))
        if 2 <= tick < stages:
            results[tick] = arrived[tick - 2]

    def flip(bit):
        return [(i, i ^ (1 << bit)) for i in range(shards)]

    def across(step):
        return [(i, i ^ (1 << orders[i & 1][step])) for i in range(shards)]

    def swap(array, pairs):
        return lax.ppermute(array, "dp", pairs)

    second_last = last
    x, qkv, probs, context, unit_one, normed, hidden, slope, unit_two, scales = slots[0]
    qkv_w, out_w, in_w, down_w, vec = weights
    args = [info, near(arrived[0]), in_w, down_w, vec] + [near(a) for a in (slope, unit_one, unit_two, scales, proj[0][1], sums)]
    d_pre, d_down, sums, d_resid = call(
        partial(last_ffn_kernel, 0, stages),
        "last_ffn_backward",
        (held((seq_len, hidden_width), BF16), held((seq_len, width), BF16), held((SMALL, width), F32), held((seq_len, width), F32)),
        args,
        [VMEM] * len(args),
        aliases={5: 0, 9: 1, 10: 2},
    )
    LIGHT = 100_000_000
    tail = [d_resid]
    token = held((8, 128), F32)

    def run(name, *pieces, flops=10_000_000_000, **rest):
        split = fused(name, pieces, after=[tail[0]], flops=flops, **rest)
        tail[0] = split[-1][-1]
        return split

    unit = 16 * shards // 2
    half_hidden = hidden_width // 2
    small_start = 2 * width
    rows = {
        "down": half_hidden,
        "in": half_hidden * width // BLOCK,
        "attention": -(-(small_start + SMALL // 2) // unit) * unit,
    }
    mine, came = {}, {}

    def kept(index):
        return [near(slots[s][index]) for s in range(stages)]

    def products(p, theirs):
        if p == "down":
            kernel, arrays = down_weights, kept(6) + [near(d_down if s == 0 else proj[s][1]) for s in range(stages)]
        elif p == "in":
            kernel, arrays = in_weights, kept(5) + [near(d_pre if s == 0 else slots[s][7]) for s in range(stages)]
        else:
            kernel = attention_weights
            arrays = kept(0) + kept(3) + kept(1) + [near(proj[s][0]) for s in range(stages)] + [near(sums)]
        args = [info] + arrays
        return piece(partial(kernel, theirs), args, [VMEM] * len(args), (held((rows[p], width), BF16),))

    def split(p, step):
        out = held((mine[p].shape[0] // 2, width), BF16)
        ((mine[p], send),) = run("split_sum", flops=SPLIT, *(piece(partial(split_kernel, step), (info, near(mine[p]), near(came[p])), [VMEM] * 3, (out, out)),))
        came[p] = swap(send, across(step))

    def whole(p):
        ((mine[p],),) = run("last_sum", piece(add_kernel, (near(mine[p]), near(came[p])), [VMEM] * 2, (held(mine[p].shape, BF16),)), flops=WHOLE)
        came[p] = swap(mine[p], across(bits - 2))

    COST = {("attention", 1): J_A1, ("down", 0): J_D0, ("in", 0): J_I0, ("attention", 0): J_A0, ("down", 1): J_D1, ("in", 1): J_I1}

    def join(p, step, beside=()):
        out = held((2 * mine[p].shape[0], width), BF16)
        joined = piece(partial(join_kernel, step), (info, near(mine[p]), near(came[p])), [VMEM] * 3, (out,))
        *others, (mine[p],) = run("join", *beside, joined, flops=COST.get((p, step), HEAVY), limit=8)
        came[p] = swap(mine[p], across(step - 1) if step else flip(0))
        return others

    dims = {"down": ((1, hidden_width, width),), "in": ((1, width, hidden_width),), "attention": ((1, width, 3 * width), (1, width, width))}
    out_grads = {}

    def stored(p, sides):
        known = out_grads.get(p, ())
        parts = tuple(near(came[p] if theirs else mine[p]) for theirs in sides)
        args = (info,) + parts + tuple(far(g) for g in known)
        size = len(sides) * (2 * width if p == "attention" else rows[p])
        return piece(
            partial(store_kernel, p, sides, len(known)),
            args,
            [VMEM] * (1 + len(sides)) + [ANY] * len(known),
            tuple(pltpu.HBM(d, F32) for d in dims[p]) + (token,),
            (ANY,) * len(dims[p]) + (VMEM,),
            {1 + len(sides) + i: i for i in range(len(known))},
            [pltpu.VMEM((size, width), F32), pltpu.SemaphoreType.DMA((4 * len(sides),))],
        )

    ((theirs,),) = run("down_gradients", products("down", True), flops=LIGHT)
    came["down"] = swap(theirs, flip(0))
    (mine["down"],), (theirs,) = run("ffn_gradients", products("down", False), products("in", True), flops=LIGHT)
    came["in"] = swap(theirs, flip(0))
    split("down", 0)
    ((mine["in"],),) = run("in_gradients", products("in", False), flops=LIGHT)
    split("in", 0)
    args = [info, near(d_resid), qkv_w, out_w] + [near(a) for a in (probs, scales, qkv, proj[0][0], sums)]
    ((last, d_mixed, d_proj, sums),) = run(
        "last_attention_backward",
        piece(
            partial(last_attention_kernel, 0, stages),
            args,
            [VMEM] * len(args),
            (held(block, BF16), held((seq_len, 3 * width), BF16), held((seq_len, width), BF16), held((SMALL, width), F32)),
            aliases={6: 1, 7: 2, 8: 3},
            scratch=[pltpu.VMEM((seq_len, width), BF16)],
        ),
        flops=LIGHT,
    )
    results[0] = last
    results[1] = second_last
    slots[0] = (x, d_mixed) + slots[0][2:]
    proj[0] = (d_proj, d_down)
    (theirs,), (mine["attention"],) = run("attention_gradients", products("attention", True), products("attention", False), flops=LIGHT)
    came["attention"] = swap(theirs, flip(0))
    split("down", 1)
    split("attention", 0)
    ((results[1],),) = run("relay", piece(relay_kernel, (near(results[1]),), [VMEM], (held(block, BF16),)))
    results[1] = move(results[1], [(0, 1)])
    pick = piece(
        pick_kernel, [info] + [near(results[s]) for s in range(stages)], [VMEM] * (1 + stages), (shape((seq_len, width), BF16), token)
    )
    rows_out = piece(
        partial(loss_kernel, stages),
        [info, head_b] + [near(f) for f in finals] + [near(cot_block), near(head_w)],
        [VMEM] * (stages + 4),
        (shape((seq_len, width), BF16), shape(task_ids.shape, F32)),
        scratch=[pltpu.VMEM(block, BF16)],
    )
    moves = [partial(split, step=step) for step in range(1, bits - 1)] + [whole] + [partial(join, step=step) for step in reversed(range(bits - 1))]
    todo = {"in": moves[:-1], "down": moves[1:], "attention": moves[:-1]}
    while any(todo.values()):
        for p, steps in todo.items():
            if steps:
                steps.pop(0)(p)
                if p == "in" and len(steps) == PICK:
                    (hidden_out, losses), (hidden_grad, _) = run("pick_gradient", rows_out, pick)
    (((*out_grads["down"], _)),) = join("in", 0, [stored("down", (False, True))])
    (((*out_grads["in"], _)),) = run("store", stored("in", (False,)), flops=STORE)
    join("attention", 0)
    (*out_grads["in"], _), (*out_grads["attention"], _) = run(
        "store", stored("in", (True,)), stored("attention", (False,)), limit=8, flops=HEAVY
    )
    vectors = tuple(shape((1, n), F32) for n in (2 * width, width, width, width, hidden_width, width, width, width))
    small = piece(
        partial(small_store_kernel, small_start),
        [info, near(mine["attention"]), near(came["attention"])],
        [VMEM] * 3,
        vectors + (shape((class_count, task_count, width), F32), shape((task_count, class_count), F32), token),
    )
    (*out_grads["attention"], _), (*vectors, head_w_grad, head_b_grad, _) = run("store", stored("attention", (True,)), small)
    qv_grad, out_b_grad, gain_one_grad, shift_one_grad, in_b_grad, down_b_grad, gain_two_grad, shift_two_grad = vectors
    return (
        hidden_out[None],
        losses,
        hidden_grad[None],
        out_grads["attention"][0],
        qv_grad,
        out_grads["attention"][1],
        out_b_grad,
        gain_one_grad,
        shift_one_grad,
        out_grads["in"][0],
        in_b_grad,
        out_grads["down"][0],
        down_b_grad,
        gain_two_grad,
        shift_two_grad,
        head_w_grad.transpose(1, 2, 0),
        head_b_grad,
    )


def solution(mesh):
    rows = P(("dp", "pipe"), None, None)
    ids = P(("dp", "pipe"), None)
    big = P("pipe", None, None)
    vec = P("pipe", None)
    return jax.shard_map(
        local,
        mesh=mesh,
        in_specs=(rows, ids, ids, ids, rows, big, vec, big, vec, vec, vec, big, vec, big, vec, vec, vec, P(), P()),
        out_specs=(rows, ids, rows, big, vec, big, vec, vec, vec, big, vec, big, vec, vec, vec, P(), P()),
        check_vma=False,
    )
```

```python
from functools import partial

import jax
import jax.numpy as jnp
from jax import lax
from jax.experimental import pallas as pl
from jax.experimental.pallas import tpu as pltpu
from jax.sharding import PartitionSpec as P

HEADS = 8
EPS = 1e-12
NEG = -1000000000.0
SEGS = 4
EXTRA = 16
SMALL = 32
BLOCK = 512
F32 = jnp.float32
BF16 = jnp.bfloat16
VMEM = pl.BlockSpec(memory_space=pltpu.VMEM)
ANY = pl.BlockSpec(memory_space=pl.ANY)
MIB = 1024 * 1024
HEADF = 100_000_000
PASSED = {
    0: {2: "home"}, 1: {1: "cot", 3: "home"}, 2: {2: "cot"}, 3: {2: "came"}, 4: {0: "cot"}, 6: {1: "came"}, 8: {2: "came"},
}
ADDED = {1: [(1, 2)], 2: [(2, 3)], 3: [(2, 3)], 4: [(0, 1)], 6: [(1, 2)], 8: [(2, 3)]}
PICK = 2
SPLIT = 20_000_000_000
WHOLE = 10_000_000_000
HEAVY = 10_000_000_000
J_A1 = 10_000_000_000
J_D0 = 100_000_000
J_I0 = 10_000_000_000
J_A0 = 10_000_000_000
J_D1 = 10_000_000_000
J_I1 = 10_000_000_000
STORE = 100_000_000
LIMIT = 12
QV_B, OUT_B, GAIN_ONE, SHIFT_ONE, IN_B, DOWN_B, GAIN_TWO, SHIFT_TWO = 0, 2, 3, 4, 5, 9, 10, 11


def mm(a, b):
    return lax.dot_general(a, b, (((1,), (0,)), ((), ())), preferred_element_type=F32)


def mm_nt(a, b):
    return lax.dot_general(a, b, (((1,), (1,)), ((), ())), preferred_element_type=F32)


def mm_tn(a, b):
    return lax.dot_general(a, b, (((0,), (0,)), ((), ())), preferred_element_type=F32)


def lane_masks(width):
    lanes = lax.broadcasted_iota(jnp.int32, (1, 2 * width), 1)
    return (lanes < width).astype(BF16), (lanes >= width).astype(BF16)


def segment_onehot(meta, count, seq_len):
    numbers = lax.broadcasted_iota(jnp.int32, (count, seq_len), 0).astype(F32)
    return (meta[0:1, :seq_len].astype(F32) == numbers).astype(F32)


def norm_stats(values):
    centre = values - jnp.mean(values, axis=-1, keepdims=True)
    spread = jnp.mean(centre * centre, axis=-1, keepdims=True)
    scale = lax.rsqrt(spread + EPS)
    return centre * scale, scale


def norm_back(grad, unit, scale, gain):
    scaled = grad * gain
    mean_one = jnp.mean(scaled, axis=-1, keepdims=True)
    mean_two = jnp.mean(scaled * unit, axis=-1, keepdims=True)
    return scale * (scaled - mean_one - unit * mean_two)


def column_sum(values):
    return jnp.sum(values.astype(F32), axis=0, keepdims=True)


def prepare_kernel(
    x_ref, cot_ref, seg_ref, task_ref, label_ref, qv_b, out_b, gain_one, shift_one, in_b, down_b, gain_two, shift_two, head_ref,
    block_ref, cot_block_ref, vec_ref, head_w_ref,
):
    _, seq_len, width = x_ref.shape
    block_ref[:seq_len, :] = x_ref[0]
    segs = task_ref.shape[1]
    lanes = lax.broadcasted_iota(jnp.int32, (1, width), 1)
    tags = jnp.zeros((1, width), jnp.int32)
    for s in range(segs):
        tags = jnp.where(lanes == seq_len + s, task_ref[0, s], tags)
        tags = jnp.where(lanes == seq_len + segs + s, label_ref[0, s], tags)
    block_ref[seq_len:, :] = jnp.broadcast_to(tags.astype(F32).astype(BF16), (EXTRA, width))
    block_ref[seq_len:, :seq_len] = jnp.broadcast_to(seg_ref[...].astype(F32).astype(BF16), (EXTRA, seq_len))
    cot_block_ref[:seq_len, :] = cot_ref[0]
    cot_block_ref[seq_len:, :] = jnp.zeros((EXTRA, width), BF16)

    row = 0
    for vector in (qv_b, out_b, gain_one, shift_one, in_b, down_b, gain_two, shift_two):
        for part in range(vector.shape[1] // width):
            vec_ref[row : row + 1, :] = vector[:, part * width : (part + 1) * width]
            row += 1
    classes, tasks, _ = head_ref.shape
    head_w_ref[...] = jnp.zeros_like(head_w_ref)
    for c in range(classes):
        head_w_ref[c * tasks : (c + 1) * tasks, :] = head_ref[c]


def forward_kernel(tick, stages, carry, fresh, info, x_ref, *refs):
    refs = list(refs)
    home_ref, cot_ref = (refs.pop(0), refs.pop(0)) if carry else (None, None)
    if tick == 0:
        vec, refs, sems = refs[4], refs[:4] + refs[5:-1], refs[-1]
        qkv_w, out_w, in_w, down_w = weights = refs[-4:]
        copies = [pltpu.make_async_copy(refs[i].at[0], weights[i], sems.at[i]) for i in range(4)]
        for copy in copies:
            copy.start()
        refs = refs[4:-4]
    else:
        copies = []
        qkv_w, out_w, in_w, down_w, vec = refs[:5]
        refs = refs[5:]

    def ready(*which):
        for i in which:
            if copies:
                copies[i].wait()

    if not fresh:
        refs = refs[10:]
    y_ref, keep_ref, qkv_ref, probs_ref, context_ref, unit_one_ref, normed_ref, hidden_ref, slope_ref, unit_two_ref, scales_ref = refs
    seq_len = x_ref.shape[0] - EXTRA
    width = x_ref.shape[1]
    head_dim = width // HEADS
    place = tick - 2 * info[0, 0]
    active = (place >= 0) & (place < stages)

    for stage, what in PASSED.get(tick, {}).items():

        @pl.when(info[0, 0] == stage)
        def _(what=what):
            y_ref[...] = {"home": home_ref, "cot": cot_ref, "came": x_ref}[what][...]

    if tick == 0:

        @pl.when(jnp.logical_not(active))
        def _():
            ready(0, 1, 2, 3)

    @pl.when(active)
    def _():
        meta = x_ref[seq_len:, :]
        y_ref[seq_len:, :] = meta
        x = x_ref[:seq_len, :]
        keep_ref[...] = x
        onehot = segment_onehot(meta, EXTRA, seq_len).astype(BF16)
        barred = jnp.where(mm_tn(onehot, onehot) > 0.5, 0.0, NEG)
        ready(0)
        q = (mm(x, qkv_w[:, :width]) + vec[QV_B : QV_B + 1]).astype(BF16)
        k = mm(x, qkv_w[:, width : 2 * width]).astype(BF16)
        v = (mm(x, qkv_w[:, 2 * width :]) + vec[QV_B + 1 : QV_B + 2]).astype(BF16)
        qkv_ref[:, :width] = q
        qkv_ref[:, width : 2 * width] = k
        qkv_ref[:, 2 * width :] = v
        v_t = v.T
        mask_a, mask_b = lane_masks(head_dim)
        factor = head_dim**-0.5

        def raw_scores(pair):
            cols = slice(pair * 2 * head_dim, (pair + 1) * 2 * head_dim)
            k_two = jnp.concatenate([k[:, cols] * (mask * factor).astype(BF16) for mask in (mask_a, mask_b)], axis=0)
            return mm_nt(k_two, q[:, cols])

        context_parts = []
        shares = []
        ahead = raw_scores(0)
        for pair in range(HEADS // 2):
            both = ahead
            if pair + 1 < HEADS // 2:
                ahead = raw_scores(pair + 1)
            for side in range(2):
                head = 2 * pair + side
                scores = both[side * seq_len : (side + 1) * seq_len] + barred
                expo = jnp.exp(scores - jnp.max(scores, axis=0, keepdims=True))
                share = 1.0 / jnp.sum(expo, axis=0, keepdims=True)
                expo_low = expo.astype(BF16)
                probs_ref[head * seq_len : (head + 1) * seq_len, :] = expo_low
                shares.append(share)
                context_parts.append(mm(v_t[head * head_dim : (head + 1) * head_dim, :], expo_low) * share)
        context = jnp.concatenate(context_parts, axis=0).T.astype(BF16)
        scales_ref[:, 256 : 256 + HEADS] = jnp.concatenate(shares, axis=0).T
        context_ref[...] = context
        ready(1)
        resid = x.astype(F32) + mm(context, out_w[...]) + vec[OUT_B : OUT_B + 1]
        unit_one, scale_one = norm_stats(resid)
        unit_one_ref[...] = unit_one
        normed = unit_one * vec[GAIN_ONE : GAIN_ONE + 1] + vec[SHIFT_ONE : SHIFT_ONE + 1]
        normed_low = normed.astype(BF16)
        normed_ref[...] = normed_low
        summed = normed + vec[DOWN_B : DOWN_B + 1]
        ready(2, 3)
        parts = in_w.shape[1] // 256
        ahead = mm(normed_low, in_w[:, :256])
        for part in range(parts):
            cols = slice(part * 256, (part + 1) * 256)
            pre = ahead + vec[IN_B + part // 2 : IN_B + part // 2 + 1, (part % 2) * 256 : (part % 2 + 1) * 256]
            if part + 1 < parts:
                ahead = mm(normed_low, in_w[:, (part + 1) * 256 : (part + 2) * 256])
            gate = 0.5 + 0.5 * lax.erf(pre * (0.5**0.5))
            slope_ref[:, cols] = (gate + pre * (jnp.exp(-0.5 * pre * pre) * 0.3989422804014327)).astype(BF16)
            hidden = (pre * gate).astype(BF16)
            hidden_ref[:, cols] = hidden
            summed = summed + mm(hidden, down_w[cols, :])
        unit_two, scale_two = norm_stats(summed)
        unit_two_ref[...] = unit_two
        y_ref[:seq_len, :] = (unit_two * vec[GAIN_TWO : GAIN_TWO + 1] + vec[SHIFT_TWO : SHIFT_TWO + 1]).astype(BF16)
        scales_ref[:, 0:128] = jnp.broadcast_to(scale_one, (seq_len, 128))
        scales_ref[:, 128:256] = jnp.broadcast_to(scale_two, (seq_len, 128))


def head_parts(y, meta, cot, head_w, head_b_ref):
    seq_len, width = y.shape
    task_count, class_count = head_b_ref.shape
    high = lax.Precision.HIGHEST
    segs = 8
    onehot = segment_onehot(meta, segs, seq_len)
    row = meta[0:1, :seq_len].astype(F32)
    lanes = lax.broadcasted_iota(jnp.int32, (1, seq_len), 1)
    previous = jnp.where(lanes == 0, -1.0, pltpu.roll(row, 1, 1))
    pick = onehot * (row != previous).astype(F32)
    live = jnp.max(pick, axis=1, keepdims=True)
    cls = mm(pick.astype(BF16), y)
    logits = lax.dot_general(cls, head_w[...], (((1,), (1,)), ((), ())), precision=high, preferred_element_type=F32)
    slots = lax.broadcasted_iota(jnp.int32, (1, logits.shape[1]), 1)
    bias = jnp.zeros((1, logits.shape[1]), F32)
    for t in range(task_count):
        for c in range(class_count):
            bias = jnp.where(slots == c * task_count + t, head_b_ref[t, c], bias)
    logits = logits + bias
    tags = meta[0:1, :].astype(F32)
    spots = lax.broadcasted_iota(jnp.int32, (segs, width), 1) - lax.broadcasted_iota(jnp.int32, (segs, width), 0)
    task = jnp.sum(jnp.where(spots == seq_len, tags, 0.0), axis=1, keepdims=True).astype(jnp.int32)
    label = jnp.sum(jnp.where(spots == seq_len + SEGS, tags, 0.0), axis=1, keepdims=True).astype(jnp.int32)
    mine = jnp.zeros(logits.shape, jnp.bool_)
    for c in range(class_count):
        mine = mine | (slots == task + c * task_count)
    label_hot = slots == task + label * task_count
    masked = jnp.where(mine, logits, -jnp.inf)
    top = jnp.max(masked, axis=1, keepdims=True)
    expo = jnp.exp(masked - top)
    total = jnp.sum(expo, axis=1, keepdims=True)
    right = jnp.sum(jnp.where(label_hot, logits, 0.0), axis=1, keepdims=True)
    loss = live * (top + jnp.log(total) - right)
    d_logits = live * (expo / total - label_hot.astype(F32))
    d_cls = lax.dot_general(d_logits, head_w[...], (((1,), (0,)), ((), ())), precision=high, preferred_element_type=F32)
    upper = d_cls.astype(BF16)
    lower = (d_cls - upper.astype(F32)).astype(BF16)
    ones = pick.astype(BF16)
    d_final = mm_tn(jnp.concatenate([ones, ones], axis=0), jnp.concatenate([upper, lower], axis=0))
    grad = (cot.astype(F32) + d_final).astype(BF16)
    g_w = lax.dot_general(d_logits, cls, (((0,), (0,)), ((), ())), precision=high, preferred_element_type=F32)
    g_b = jnp.concatenate([column_sum(d_logits)] * (width // logits.shape[1]), axis=1)
    rows = lax.broadcasted_iota(jnp.int32, (EXTRA, 1), 0)
    count = task_count * class_count
    heads = jnp.where(rows < count, g_w[:EXTRA], jnp.where(rows == count, g_b, 0.0)).astype(BF16)
    return loss, grad, heads


def row_head_kernel(stages, info, y_ref, cot_ref, head_b_ref, head_w, g_ref):
    seq_len = y_ref.shape[0] - EXTRA

    @pl.when(info[0, 0] == stages - 1)
    def _():
        _, grad, heads = head_parts(y_ref[:seq_len, :], y_ref[seq_len:, :], cot_ref[:seq_len, :], head_w, head_b_ref)
        g_ref[:seq_len, :] = grad
        g_ref[seq_len:, :] = heads


def loss_kernel(stages, info, head_b_ref, *refs):
    y_refs = refs[:stages]
    cot_ref, head_w, final_ref, loss_ref, picked = refs[stages:]
    for s in range(stages):

        @pl.when(info[0, 0] == s)
        def _(s=s):
            picked[...] = y_refs[s][...]

    seq_len, _ = final_ref.shape
    y = picked[:seq_len, :]
    final_ref[...] = y
    loss, _, _ = head_parts(y, picked[seq_len:, :], cot_ref[:seq_len, :], head_w, head_b_ref)
    segs = loss.shape[0]
    wide = lax.broadcasted_iota(jnp.int32, (segs, 128), 1)
    numbers = lax.broadcasted_iota(jnp.int32, (segs, 1), 0)
    loss_ref[...] = jnp.sum(jnp.where(wide == numbers, loss, 0.0), axis=0, keepdims=True)[:, : loss_ref.shape[1]]


def adder(sums_ref):
    def add(row, value):
        sums_ref[row : row + 1, :] += value

    return add


def ffn_back(g_ref, slope_ref, unit_one_ref, unit_two_ref, scales_ref, in_w, down_w, vec, d_pre_ref, d_down_ref, sums_ref):
    seq_len = g_ref.shape[0] - EXTRA
    add = adder(sums_ref)
    sums_ref[SMALL - EXTRA :, :] += g_ref[seq_len:, :].astype(F32)
    grad = g_ref[:seq_len, :].astype(F32)
    scale_one = scales_ref[:, 0:1]
    scale_two = scales_ref[:, 128:129]
    unit_two = unit_two_ref[...]
    add(GAIN_TWO, column_sum(grad * unit_two))
    add(SHIFT_TWO, column_sum(grad))
    d_summed = norm_back(grad, unit_two, scale_two, vec[GAIN_TWO : GAIN_TWO + 1])
    d_down = d_summed.astype(BF16)
    d_down_ref[...] = d_down
    add(DOWN_B, column_sum(d_down))
    d_normed = d_summed
    for part in range(in_w.shape[1] // 256):
        cols = slice(part * 256, (part + 1) * 256)
        d_pre = (mm_nt(d_down, down_w[cols, :]) * slope_ref[:, cols].astype(F32)).astype(BF16)
        d_pre_ref[:, cols] = d_pre
        sums_ref[IN_B + part // 2 : IN_B + part // 2 + 1, (part % 2) * 256 : (part % 2 + 1) * 256] += column_sum(d_pre)
        d_normed = d_normed + mm_nt(d_pre, in_w[:, cols])
    unit_one = unit_one_ref[...]
    add(GAIN_ONE, column_sum(d_normed * unit_one))
    add(SHIFT_ONE, column_sum(d_normed))
    return norm_back(d_normed, unit_one, scale_one, vec[GAIN_ONE : GAIN_ONE + 1])


def attention_back(d_resid, qkv_ref, probs_ref, scales_ref, qkv_w, out_w, next_ref, d_mixed_ref, d_proj_ref, sums_ref, queries):
    seq_len, width = d_resid.shape
    head_dim = width // HEADS
    add = adder(sums_ref)
    d_proj = d_resid.astype(BF16)
    d_proj_ref[...] = d_proj
    add(OUT_B, column_sum(d_proj))
    d_context = mm_nt(d_proj, out_w[...])
    factor = head_dim**-0.5
    mask_a, mask_b = lane_masks(head_dim)
    queries[...] = qkv_ref[:, :width]
    keys = qkv_ref[:, width : 2 * width]
    k_t = (keys * jnp.asarray(factor, BF16)).T
    shares = scales_ref[:, 256 : 256 + HEADS]
    share_rows = shares.T
    d_query_parts = []
    first = lax.broadcasted_iota(jnp.int32, (seq_len, 2 * head_dim), 1) < head_dim

    def weight_gradients_of(pair):
        cols = slice(pair * 2 * head_dim, (pair + 1) * 2 * head_dim)
        v_cols = qkv_ref[:, slice(cols.start + 2 * width, cols.stop + 2 * width)]
        scale = jnp.where(first, shares[:, 2 * pair : 2 * pair + 1], shares[:, 2 * pair + 1 : 2 * pair + 2])
        scaled = (d_context[:, cols] * scale).astype(BF16)
        v_two = jnp.concatenate([v_cols * mask for mask in (mask_a, mask_b)], axis=0)
        return scaled, mm_nt(v_two, scaled)

    ahead = weight_gradients_of(0)
    for pair in range(HEADS // 2):
        scaled, d_probs = ahead
        if pair + 1 < HEADS // 2:
            ahead = weight_gradients_of(pair + 1)
        cols = slice(pair * 2 * head_dim, (pair + 1) * 2 * head_dim)
        rows = slice(pair * 2 * seq_len, (pair + 1) * 2 * seq_len)
        probs = probs_ref[rows, :]
        d_values = mm(probs, scaled)
        parts = []
        for side in range(2):
            half = slice(side * seq_len, (side + 1) * seq_len)
            head = 2 * pair + side
            probs_wide = probs[half].astype(F32)
            total = jnp.sum(probs_wide * d_probs[half], axis=0, keepdims=True) * share_rows[head : head + 1, :]
            d_scores = (probs_wide * (d_probs[half] - total)).astype(BF16)
            parts.append(d_scores)
            d_query_parts.append(mm(k_t[head * head_dim : (head + 1) * head_dim, :], d_scores))
        d_keys = mm(jnp.concatenate(parts, axis=0), queries[:, cols] * jnp.asarray(factor, BF16))
        d_mixed_ref[:, slice(cols.start + width, cols.stop + width)] = jnp.where(first, d_keys[:seq_len], d_keys[seq_len:]).astype(BF16)
        d_mixed_ref[:, slice(cols.start + 2 * width, cols.stop + 2 * width)] = jnp.where(
            first, d_values[:seq_len], d_values[seq_len:]
        ).astype(BF16)
    d_queries = jnp.concatenate(d_query_parts, axis=0).T.astype(BF16)
    d_mixed_ref[:, :width] = d_queries
    add(QV_B, column_sum(d_queries))
    add(QV_B + 1, column_sum(d_mixed_ref[:, 2 * width :]))
    d_input = d_resid + mm_nt(d_mixed_ref[...], qkv_w[...])
    next_ref[:seq_len, :] = d_input.astype(BF16)


def is_active(info, tick, stages):
    place = tick - 2 * info[0, 0]
    return (place >= 0) & (place < stages)


def backward_kernel(tick, stages, own, fresh_proj, fresh_sums, info, g_ref, *refs):
    refs = list(refs)
    own_ref = refs.pop(0) if own else None
    qkv_w, out_w, in_w, down_w, vec = refs[:5]
    qkv_ref, slope_ref, probs_ref, unit_one_ref, unit_two_ref, scales_ref = refs[5:11]
    refs = refs[11:]
    if not fresh_proj:
        refs = refs[2:]
    if not fresh_sums:
        refs = refs[1:]
    next_ref, d_mixed_ref, d_pre_ref, d_proj_ref, d_down_ref, sums_ref, queries, picked = refs
    seq_len = g_ref.shape[0] - EXTRA
    active = is_active(info, tick, stages)

    if own:

        @pl.when(info[0, 0] == stages - 1)
        def _():
            picked[...] = own_ref[...]

        @pl.when(info[0, 0] != stages - 1)
        def _():
            picked[...] = g_ref[...]

        g_ref = picked
    if fresh_sums:
        sums_ref[...] = jnp.zeros_like(sums_ref)

    @pl.when(active)
    def _():
        next_ref[seq_len:, :] = g_ref[seq_len:, :]
        d_resid = ffn_back(
            g_ref, slope_ref, unit_one_ref, unit_two_ref, scales_ref, in_w, down_w, vec, d_pre_ref, d_down_ref, sums_ref
        )
        attention_back(d_resid, qkv_ref, probs_ref, scales_ref, qkv_w, out_w, next_ref, d_mixed_ref, d_proj_ref, sums_ref, queries)


def last_ffn_kernel(
    tick, stages, info, g_ref, in_w, down_w, vec, slope_ref, unit_one_ref, unit_two_ref, scales_ref, d_down_in, sums_in,
    d_pre_ref, d_down_ref, sums_ref, d_resid_ref,
):
    @pl.when(is_active(info, tick, stages))
    def _():
        d_resid_ref[...] = ffn_back(
            g_ref, slope_ref, unit_one_ref, unit_two_ref, scales_ref, in_w, down_w, vec, d_pre_ref, d_down_ref, sums_ref
        )


def last_attention_kernel(
    tick, stages, info, d_resid_ref, qkv_w, out_w, probs_ref, scales_ref, qkv_ref, d_proj_in, sums_in,
    next_ref, d_mixed_ref, d_proj_ref, sums_ref, queries,
):
    @pl.when(is_active(info, tick, stages))
    def _():
        attention_back(d_resid_ref[...], qkv_ref, probs_ref, scales_ref, qkv_w, out_w, next_ref, d_mixed_ref, d_proj_ref, sums_ref, queries)


def half_of(info, theirs):
    return 1 - info[1, 0] if theirs else info[1, 0]


def outer(left, right, rows=None, cols=None):
    rows = slice(None) if rows is None else rows
    cols = slice(None) if cols is None else cols
    return sum(mm_tn(a[:, rows], b[:, cols]) for a, b in zip(left, right))


def down_weights(theirs, info, *refs):
    *refs, out_ref = refs
    hidden, d_down = refs[: len(refs) // 2], refs[len(refs) // 2 :]
    span = hidden[0].shape[1] // 2
    for start in range(0, span, BLOCK):
        at = pl.ds(pl.multiple_of(half_of(info, theirs) * span + start, BLOCK), BLOCK)
        out_ref[start : start + BLOCK, :] = outer(hidden, d_down, rows=at).astype(BF16)


def in_weights(theirs, info, *refs):
    *refs, out_ref = refs
    normed, d_pre = refs[: len(refs) // 2], refs[len(refs) // 2 :]
    width = normed[0].shape[1]
    span = d_pre[0].shape[1] // 2
    for part in range(span // BLOCK):
        at = pl.ds(pl.multiple_of(half_of(info, theirs) * span + part * BLOCK, BLOCK), BLOCK)
        out_ref[part * width : (part + 1) * width, :] = outer(normed, d_pre, cols=at).astype(BF16)


def attention_weights(theirs, info, *refs):
    *refs, sums_ref, out_ref = refs
    slots = len(refs) // 4
    x, context, d_mixed, d_proj = (refs[i * slots : (i + 1) * slots] for i in range(4))
    half = half_of(info, theirs)
    width = x[0].shape[1]
    span = width // 2
    at = pl.ds(pl.multiple_of(half * span, span), span)
    for part in range(3):
        cols = slice(part * width, (part + 1) * width)
        out_ref[part * span : (part + 1) * span, :] = outer(x, d_mixed, rows=at, cols=cols).astype(BF16)
    out_ref[3 * span : 4 * span, :] = outer(context, d_proj, rows=at).astype(BF16)
    out_ref[4 * span :, :] = jnp.zeros((out_ref.shape[0] - 4 * span, width), BF16)
    share = SMALL // 2
    out_ref[4 * span : 4 * span + share, :] = sums_ref[pl.ds(pl.multiple_of(half * share, share), share), :].astype(BF16)


def split_kernel(step, info, mine_ref, came_ref, keep_ref, send_ref):
    rows = keep_ref.shape[0]
    bit = info[2 + step, 0]
    for ref, side in ((send_ref, 1 - bit), (keep_ref, bit)):
        at = pl.ds(pl.multiple_of(side * rows, 16), rows)
        ref[...] = (mine_ref[at, :].astype(F32) + came_ref[at, :].astype(F32)).astype(BF16)


def add_kernel(mine_ref, came_ref, out_ref):
    out_ref[...] = (mine_ref[...].astype(F32) + came_ref[...].astype(F32)).astype(BF16)


def join_kernel(step, info, mine_ref, came_ref, out_ref):
    rows = mine_ref.shape[0]
    bit = info[2 + step, 0]
    out_ref[pl.ds(pl.multiple_of(bit * rows, 16), rows), :] = mine_ref[...]
    out_ref[pl.ds(pl.multiple_of((1 - bit) * rows, 16), rows), :] = came_ref[...]


def store_kernel(name, sides, known, info, *refs):
    parts = refs[: len(sides)]
    token, stage_ref, sems = refs[-3:]
    outs = refs[len(sides) + known : -3]
    token[...] = jnp.zeros_like(token)
    copies = []
    row = 0
    for theirs, part_ref in zip(sides, parts):
        half = half_of(info, theirs)
        width = part_ref.shape[1]
        targets = []
        if name == "down":
            span = outs[0].shape[1] // 2
            for start in range(0, span, BLOCK):
                targets.append((BLOCK, outs[0].at[0, pl.ds(pl.multiple_of(half * span + start, BLOCK), BLOCK), :]))
        elif name == "in":
            span = outs[0].shape[2] // 2
            for start in range(0, span, BLOCK):
                targets.append((width, outs[0].at[0, :, pl.ds(pl.multiple_of(half * span + start, BLOCK), BLOCK)]))
        else:
            span = width // 2
            at = pl.ds(pl.multiple_of(half * span, span), span)
            targets = [(span, outs[0].at[0, at, i * width : (i + 1) * width]) for i in range(3)] + [(span, outs[1].at[0, at, :])]
        start = 0
        for size, dst in targets:
            stage_ref[row : row + size, :] = part_ref[start : start + size, :].astype(F32)
            copies.append(pltpu.make_async_copy(stage_ref.at[row : row + size], dst, sems.at[len(copies)]))
            copies[-1].start()
            start += size
            row += size
    for copy in copies:
        copy.wait()


def small_store_kernel(
    start, info, mine_ref, came_ref, qv_b, out_b, gain_one, shift_one, in_b, down_b, gain_two, shift_two, head_w, head_b, token
):
    token[...] = jnp.zeros_like(token)
    share = SMALL // 2
    mine = mine_ref[start : start + share, :].astype(F32)
    came = came_ref[start : start + share, :].astype(F32)
    first = info[1, 0] == 0
    low = jnp.where(first, mine, came)
    high = jnp.where(first, came, mine)
    width = low.shape[1]
    row = 0
    for vector in (qv_b, out_b, gain_one, shift_one, in_b, down_b, gain_two, shift_two):
        for part in range(vector.shape[1] // width):
            vector[:, part * width : (part + 1) * width] = low[row : row + 1, :]
            row += 1
    classes, tasks, _ = head_w.shape
    for c in range(classes):
        head_w[c] = high[c * tasks : (c + 1) * tasks, :]
    line = high[classes * tasks : classes * tasks + 1, :128]
    lanes = lax.broadcasted_iota(jnp.int32, (16, 128), 1)
    spread = jnp.where(lanes % tasks == lax.broadcasted_iota(jnp.int32, (16, 128), 0), line, 0.0).astype(BF16)
    gather = (lax.broadcasted_iota(jnp.int32, (128, 128), 0) // tasks == lax.broadcasted_iota(jnp.int32, (128, 128), 1)).astype(BF16)
    head_b[...] = mm(spread, gather)[:tasks, :classes]


def relay_kernel(in_ref, out_ref):
    out_ref[...] = in_ref[...]


def pick_kernel(info, *refs):
    *grads, out_ref, token = refs
    token[...] = jnp.zeros_like(token)
    for s, grad in enumerate(grads):

        @pl.when(info[0, 0] == s)
        def _(grad=grad):
            out_ref[...] = grad[: out_ref.shape[0], :]


def shape(dims, dtype):
    return jax.ShapeDtypeStruct(dims, dtype)


def held(dims, dtype):
    return pltpu.VMEM(dims, dtype)


def near(array):
    return pltpu.with_memory_space_constraint(array, pltpu.VMEM)


def far(array):
    return pltpu.with_memory_space_constraint(array, pltpu.HBM)


def call(kernel, name, out_shape, args, in_specs, out_specs=None, aliases=None, scratch=(), flops=0, limit=LIMIT, after=()):
    single = not isinstance(out_shape, tuple)
    if out_specs is None:
        out_specs = VMEM if single else (VMEM,) * len(out_shape)
    count, extra = len(args), len(after)

    def body(*refs):
        kernel(*refs[:count], *refs[count + extra :])

    args = tuple(args) + tuple(near(a) for a in after)
    in_specs = list(in_specs) + [ANY] * extra
    return pl.pallas_call(
        body,
        out_shape=out_shape,
        in_specs=in_specs,
        out_specs=out_specs,
        scratch_shapes=scratch,
        input_output_aliases=aliases or {},
        compiler_params=pltpu.CompilerParams(vmem_limit_bytes=limit * MIB),
        cost_estimate=pl.CostEstimate(flops=flops, bytes_accessed=0, transcendentals=0),
        name=name,
    )(*args)


def piece(kernel, args, specs, out_shape, out_specs=None, aliases=None, scratch=()):
    return kernel, tuple(args), list(specs), tuple(out_shape), out_specs or (VMEM,) * len(out_shape), aliases or {}, list(scratch)


def fused(name, pieces, **rest):
    counts = [(len(args), len(outs), len(scratch)) for _, args, _, outs, _, _, scratch in pieces]
    sums = [sum(c[i] for c in counts) for i in range(3)]

    def kernel(*refs):
        ins, outs, scratch = refs[: sums[0]], refs[sums[0] : sums[0] + sums[1]], refs[sums[0] + sums[1] :]
        for (part, *_), (a, b, c) in zip(pieces, counts):
            part(*ins[:a], *outs[:b], *scratch[:c])
            ins, outs, scratch = ins[a:], outs[b:], scratch[c:]

    aliases = {}
    a = b = 0
    for (_, _, _, _, _, own, _), count in zip(pieces, counts):
        aliases |= {a + i: b + o for i, o in own.items()}
        a, b = a + count[0], b + count[1]
    results = call(
        kernel,
        name,
        sum((p[3] for p in pieces), ()),
        sum((p[1] for p in pieces), ()),
        sum((p[2] for p in pieces), []),
        sum((tuple(p[4]) for p in pieces), ()),
        aliases=aliases,
        scratch=sum((p[6] for p in pieces), []),
        **rest,
    )
    split = []
    for count in counts:
        split.append(results[: count[1]])
        results = results[count[1] :]
    return split


def local(
    hidden_in, segment_ids, task_ids, labels, cotangent, qkv_weight, qv_bias, out_weight, out_bias, norm1_gain, norm1_bias,
    ffn_in_weight, ffn_in_bias, ffn_out_weight, ffn_out_bias, norm2_gain, norm2_bias, head_weight, head_bias,
):
    stages = lax.axis_size("pipe")
    stage = lax.axis_index("pipe")
    shards = lax.axis_size("dp")
    shard = lax.axis_index("dp")
    _, seq_len, width = hidden_in.shape
    hidden_width = ffn_in_weight.shape[2]
    task_count, _, class_count = head_weight.shape
    block = (seq_len + EXTRA, width)

    bits = shards.bit_length() - 1
    upward = list(range(1, bits))
    orders = (upward, upward[::-1])
    core = shard & 1
    sides = [jnp.where(core == 0, (shard >> orders[0][j]) & 1, (shard >> orders[1][j]) & 1) for j in range(bits - 1)]
    info = jnp.stack([stage, core] + sides + [stage] * (6 - len(sides))).astype(jnp.int32)
    info = near(jnp.broadcast_to(info[:, None], (8, 128)))

    home, cot_block, vec, head_w = call(
        prepare_kernel,
        "prepare",
        (held(block, BF16), held(block, BF16), held((16, width), F32), held((16, width), F32)),
        tuple(
            far(a)
            for a in (
                hidden_in, cotangent, segment_ids, task_ids, labels, qv_bias, out_bias, norm1_gain, norm1_bias, ffn_in_bias, ffn_out_bias,
                norm2_gain, norm2_bias, head_weight.transpose(2, 0, 1),
            )
        ),
        [VMEM] * 14,
    )
    head_b = near(head_bias)
    weights = tuple(far(w) for w in (qkv_weight, out_weight, ffn_in_weight, ffn_out_weight)) + (near(vec),)
    weight_shapes = tuple(held(w.shape[1:], BF16) for w in weights[:4])

    def move(array, pairs):
        return lax.ppermute(array, "pipe", pairs)

    def route(tick):
        pairs = [(s, s + 1) for s in range(stages - 1) if 0 <= tick - 2 * s < stages]
        if tick + 2 < stages:
            pairs.append((tick + 2, 0))
        pairs += ADDED.get(tick, [])
        late = tick - 2 * (stages - 1)
        if 0 <= late < stages - 1:
            pairs.append((stages - 1, late))
        return pairs

    def back(tick):
        pairs = [(s + 1, s) for s in range(stages - 1) if 0 <= tick - 2 * s < stages]
        if tick + 2 < stages:
            pairs.append((0, tick + 2))
        return pairs

    ticks = 2 * (stages - 1) + stages
    saved_shapes = (
        held((seq_len, width), BF16),
        held((seq_len, 3 * width), BF16),
        held((HEADS * seq_len, seq_len), BF16),
        held((seq_len, width), BF16),
        held((seq_len, width), F32),
        held((seq_len, width), BF16),
        held((seq_len, hidden_width), BF16),
        held((seq_len, hidden_width), BF16),
        held((seq_len, width), F32),
        held((seq_len, 384), F32),
    )
    arrived = {0: home, 1: move(home, [(1, 0)])}
    slots = [None] * stages
    last = None
    own_heads, final_blocks = {}, {}

    def row_heads(final, cots, after=()):
        return call(
            partial(row_head_kernel, stages),
            "row_heads",
            held(block, BF16),
            [info, near(final), near(cots), head_b, near(head_w)],
            [VMEM] * 5,
            flops=HEADF,
            after=after,
        )

    for tick in range(ticks):
        carry = any(what != "came" for what in PASSED.get(tick, {}).values())
        fresh = slots[tick % stages] is None
        args = [info, near(arrived[tick])] + ([near(home), near(cot_block)] if carry else []) + list(weights)
        aliases = {}
        if not fresh:
            aliases = {len(args) + i: 1 + i for i in range(len(saved_shapes))}
            args += [near(a) for a in slots[tick % stages]]
        outs = call(
            partial(forward_kernel, tick, stages, carry, fresh),
            "layer_forward",
            (held(block, BF16),) + saved_shapes + (() if tick else weight_shapes),
            args,
            [ANY if a is w else VMEM for a in args for w in [next((w for w in weights[:4] if w is a and not tick), None)]],
            aliases=aliases,
            scratch=[] if tick else [pltpu.SemaphoreType.DMA((4,))],
            flops=4_000_000_000,
        )
        if tick == 0:
            weights = tuple(near(w) for w in outs[-4:]) + (near(vec),)
        slots[tick % stages] = tuple(outs[1:11])
        last = outs[0]
        if route(tick):
            arrived[tick + 2] = move(last, route(tick))
        if tick >= 2 * (stages - 1):
            final_blocks[tick] = last
    finals = [arrived[2 * (stages - 1) + 2 + s] for s in range(stages - 1)] + [last]
    own_heads[ticks - 1] = row_heads(last, cot_block)

    cots = {8: arrived[4], 7: arrived[5], 6: arrived[10]}
    arrived = {ticks - 1: own_heads[ticks - 1]}
    proj = [None] * stages
    sums = None
    results = {}
    for tick in reversed(range(1, ticks)):
        slot = tick % stages
        if tick in cots:
            own_heads[tick] = row_heads(final_blocks[tick], cots[tick], [last])
            arrived.setdefault(tick, own_heads[tick])
        own = tick in own_heads and tick < ticks - 2
        x, qkv, probs, context, unit_one, normed, hidden, slope, unit_two, scales = slots[slot]
        args = [info, near(arrived[tick])] + ([near(own_heads[tick])] if own else []) + list(weights)
        aliases = {len(args): 1, len(args) + 1: 2}
        args += [near(a) for a in (qkv, slope, probs, unit_one, unit_two, scales)]
        fresh_proj, fresh_sums = proj[slot] is None, sums is None
        if not fresh_proj:
            aliases |= {len(args): 3, len(args) + 1: 4}
            args += [near(a) for a in proj[slot]]
        if not fresh_sums:
            aliases |= {len(args): 5}
            args += [near(sums)]
        last, d_mixed, d_pre, d_proj, d_down, sums = call(
            partial(backward_kernel, tick, stages, own, fresh_proj, fresh_sums),
            "layer_backward",
            (
                held(block, BF16),
                held((seq_len, 3 * width), BF16),
                held((seq_len, hidden_width), BF16),
                held((seq_len, width), BF16),
                held((seq_len, width), BF16),
                held((SMALL, width), F32),
            ),
            args,
            [VMEM] + [VMEM] * (len(args) - 1),
            aliases=aliases,
            scratch=[pltpu.VMEM((seq_len, width), BF16), pltpu.VMEM(block, BF16)],
            flops=4_000_000_000,
        )
        proj[slot] = (d_proj, d_down)
        slots[slot] = (x, d_mixed, probs, context, unit_one, normed, hidden, d_pre, unit_two, scales)
        if tick >= 2:
            arrived[tick - 2] = move(last, back(tick - 2))
        if 2 <= tick < stages:
            results[tick] = arrived[tick - 2]

    def flip(bit):
        return [(i, i ^ (1 << bit)) for i in range(shards)]

    def across(step):
        return [(i, i ^ (1 << orders[i & 1][step])) for i in range(shards)]

    def swap(array, pairs):
        return lax.ppermute(array, "dp", pairs)

    second_last = last
    x, qkv, probs, context, unit_one, normed, hidden, slope, unit_two, scales = slots[0]
    qkv_w, out_w, in_w, down_w, vec = weights
    args = [info, near(arrived[0]), in_w, down_w, vec] + [near(a) for a in (slope, unit_one, unit_two, scales, proj[0][1], sums)]
    d_pre, d_down, sums, d_resid = call(
        partial(last_ffn_kernel, 0, stages),
        "last_ffn_backward",
        (held((seq_len, hidden_width), BF16), held((seq_len, width), BF16), held((SMALL, width), F32), held((seq_len, width), F32)),
        args,
        [VMEM] * len(args),
        aliases={5: 0, 9: 1, 10: 2},
    )
    LIGHT = 100_000_000
    tail = [d_resid]
    token = held((8, 128), F32)

    def run(name, *pieces, flops=10_000_000_000, **rest):
        split = fused(name, pieces, after=[tail[0]], flops=flops, **rest)
        tail[0] = split[-1][-1]
        return split

    unit = 16 * shards // 2
    half_hidden = hidden_width // 2
    small_start = 2 * width
    rows = {
        "down": half_hidden,
        "in": half_hidden * width // BLOCK,
        "attention": -(-(small_start + SMALL // 2) // unit) * unit,
    }
    mine, came = {}, {}

    def kept(index):
        return [near(slots[s][index]) for s in range(stages)]

    def products(p, theirs):
        if p == "down":
            kernel, arrays = down_weights, kept(6) + [near(d_down if s == 0 else proj[s][1]) for s in range(stages)]
        elif p == "in":
            kernel, arrays = in_weights, kept(5) + [near(d_pre if s == 0 else slots[s][7]) for s in range(stages)]
        else:
            kernel = attention_weights
            arrays = kept(0) + kept(3) + kept(1) + [near(proj[s][0]) for s in range(stages)] + [near(sums)]
        args = [info] + arrays
        return piece(partial(kernel, theirs), args, [VMEM] * len(args), (held((rows[p], width), BF16),))

    def split(p, step):
        out = held((mine[p].shape[0] // 2, width), BF16)
        ((mine[p], send),) = run("split_sum", flops=SPLIT, *(piece(partial(split_kernel, step), (info, near(mine[p]), near(came[p])), [VMEM] * 3, (out, out)),))
        came[p] = swap(send, across(step))

    def whole(p):
        ((mine[p],),) = run("last_sum", piece(add_kernel, (near(mine[p]), near(came[p])), [VMEM] * 2, (held(mine[p].shape, BF16),)), flops=WHOLE)
        came[p] = swap(mine[p], across(bits - 2))

    COST = {("attention", 1): J_A1, ("down", 0): J_D0, ("in", 0): J_I0, ("attention", 0): J_A0, ("down", 1): J_D1, ("in", 1): J_I1}

    def join(p, step, beside=()):
        out = held((2 * mine[p].shape[0], width), BF16)
        joined = piece(partial(join_kernel, step), (info, near(mine[p]), near(came[p])), [VMEM] * 3, (out,))
        *others, (mine[p],) = run("join", *beside, joined, flops=COST.get((p, step), HEAVY), limit=8)
        came[p] = swap(mine[p], across(step - 1) if step else flip(0))
        return others

    dims = {"down": ((1, hidden_width, width),), "in": ((1, width, hidden_width),), "attention": ((1, width, 3 * width), (1, width, width))}
    out_grads = {}

    def stored(p, sides):
        known = out_grads.get(p, ())
        parts = tuple(near(came[p] if theirs else mine[p]) for theirs in sides)
        args = (info,) + parts + tuple(far(g) for g in known)
        size = len(sides) * (2 * width if p == "attention" else rows[p])
        return piece(
            partial(store_kernel, p, sides, len(known)),
            args,
            [VMEM] * (1 + len(sides)) + [ANY] * len(known),
            tuple(pltpu.HBM(d, F32) for d in dims[p]) + (token,),
            (ANY,) * len(dims[p]) + (VMEM,),
            {1 + len(sides) + i: i for i in range(len(known))},
            [pltpu.VMEM((size, width), F32), pltpu.SemaphoreType.DMA((4 * len(sides),))],
        )

    ((theirs,),) = run("down_gradients", products("down", True), flops=LIGHT)
    came["down"] = swap(theirs, flip(0))
    (mine["down"],), (theirs,) = run("ffn_gradients", products("down", False), products("in", True), flops=LIGHT)
    came["in"] = swap(theirs, flip(0))
    split("down", 0)
    ((mine["in"],),) = run("in_gradients", products("in", False), flops=LIGHT)
    split("in", 0)
    args = [info, near(d_resid), qkv_w, out_w] + [near(a) for a in (probs, scales, qkv, proj[0][0], sums)]
    ((last, d_mixed, d_proj, sums),) = run(
        "last_attention_backward",
        piece(
            partial(last_attention_kernel, 0, stages),
            args,
            [VMEM] * len(args),
            (held(block, BF16), held((seq_len, 3 * width), BF16), held((seq_len, width), BF16), held((SMALL, width), F32)),
            aliases={6: 1, 7: 2, 8: 3},
            scratch=[pltpu.VMEM((seq_len, width), BF16)],
        ),
        flops=LIGHT,
    )
    results[0] = last
    results[1] = second_last
    slots[0] = (x, d_mixed) + slots[0][2:]
    proj[0] = (d_proj, d_down)
    (theirs,), (mine["attention"],) = run("attention_gradients", products("attention", True), products("attention", False), flops=LIGHT)
    came["attention"] = swap(theirs, flip(0))
    split("down", 1)
    split("attention", 0)
    ((results[1],),) = run("relay", piece(relay_kernel, (near(results[1]),), [VMEM], (held(block, BF16),)))
    results[1] = move(results[1], [(0, 1)])
    pick = piece(
        pick_kernel, [info] + [near(results[s]) for s in range(stages)], [VMEM] * (1 + stages), (shape((seq_len, width), BF16), token)
    )
    rows_out = piece(
        partial(loss_kernel, stages),
        [info, head_b] + [near(f) for f in finals] + [near(cot_block), near(head_w)],
        [VMEM] * (stages + 4),
        (shape((seq_len, width), BF16), shape(task_ids.shape, F32)),
        scratch=[pltpu.VMEM(block, BF16)],
    )
    moves = [partial(split, step=step) for step in range(1, bits - 1)] + [whole] + [partial(join, step=step) for step in reversed(range(bits - 1))]
    todo = {"in": moves[:-1], "down": moves[1:], "attention": moves[:-1]}
    while any(todo.values()):
        for p, steps in todo.items():
            if steps:
                steps.pop(0)(p)
                if p == "in" and len(steps) == PICK:
                    (hidden_out, losses), (hidden_grad, _) = run("pick_gradient", rows_out, pick)
    (((*out_grads["down"], _)),) = join("in", 0, [stored("down", (False, True))])
    (((*out_grads["in"], _)),) = run("store", stored("in", (False,)), flops=STORE)
    join("attention", 0)
    (*out_grads["in"], _), (*out_grads["attention"], _) = run(
        "store", stored("in", (True,)), stored("attention", (False,)), limit=8, flops=HEAVY
    )
    vectors = tuple(shape((1, n), F32) for n in (2 * width, width, width, width, hidden_width, width, width, width))
    small = piece(
        partial(small_store_kernel, small_start),
        [info, near(mine["attention"]), near(came["attention"])],
        [VMEM] * 3,
        vectors + (shape((class_count, task_count, width), F32), shape((task_count, class_count), F32), token),
    )
    (*out_grads["attention"], _), (*vectors, head_w_grad, head_b_grad, _) = run("store", stored("attention", (True,)), small)
    qv_grad, out_b_grad, gain_one_grad, shift_one_grad, in_b_grad, down_b_grad, gain_two_grad, shift_two_grad = vectors
    return (
        hidden_out[None],
        losses,
        hidden_grad[None],
        out_grads["attention"][0],
        qv_grad,
        out_grads["attention"][1],
        out_b_grad,
        gain_one_grad,
        shift_one_grad,
        out_grads["in"][0],
        in_b_grad,
        out_grads["down"][0],
        down_b_grad,
        gain_two_grad,
        shift_two_grad,
        head_w_grad.transpose(1, 2, 0),
        head_b_grad,
    )


def solution(mesh):
    rows = P(("dp", "pipe"), None, None)
    ids = P(("dp", "pipe"), None)
    big = P("pipe", None, None)
    vec = P("pipe", None)
    return jax.shard_map(
        local,
        mesh=mesh,
        in_specs=(rows, ids, ids, ids, rows, big, vec, big, vec, vec, vec, big, vec, big, vec, vec, vec, P(), P()),
        out_specs=(rows, ids, rows, big, vec, big, vec, vec, vec, big, vec, big, vec, vec, vec, P(), P()),
        check_vma=False,
    )
```

```python
from functools import partial

import jax
import jax.numpy as jnp
from jax import lax
from jax.experimental import pallas as pl
from jax.experimental.pallas import tpu as pltpu
from jax.sharding import PartitionSpec as P

HEADS = 8
EPS = 1e-12
NEG = -1000000000.0
SEGS = 4
EXTRA = 16
SMALL = 32
BLOCK = 512
F32 = jnp.float32
BF16 = jnp.bfloat16
VMEM = pl.BlockSpec(memory_space=pltpu.VMEM)
ANY = pl.BlockSpec(memory_space=pl.ANY)
MIB = 1024 * 1024
HEADF = 100_000_000
PASSED = {
    0: {2: "home"}, 1: {1: "cot", 3: "home"}, 2: {2: "cot"}, 3: {2: "came"}, 4: {0: "cot"}, 6: {1: "came"}, 8: {2: "came"},
}
ADDED = {1: [(1, 2)], 2: [(2, 3)], 3: [(2, 3)], 4: [(0, 1)], 6: [(1, 2)], 8: [(2, 3)]}
PICK = 2
SPLIT = 20_000_000_000
WHOLE = 10_000_000_000
HEAVY = 10_000_000_000
J_A1 = 10_000_000_000
J_D0 = 100_000_000
J_I0 = 10_000_000_000
J_A0 = 10_000_000_000
J_D1 = 10_000_000_000
J_I1 = 10_000_000_000
STORE = 100_000_000
LIMIT = 12
QV_B, OUT_B, GAIN_ONE, SHIFT_ONE, IN_B, DOWN_B, GAIN_TWO, SHIFT_TWO = 0, 2, 3, 4, 5, 9, 10, 11


def mm(a, b):
    return lax.dot_general(a, b, (((1,), (0,)), ((), ())), preferred_element_type=F32)


def mm_nt(a, b):
    return lax.dot_general(a, b, (((1,), (1,)), ((), ())), preferred_element_type=F32)


def mm_tn(a, b):
    return lax.dot_general(a, b, (((0,), (0,)), ((), ())), preferred_element_type=F32)


def lane_masks(width):
    lanes = lax.broadcasted_iota(jnp.int32, (1, 2 * width), 1)
    return (lanes < width).astype(BF16), (lanes >= width).astype(BF16)


def segment_onehot(meta, count, seq_len):
    numbers = lax.broadcasted_iota(jnp.int32, (count, seq_len), 0).astype(F32)
    return (meta[0:1, :seq_len].astype(F32) == numbers).astype(F32)


def norm_stats(values):
    centre = values - jnp.mean(values, axis=-1, keepdims=True)
    spread = jnp.mean(centre * centre, axis=-1, keepdims=True)
    scale = lax.rsqrt(spread + EPS)
    return centre * scale, scale


def norm_back(grad, unit, scale, gain):
    scaled = grad * gain
    mean_one = jnp.mean(scaled, axis=-1, keepdims=True)
    mean_two = jnp.mean(scaled * unit, axis=-1, keepdims=True)
    return scale * (scaled - mean_one - unit * mean_two)


def column_sum(values):
    return jnp.sum(values.astype(F32), axis=0, keepdims=True)


def prepare_kernel(
    x_ref, cot_ref, seg_ref, task_ref, label_ref, qv_b, out_b, gain_one, shift_one, in_b, down_b, gain_two, shift_two, head_ref,
    block_ref, cot_block_ref, vec_ref, head_w_ref,
):
    _, seq_len, width = x_ref.shape
    block_ref[:seq_len, :] = x_ref[0]
    segs = task_ref.shape[1]
    lanes = lax.broadcasted_iota(jnp.int32, (1, width), 1)
    tags = jnp.zeros((1, width), jnp.int32)
    for s in range(segs):
        tags = jnp.where(lanes == seq_len + s, task_ref[0, s], tags)
        tags = jnp.where(lanes == seq_len + segs + s, label_ref[0, s], tags)
    block_ref[seq_len:, :] = jnp.broadcast_to(tags.astype(F32).astype(BF16), (EXTRA, width))
    block_ref[seq_len:, :seq_len] = jnp.broadcast_to(seg_ref[...].astype(F32).astype(BF16), (EXTRA, seq_len))
    cot_block_ref[:seq_len, :] = cot_ref[0]
    cot_block_ref[seq_len:, :] = jnp.zeros((EXTRA, width), BF16)

    row = 0
    for vector in (qv_b, out_b, gain_one, shift_one, in_b, down_b, gain_two, shift_two):
        for part in range(vector.shape[1] // width):
            vec_ref[row : row + 1, :] = vector[:, part * width : (part + 1) * width]
            row += 1
    classes, tasks, _ = head_ref.shape
    head_w_ref[...] = jnp.zeros_like(head_w_ref)
    for c in range(classes):
        head_w_ref[c * tasks : (c + 1) * tasks, :] = head_ref[c]


def forward_kernel(tick, stages, carry, fresh, info, x_ref, *refs):
    refs = list(refs)
    home_ref, cot_ref = (refs.pop(0), refs.pop(0)) if carry else (None, None)
    if tick == 0:
        vec, refs, sems = refs[4], refs[:4] + refs[5:-1], refs[-1]
        qkv_w, out_w, in_w, down_w = weights = refs[-4:]
        copies = [pltpu.make_async_copy(refs[i].at[0], weights[i], sems.at[i]) for i in range(4)]
        for copy in copies:
            copy.start()
        refs = refs[4:-4]
    else:
        copies = []
        qkv_w, out_w, in_w, down_w, vec = refs[:5]
        refs = refs[5:]

    def ready(*which):
        for i in which:
            if copies:
                copies[i].wait()

    if not fresh:
        refs = refs[10:]
    y_ref, keep_ref, qkv_ref, probs_ref, context_ref, unit_one_ref, normed_ref, hidden_ref, slope_ref, unit_two_ref, scales_ref = refs
    seq_len = x_ref.shape[0] - EXTRA
    width = x_ref.shape[1]
    head_dim = width // HEADS
    place = tick - 2 * info[0, 0]
    active = (place >= 0) & (place < stages)

    for stage, what in PASSED.get(tick, {}).items():

        @pl.when(info[0, 0] == stage)
        def _(what=what):
            y_ref[...] = {"home": home_ref, "cot": cot_ref, "came": x_ref}[what][...]

    if tick == 0:

        @pl.when(jnp.logical_not(active))
        def _():
            ready(0, 1, 2, 3)

    @pl.when(active)
    def _():
        meta = x_ref[seq_len:, :]
        y_ref[seq_len:, :] = meta
        x = x_ref[:seq_len, :]
        keep_ref[...] = x
        onehot = segment_onehot(meta, EXTRA, seq_len).astype(BF16)
        barred = jnp.where(mm_tn(onehot, onehot) > 0.5, 0.0, NEG)
        ready(0)
        q = (mm(x, qkv_w[:, :width]) + vec[QV_B : QV_B + 1]).astype(BF16)
        k = mm(x, qkv_w[:, width : 2 * width]).astype(BF16)
        v = (mm(x, qkv_w[:, 2 * width :]) + vec[QV_B + 1 : QV_B + 2]).astype(BF16)
        qkv_ref[:, :width] = q
        qkv_ref[:, width : 2 * width] = k
        qkv_ref[:, 2 * width :] = v
        v_t = v.T
        mask_a, mask_b = lane_masks(head_dim)
        factor = head_dim**-0.5

        def raw_scores(pair):
            cols = slice(pair * 2 * head_dim, (pair + 1) * 2 * head_dim)
            k_two = jnp.concatenate([k[:, cols] * (mask * factor).astype(BF16) for mask in (mask_a, mask_b)], axis=0)
            return mm_nt(k_two, q[:, cols])

        context_parts = []
        shares = []
        ahead = raw_scores(0)
        for pair in range(HEADS // 2):
            both = ahead
            if pair + 1 < HEADS // 2:
                ahead = raw_scores(pair + 1)
            for side in range(2):
                head = 2 * pair + side
                scores = both[side * seq_len : (side + 1) * seq_len] + barred
                expo = jnp.exp(scores - jnp.max(scores, axis=0, keepdims=True))
                share = 1.0 / jnp.sum(expo, axis=0, keepdims=True)
                expo_low = expo.astype(BF16)
                probs_ref[head * seq_len : (head + 1) * seq_len, :] = expo_low
                shares.append(share)
                context_parts.append(mm(v_t[head * head_dim : (head + 1) * head_dim, :], expo_low) * share)
        context = jnp.concatenate(context_parts, axis=0).T.astype(BF16)
        scales_ref[:, 256 : 256 + HEADS] = jnp.concatenate(shares, axis=0).T
        context_ref[...] = context
        ready(1)
        resid = x.astype(F32) + mm(context, out_w[...]) + vec[OUT_B : OUT_B + 1]
        unit_one, scale_one = norm_stats(resid)
        unit_one_ref[...] = unit_one
        normed = unit_one * vec[GAIN_ONE : GAIN_ONE + 1] + vec[SHIFT_ONE : SHIFT_ONE + 1]
        normed_low = normed.astype(BF16)
        normed_ref[...] = normed_low
        summed = normed + vec[DOWN_B : DOWN_B + 1]
        ready(2, 3)
        parts = in_w.shape[1] // 2048
        ahead = mm(normed_low, in_w[:, :2048])
        for part in range(parts):
            cols = slice(part * 2048, (part + 1) * 2048)
            pre = ahead + jnp.concatenate([vec[IN_B + part * 4 + i : IN_B + part * 4 + i + 1] for i in range(4)], axis=1)
            if part + 1 < parts:
                ahead = mm(normed_low, in_w[:, (part + 1) * 2048 : (part + 2) * 2048])
            gate = 0.5 + 0.5 * lax.erf(pre * (0.5**0.5))
            slope_ref[:, cols] = (gate + pre * (jnp.exp(-0.5 * pre * pre) * 0.3989422804014327)).astype(BF16)
            hidden = (pre * gate).astype(BF16)
            hidden_ref[:, cols] = hidden
            summed = summed + mm(hidden, down_w[cols, :])
        unit_two, scale_two = norm_stats(summed)
        unit_two_ref[...] = unit_two
        y_ref[:seq_len, :] = (unit_two * vec[GAIN_TWO : GAIN_TWO + 1] + vec[SHIFT_TWO : SHIFT_TWO + 1]).astype(BF16)
        scales_ref[:, 0:128] = jnp.broadcast_to(scale_one, (seq_len, 128))
        scales_ref[:, 128:256] = jnp.broadcast_to(scale_two, (seq_len, 128))


def head_parts(y, meta, cot, head_w, head_b_ref):
    seq_len, width = y.shape
    task_count, class_count = head_b_ref.shape
    high = lax.Precision.HIGHEST
    segs = 8
    onehot = segment_onehot(meta, segs, seq_len)
    row = meta[0:1, :seq_len].astype(F32)
    lanes = lax.broadcasted_iota(jnp.int32, (1, seq_len), 1)
    previous = jnp.where(lanes == 0, -1.0, pltpu.roll(row, 1, 1))
    pick = onehot * (row != previous).astype(F32)
    live = jnp.max(pick, axis=1, keepdims=True)
    cls = mm(pick.astype(BF16), y)
    logits = lax.dot_general(cls, head_w[...], (((1,), (1,)), ((), ())), precision=high, preferred_element_type=F32)
    slots = lax.broadcasted_iota(jnp.int32, (1, logits.shape[1]), 1)
    bias = jnp.zeros((1, logits.shape[1]), F32)
    for t in range(task_count):
        for c in range(class_count):
            bias = jnp.where(slots == c * task_count + t, head_b_ref[t, c], bias)
    logits = logits + bias
    tags = meta[0:1, :].astype(F32)
    spots = lax.broadcasted_iota(jnp.int32, (segs, width), 1) - lax.broadcasted_iota(jnp.int32, (segs, width), 0)
    task = jnp.sum(jnp.where(spots == seq_len, tags, 0.0), axis=1, keepdims=True).astype(jnp.int32)
    label = jnp.sum(jnp.where(spots == seq_len + SEGS, tags, 0.0), axis=1, keepdims=True).astype(jnp.int32)
    mine = jnp.zeros(logits.shape, jnp.bool_)
    for c in range(class_count):
        mine = mine | (slots == task + c * task_count)
    label_hot = slots == task + label * task_count
    masked = jnp.where(mine, logits, -jnp.inf)
    top = jnp.max(masked, axis=1, keepdims=True)
    expo = jnp.exp(masked - top)
    total = jnp.sum(expo, axis=1, keepdims=True)
    right = jnp.sum(jnp.where(label_hot, logits, 0.0), axis=1, keepdims=True)
    loss = live * (top + jnp.log(total) - right)
    d_logits = live * (expo / total - label_hot.astype(F32))
    d_cls = lax.dot_general(d_logits, head_w[...], (((1,), (0,)), ((), ())), precision=high, preferred_element_type=F32)
    upper = d_cls.astype(BF16)
    lower = (d_cls - upper.astype(F32)).astype(BF16)
    ones = pick.astype(BF16)
    d_final = mm_tn(jnp.concatenate([ones, ones], axis=0), jnp.concatenate([upper, lower], axis=0))
    grad = (cot.astype(F32) + d_final).astype(BF16)
    g_w = lax.dot_general(d_logits, cls, (((0,), (0,)), ((), ())), precision=high, preferred_element_type=F32)
    g_b = jnp.concatenate([column_sum(d_logits)] * (width // logits.shape[1]), axis=1)
    rows = lax.broadcasted_iota(jnp.int32, (EXTRA, 1), 0)
    count = task_count * class_count
    heads = jnp.where(rows < count, g_w[:EXTRA], jnp.where(rows == count, g_b, 0.0)).astype(BF16)
    return loss, grad, heads


def row_head_kernel(stages, info, y_ref, cot_ref, head_b_ref, head_w, g_ref):
    seq_len = y_ref.shape[0] - EXTRA

    @pl.when(info[0, 0] == stages - 1)
    def _():
        _, grad, heads = head_parts(y_ref[:seq_len, :], y_ref[seq_len:, :], cot_ref[:seq_len, :], head_w, head_b_ref)
        g_ref[:seq_len, :] = grad
        g_ref[seq_len:, :] = heads


def loss_kernel(stages, info, head_b_ref, *refs):
    y_refs = refs[:stages]
    cot_ref, head_w, final_ref, loss_ref, picked = refs[stages:]
    for s in range(stages):

        @pl.when(info[0, 0] == s)
        def _(s=s):
            picked[...] = y_refs[s][...]

    seq_len, _ = final_ref.shape
    y = picked[:seq_len, :]
    final_ref[...] = y
    loss, _, _ = head_parts(y, picked[seq_len:, :], cot_ref[:seq_len, :], head_w, head_b_ref)
    segs = loss.shape[0]
    wide = lax.broadcasted_iota(jnp.int32, (segs, 128), 1)
    numbers = lax.broadcasted_iota(jnp.int32, (segs, 1), 0)
    loss_ref[...] = jnp.sum(jnp.where(wide == numbers, loss, 0.0), axis=0, keepdims=True)[:, : loss_ref.shape[1]]


def adder(sums_ref):
    def add(row, value):
        sums_ref[row : row + 1, :] += value

    return add


def ffn_back(g_ref, slope_ref, unit_one_ref, unit_two_ref, scales_ref, in_w, down_w, vec, d_pre_ref, d_down_ref, sums_ref):
    seq_len = g_ref.shape[0] - EXTRA
    add = adder(sums_ref)
    sums_ref[SMALL - EXTRA :, :] += g_ref[seq_len:, :].astype(F32)
    grad = g_ref[:seq_len, :].astype(F32)
    scale_one = scales_ref[:, 0:1]
    scale_two = scales_ref[:, 128:129]
    unit_two = unit_two_ref[...]
    add(GAIN_TWO, column_sum(grad * unit_two))
    add(SHIFT_TWO, column_sum(grad))
    d_summed = norm_back(grad, unit_two, scale_two, vec[GAIN_TWO : GAIN_TWO + 1])
    d_down = d_summed.astype(BF16)
    d_down_ref[...] = d_down
    add(DOWN_B, column_sum(d_down))
    d_normed = d_summed
    for part in range(in_w.shape[1] // 256):
        cols = slice(part * 256, (part + 1) * 256)
        d_pre = (mm_nt(d_down, down_w[cols, :]) * slope_ref[:, cols].astype(F32)).astype(BF16)
        d_pre_ref[:, cols] = d_pre
        sums_ref[IN_B + part // 2 : IN_B + part // 2 + 1, (part % 2) * 256 : (part % 2 + 1) * 256] += column_sum(d_pre)
        d_normed = d_normed + mm_nt(d_pre, in_w[:, cols])
    unit_one = unit_one_ref[...]
    add(GAIN_ONE, column_sum(d_normed * unit_one))
    add(SHIFT_ONE, column_sum(d_normed))
    return norm_back(d_normed, unit_one, scale_one, vec[GAIN_ONE : GAIN_ONE + 1])


def attention_back(d_resid, qkv_ref, probs_ref, scales_ref, qkv_w, out_w, next_ref, d_mixed_ref, d_proj_ref, sums_ref, queries):
    seq_len, width = d_resid.shape
    head_dim = width // HEADS
    add = adder(sums_ref)
    d_proj = d_resid.astype(BF16)
    d_proj_ref[...] = d_proj
    add(OUT_B, column_sum(d_proj))
    d_context = mm_nt(d_proj, out_w[...])
    factor = head_dim**-0.5
    mask_a, mask_b = lane_masks(head_dim)
    queries[...] = qkv_ref[:, :width]
    keys = qkv_ref[:, width : 2 * width]
    k_t = (keys * jnp.asarray(factor, BF16)).T
    shares = scales_ref[:, 256 : 256 + HEADS]
    share_rows = shares.T
    d_query_parts = []
    first = lax.broadcasted_iota(jnp.int32, (seq_len, 2 * head_dim), 1) < head_dim

    def weight_gradients_of(pair):
        cols = slice(pair * 2 * head_dim, (pair + 1) * 2 * head_dim)
        v_cols = qkv_ref[:, slice(cols.start + 2 * width, cols.stop + 2 * width)]
        scale = jnp.where(first, shares[:, 2 * pair : 2 * pair + 1], shares[:, 2 * pair + 1 : 2 * pair + 2])
        scaled = (d_context[:, cols] * scale).astype(BF16)
        v_two = jnp.concatenate([v_cols * mask for mask in (mask_a, mask_b)], axis=0)
        return scaled, mm_nt(v_two, scaled)

    ahead = weight_gradients_of(0)
    for pair in range(HEADS // 2):
        scaled, d_probs = ahead
        if pair + 1 < HEADS // 2:
            ahead = weight_gradients_of(pair + 1)
        cols = slice(pair * 2 * head_dim, (pair + 1) * 2 * head_dim)
        rows = slice(pair * 2 * seq_len, (pair + 1) * 2 * seq_len)
        probs = probs_ref[rows, :]
        d_values = mm(probs, scaled)
        parts = []
        for side in range(2):
            half = slice(side * seq_len, (side + 1) * seq_len)
            head = 2 * pair + side
            probs_wide = probs[half].astype(F32)
            total = jnp.sum(probs_wide * d_probs[half], axis=0, keepdims=True) * share_rows[head : head + 1, :]
            d_scores = (probs_wide * (d_probs[half] - total)).astype(BF16)
            parts.append(d_scores)
            d_query_parts.append(mm(k_t[head * head_dim : (head + 1) * head_dim, :], d_scores))
        d_keys = mm(jnp.concatenate(parts, axis=0), queries[:, cols] * jnp.asarray(factor, BF16))
        d_mixed_ref[:, slice(cols.start + width, cols.stop + width)] = jnp.where(first, d_keys[:seq_len], d_keys[seq_len:]).astype(BF16)
        d_mixed_ref[:, slice(cols.start + 2 * width, cols.stop + 2 * width)] = jnp.where(
            first, d_values[:seq_len], d_values[seq_len:]
        ).astype(BF16)
    d_queries = jnp.concatenate(d_query_parts, axis=0).T.astype(BF16)
    d_mixed_ref[:, :width] = d_queries
    add(QV_B, column_sum(d_queries))
    add(QV_B + 1, column_sum(d_mixed_ref[:, 2 * width :]))
    d_input = d_resid + mm_nt(d_mixed_ref[...], qkv_w[...])
    next_ref[:seq_len, :] = d_input.astype(BF16)


def is_active(info, tick, stages):
    place = tick - 2 * info[0, 0]
    return (place >= 0) & (place < stages)


def backward_kernel(tick, stages, own, fresh_proj, fresh_sums, info, g_ref, *refs):
    refs = list(refs)
    own_ref = refs.pop(0) if own else None
    qkv_w, out_w, in_w, down_w, vec = refs[:5]
    qkv_ref, slope_ref, probs_ref, unit_one_ref, unit_two_ref, scales_ref = refs[5:11]
    refs = refs[11:]
    if not fresh_proj:
        refs = refs[2:]
    if not fresh_sums:
        refs = refs[1:]
    next_ref, d_mixed_ref, d_pre_ref, d_proj_ref, d_down_ref, sums_ref, queries, picked = refs
    seq_len = g_ref.shape[0] - EXTRA
    active = is_active(info, tick, stages)

    if own:

        @pl.when(info[0, 0] == stages - 1)
        def _():
            picked[...] = own_ref[...]

        @pl.when(info[0, 0] != stages - 1)
        def _():
            picked[...] = g_ref[...]

        g_ref = picked
    if fresh_sums:
        sums_ref[...] = jnp.zeros_like(sums_ref)

    @pl.when(active)
    def _():
        next_ref[seq_len:, :] = g_ref[seq_len:, :]
        d_resid = ffn_back(
            g_ref, slope_ref, unit_one_ref, unit_two_ref, scales_ref, in_w, down_w, vec, d_pre_ref, d_down_ref, sums_ref
        )
        attention_back(d_resid, qkv_ref, probs_ref, scales_ref, qkv_w, out_w, next_ref, d_mixed_ref, d_proj_ref, sums_ref, queries)


def last_ffn_kernel(
    tick, stages, info, g_ref, in_w, down_w, vec, slope_ref, unit_one_ref, unit_two_ref, scales_ref, d_down_in, sums_in,
    d_pre_ref, d_down_ref, sums_ref, d_resid_ref,
):
    @pl.when(is_active(info, tick, stages))
    def _():
        d_resid_ref[...] = ffn_back(
            g_ref, slope_ref, unit_one_ref, unit_two_ref, scales_ref, in_w, down_w, vec, d_pre_ref, d_down_ref, sums_ref
        )


def last_attention_kernel(
    tick, stages, info, d_resid_ref, qkv_w, out_w, probs_ref, scales_ref, qkv_ref, d_proj_in, sums_in,
    next_ref, d_mixed_ref, d_proj_ref, sums_ref, queries,
):
    @pl.when(is_active(info, tick, stages))
    def _():
        attention_back(d_resid_ref[...], qkv_ref, probs_ref, scales_ref, qkv_w, out_w, next_ref, d_mixed_ref, d_proj_ref, sums_ref, queries)


def half_of(info, theirs):
    return 1 - info[1, 0] if theirs else info[1, 0]


def outer(left, right, rows=None, cols=None):
    rows = slice(None) if rows is None else rows
    cols = slice(None) if cols is None else cols
    return sum(mm_tn(a[:, rows], b[:, cols]) for a, b in zip(left, right))


def down_weights(theirs, info, *refs):
    *refs, out_ref = refs
    hidden, d_down = refs[: len(refs) // 2], refs[len(refs) // 2 :]
    span = hidden[0].shape[1] // 2
    for start in range(0, span, BLOCK):
        at = pl.ds(pl.multiple_of(half_of(info, theirs) * span + start, BLOCK), BLOCK)
        out_ref[start : start + BLOCK, :] = outer(hidden, d_down, rows=at).astype(BF16)


def in_weights(theirs, info, *refs):
    *refs, out_ref = refs
    normed, d_pre = refs[: len(refs) // 2], refs[len(refs) // 2 :]
    width = normed[0].shape[1]
    span = d_pre[0].shape[1] // 2
    for part in range(span // BLOCK):
        at = pl.ds(pl.multiple_of(half_of(info, theirs) * span + part * BLOCK, BLOCK), BLOCK)
        out_ref[part * width : (part + 1) * width, :] = outer(normed, d_pre, cols=at).astype(BF16)


def attention_weights(theirs, info, *refs):
    *refs, sums_ref, out_ref = refs
    slots = len(refs) // 4
    x, context, d_mixed, d_proj = (refs[i * slots : (i + 1) * slots] for i in range(4))
    half = half_of(info, theirs)
    width = x[0].shape[1]
    span = width // 2
    at = pl.ds(pl.multiple_of(half * span, span), span)
    for part in range(3):
        cols = slice(part * width, (part + 1) * width)
        out_ref[part * span : (part + 1) * span, :] = outer(x, d_mixed, rows=at, cols=cols).astype(BF16)
    out_ref[3 * span : 4 * span, :] = outer(context, d_proj, rows=at).astype(BF16)
    out_ref[4 * span :, :] = jnp.zeros((out_ref.shape[0] - 4 * span, width), BF16)
    share = SMALL // 2
    out_ref[4 * span : 4 * span + share, :] = sums_ref[pl.ds(pl.multiple_of(half * share, share), share), :].astype(BF16)


def split_kernel(step, info, mine_ref, came_ref, keep_ref, send_ref):
    rows = keep_ref.shape[0]
    bit = info[2 + step, 0]
    for ref, side in ((send_ref, 1 - bit), (keep_ref, bit)):
        at = pl.ds(pl.multiple_of(side * rows, 16), rows)
        ref[...] = (mine_ref[at, :].astype(F32) + came_ref[at, :].astype(F32)).astype(BF16)


def add_kernel(mine_ref, came_ref, out_ref):
    out_ref[...] = (mine_ref[...].astype(F32) + came_ref[...].astype(F32)).astype(BF16)


def join_kernel(step, info, mine_ref, came_ref, out_ref):
    rows = mine_ref.shape[0]
    bit = info[2 + step, 0]
    out_ref[pl.ds(pl.multiple_of(bit * rows, 16), rows), :] = mine_ref[...]
    out_ref[pl.ds(pl.multiple_of((1 - bit) * rows, 16), rows), :] = came_ref[...]


def store_kernel(name, sides, known, info, *refs):
    parts = refs[: len(sides)]
    token, stage_ref, sems = refs[-3:]
    outs = refs[len(sides) + known : -3]
    token[...] = jnp.zeros_like(token)
    copies = []
    row = 0
    for theirs, part_ref in zip(sides, parts):
        half = half_of(info, theirs)
        width = part_ref.shape[1]
        targets = []
        if name == "down":
            span = outs[0].shape[1] // 2
            for start in range(0, span, BLOCK):
                targets.append((BLOCK, outs[0].at[0, pl.ds(pl.multiple_of(half * span + start, BLOCK), BLOCK), :]))
        elif name == "in":
            span = outs[0].shape[2] // 2
            for start in range(0, span, BLOCK):
                targets.append((width, outs[0].at[0, :, pl.ds(pl.multiple_of(half * span + start, BLOCK), BLOCK)]))
        else:
            span = width // 2
            at = pl.ds(pl.multiple_of(half * span, span), span)
            targets = [(span, outs[0].at[0, at, i * width : (i + 1) * width]) for i in range(3)] + [(span, outs[1].at[0, at, :])]
        start = 0
        for size, dst in targets:
            stage_ref[row : row + size, :] = part_ref[start : start + size, :].astype(F32)
            copies.append(pltpu.make_async_copy(stage_ref.at[row : row + size], dst, sems.at[len(copies)]))
            copies[-1].start()
            start += size
            row += size
    for copy in copies:
        copy.wait()


def small_store_kernel(
    start, info, mine_ref, came_ref, qv_b, out_b, gain_one, shift_one, in_b, down_b, gain_two, shift_two, head_w, head_b, token
):
    token[...] = jnp.zeros_like(token)
    share = SMALL // 2
    mine = mine_ref[start : start + share, :].astype(F32)
    came = came_ref[start : start + share, :].astype(F32)
    first = info[1, 0] == 0
    low = jnp.where(first, mine, came)
    high = jnp.where(first, came, mine)
    width = low.shape[1]
    row = 0
    for vector in (qv_b, out_b, gain_one, shift_one, in_b, down_b, gain_two, shift_two):
        for part in range(vector.shape[1] // width):
            vector[:, part * width : (part + 1) * width] = low[row : row + 1, :]
            row += 1
    classes, tasks, _ = head_w.shape
    for c in range(classes):
        head_w[c] = high[c * tasks : (c + 1) * tasks, :]
    line = high[classes * tasks : classes * tasks + 1, :128]
    lanes = lax.broadcasted_iota(jnp.int32, (16, 128), 1)
    spread = jnp.where(lanes % tasks == lax.broadcasted_iota(jnp.int32, (16, 128), 0), line, 0.0).astype(BF16)
    gather = (lax.broadcasted_iota(jnp.int32, (128, 128), 0) // tasks == lax.broadcasted_iota(jnp.int32, (128, 128), 1)).astype(BF16)
    head_b[...] = mm(spread, gather)[:tasks, :classes]


def relay_kernel(in_ref, out_ref):
    out_ref[...] = in_ref[...]


def pick_kernel(info, *refs):
    *grads, out_ref, token = refs
    token[...] = jnp.zeros_like(token)
    for s, grad in enumerate(grads):

        @pl.when(info[0, 0] == s)
        def _(grad=grad):
            out_ref[...] = grad[: out_ref.shape[0], :]


def shape(dims, dtype):
    return jax.ShapeDtypeStruct(dims, dtype)


def held(dims, dtype):
    return pltpu.VMEM(dims, dtype)


def near(array):
    return pltpu.with_memory_space_constraint(array, pltpu.VMEM)


def far(array):
    return pltpu.with_memory_space_constraint(array, pltpu.HBM)


def call(kernel, name, out_shape, args, in_specs, out_specs=None, aliases=None, scratch=(), flops=0, limit=LIMIT, after=()):
    single = not isinstance(out_shape, tuple)
    if out_specs is None:
        out_specs = VMEM if single else (VMEM,) * len(out_shape)
    count, extra = len(args), len(after)

    def body(*refs):
        kernel(*refs[:count], *refs[count + extra :])

    args = tuple(args) + tuple(near(a) for a in after)
    in_specs = list(in_specs) + [ANY] * extra
    return pl.pallas_call(
        body,
        out_shape=out_shape,
        in_specs=in_specs,
        out_specs=out_specs,
        scratch_shapes=scratch,
        input_output_aliases=aliases or {},
        compiler_params=pltpu.CompilerParams(vmem_limit_bytes=limit * MIB),
        cost_estimate=pl.CostEstimate(flops=flops, bytes_accessed=0, transcendentals=0),
        name=name,
    )(*args)


def piece(kernel, args, specs, out_shape, out_specs=None, aliases=None, scratch=()):
    return kernel, tuple(args), list(specs), tuple(out_shape), out_specs or (VMEM,) * len(out_shape), aliases or {}, list(scratch)


def fused(name, pieces, **rest):
    counts = [(len(args), len(outs), len(scratch)) for _, args, _, outs, _, _, scratch in pieces]
    sums = [sum(c[i] for c in counts) for i in range(3)]

    def kernel(*refs):
        ins, outs, scratch = refs[: sums[0]], refs[sums[0] : sums[0] + sums[1]], refs[sums[0] + sums[1] :]
        for (part, *_), (a, b, c) in zip(pieces, counts):
            part(*ins[:a], *outs[:b], *scratch[:c])
            ins, outs, scratch = ins[a:], outs[b:], scratch[c:]

    aliases = {}
    a = b = 0
    for (_, _, _, _, _, own, _), count in zip(pieces, counts):
        aliases |= {a + i: b + o for i, o in own.items()}
        a, b = a + count[0], b + count[1]
    results = call(
        kernel,
        name,
        sum((p[3] for p in pieces), ()),
        sum((p[1] for p in pieces), ()),
        sum((p[2] for p in pieces), []),
        sum((tuple(p[4]) for p in pieces), ()),
        aliases=aliases,
        scratch=sum((p[6] for p in pieces), []),
        **rest,
    )
    split = []
    for count in counts:
        split.append(results[: count[1]])
        results = results[count[1] :]
    return split


def local(
    hidden_in, segment_ids, task_ids, labels, cotangent, qkv_weight, qv_bias, out_weight, out_bias, norm1_gain, norm1_bias,
    ffn_in_weight, ffn_in_bias, ffn_out_weight, ffn_out_bias, norm2_gain, norm2_bias, head_weight, head_bias,
):
    stages = lax.axis_size("pipe")
    stage = lax.axis_index("pipe")
    shards = lax.axis_size("dp")
    shard = lax.axis_index("dp")
    _, seq_len, width = hidden_in.shape
    hidden_width = ffn_in_weight.shape[2]
    task_count, _, class_count = head_weight.shape
    block = (seq_len + EXTRA, width)

    bits = shards.bit_length() - 1
    upward = list(range(1, bits))
    orders = (upward, upward[::-1])
    core = shard & 1
    sides = [jnp.where(core == 0, (shard >> orders[0][j]) & 1, (shard >> orders[1][j]) & 1) for j in range(bits - 1)]
    info = jnp.stack([stage, core] + sides + [stage] * (6 - len(sides))).astype(jnp.int32)
    info = near(jnp.broadcast_to(info[:, None], (8, 128)))

    home, cot_block, vec, head_w = call(
        prepare_kernel,
        "prepare",
        (held(block, BF16), held(block, BF16), held((16, width), F32), held((16, width), F32)),
        tuple(
            far(a)
            for a in (
                hidden_in, cotangent, segment_ids, task_ids, labels, qv_bias, out_bias, norm1_gain, norm1_bias, ffn_in_bias, ffn_out_bias,
                norm2_gain, norm2_bias, head_weight.transpose(2, 0, 1),
            )
        ),
        [VMEM] * 14,
    )
    head_b = near(head_bias)
    weights = tuple(far(w) for w in (qkv_weight, out_weight, ffn_in_weight, ffn_out_weight)) + (near(vec),)
    weight_shapes = tuple(held(w.shape[1:], BF16) for w in weights[:4])

    def move(array, pairs):
        return lax.ppermute(array, "pipe", pairs)

    def route(tick):
        pairs = [(s, s + 1) for s in range(stages - 1) if 0 <= tick - 2 * s < stages]
        if tick + 2 < stages:
            pairs.append((tick + 2, 0))
        pairs += ADDED.get(tick, [])
        late = tick - 2 * (stages - 1)
        if 0 <= late < stages - 1:
            pairs.append((stages - 1, late))
        return pairs

    def back(tick):
        pairs = [(s + 1, s) for s in range(stages - 1) if 0 <= tick - 2 * s < stages]
        if tick + 2 < stages:
            pairs.append((0, tick + 2))
        return pairs

    ticks = 2 * (stages - 1) + stages
    saved_shapes = (
        held((seq_len, width), BF16),
        held((seq_len, 3 * width), BF16),
        held((HEADS * seq_len, seq_len), BF16),
        held((seq_len, width), BF16),
        held((seq_len, width), F32),
        held((seq_len, width), BF16),
        held((seq_len, hidden_width), BF16),
        held((seq_len, hidden_width), BF16),
        held((seq_len, width), F32),
        held((seq_len, 384), F32),
    )
    arrived = {0: home, 1: move(home, [(1, 0)])}
    slots = [None] * stages
    last = None
    own_heads, final_blocks = {}, {}

    def row_heads(final, cots, after=()):
        return call(
            partial(row_head_kernel, stages),
            "row_heads",
            held(block, BF16),
            [info, near(final), near(cots), head_b, near(head_w)],
            [VMEM] * 5,
            flops=HEADF,
            after=after,
        )

    for tick in range(ticks):
        carry = any(what != "came" for what in PASSED.get(tick, {}).values())
        fresh = slots[tick % stages] is None
        args = [info, near(arrived[tick])] + ([near(home), near(cot_block)] if carry else []) + list(weights)
        aliases = {}
        if not fresh:
            aliases = {len(args) + i: 1 + i for i in range(len(saved_shapes))}
            args += [near(a) for a in slots[tick % stages]]
        outs = call(
            partial(forward_kernel, tick, stages, carry, fresh),
            "layer_forward",
            (held(block, BF16),) + saved_shapes + (() if tick else weight_shapes),
            args,
            [ANY if a is w else VMEM for a in args for w in [next((w for w in weights[:4] if w is a and not tick), None)]],
            aliases=aliases,
            scratch=[] if tick else [pltpu.SemaphoreType.DMA((4,))],
            flops=4_000_000_000,
        )
        if tick == 0:
            weights = tuple(near(w) for w in outs[-4:]) + (near(vec),)
        slots[tick % stages] = tuple(outs[1:11])
        last = outs[0]
        if route(tick):
            arrived[tick + 2] = move(last, route(tick))
        if tick >= 2 * (stages - 1):
            final_blocks[tick] = last
    finals = [arrived[2 * (stages - 1) + 2 + s] for s in range(stages - 1)] + [last]
    own_heads[ticks - 1] = row_heads(last, cot_block)

    cots = {8: arrived[4], 7: arrived[5], 6: arrived[10]}
    arrived = {ticks - 1: own_heads[ticks - 1]}
    proj = [None] * stages
    sums = None
    results = {}
    for tick in reversed(range(1, ticks)):
        slot = tick % stages
        if tick in cots:
            own_heads[tick] = row_heads(final_blocks[tick], cots[tick], [last])
            arrived.setdefault(tick, own_heads[tick])
        own = tick in own_heads and tick < ticks - 2
        x, qkv, probs, context, unit_one, normed, hidden, slope, unit_two, scales = slots[slot]
        args = [info, near(arrived[tick])] + ([near(own_heads[tick])] if own else []) + list(weights)
        aliases = {len(args): 1, len(args) + 1: 2}
        args += [near(a) for a in (qkv, slope, probs, unit_one, unit_two, scales)]
        fresh_proj, fresh_sums = proj[slot] is None, sums is None
        if not fresh_proj:
            aliases |= {len(args): 3, len(args) + 1: 4}
            args += [near(a) for a in proj[slot]]
        if not fresh_sums:
            aliases |= {len(args): 5}
            args += [near(sums)]
        last, d_mixed, d_pre, d_proj, d_down, sums = call(
            partial(backward_kernel, tick, stages, own, fresh_proj, fresh_sums),
            "layer_backward",
            (
                held(block, BF16),
                held((seq_len, 3 * width), BF16),
                held((seq_len, hidden_width), BF16),
                held((seq_len, width), BF16),
                held((seq_len, width), BF16),
                held((SMALL, width), F32),
            ),
            args,
            [VMEM] + [VMEM] * (len(args) - 1),
            aliases=aliases,
            scratch=[pltpu.VMEM((seq_len, width), BF16), pltpu.VMEM(block, BF16)],
            flops=4_000_000_000,
        )
        proj[slot] = (d_proj, d_down)
        slots[slot] = (x, d_mixed, probs, context, unit_one, normed, hidden, d_pre, unit_two, scales)
        if tick >= 2:
            arrived[tick - 2] = move(last, back(tick - 2))
        if 2 <= tick < stages:
            results[tick] = arrived[tick - 2]

    def flip(bit):
        return [(i, i ^ (1 << bit)) for i in range(shards)]

    def across(step):
        return [(i, i ^ (1 << orders[i & 1][step])) for i in range(shards)]

    def swap(array, pairs):
        return lax.ppermute(array, "dp", pairs)

    second_last = last
    x, qkv, probs, context, unit_one, normed, hidden, slope, unit_two, scales = slots[0]
    qkv_w, out_w, in_w, down_w, vec = weights
    args = [info, near(arrived[0]), in_w, down_w, vec] + [near(a) for a in (slope, unit_one, unit_two, scales, proj[0][1], sums)]
    d_pre, d_down, sums, d_resid = call(
        partial(last_ffn_kernel, 0, stages),
        "last_ffn_backward",
        (held((seq_len, hidden_width), BF16), held((seq_len, width), BF16), held((SMALL, width), F32), held((seq_len, width), F32)),
        args,
        [VMEM] * len(args),
        aliases={5: 0, 9: 1, 10: 2},
    )
    LIGHT = 100_000_000
    tail = [d_resid]
    token = held((8, 128), F32)

    def run(name, *pieces, flops=10_000_000_000, **rest):
        split = fused(name, pieces, after=[tail[0]], flops=flops, **rest)
        tail[0] = split[-1][-1]
        return split

    unit = 16 * shards // 2
    half_hidden = hidden_width // 2
    small_start = 2 * width
    rows = {
        "down": half_hidden,
        "in": half_hidden * width // BLOCK,
        "attention": -(-(small_start + SMALL // 2) // unit) * unit,
    }
    mine, came = {}, {}

    def kept(index):
        return [near(slots[s][index]) for s in range(stages)]

    def products(p, theirs):
        if p == "down":
            kernel, arrays = down_weights, kept(6) + [near(d_down if s == 0 else proj[s][1]) for s in range(stages)]
        elif p == "in":
            kernel, arrays = in_weights, kept(5) + [near(d_pre if s == 0 else slots[s][7]) for s in range(stages)]
        else:
            kernel = attention_weights
            arrays = kept(0) + kept(3) + kept(1) + [near(proj[s][0]) for s in range(stages)] + [near(sums)]
        args = [info] + arrays
        return piece(partial(kernel, theirs), args, [VMEM] * len(args), (held((rows[p], width), BF16),))

    def split(p, step):
        out = held((mine[p].shape[0] // 2, width), BF16)
        ((mine[p], send),) = run("split_sum", flops=SPLIT, *(piece(partial(split_kernel, step), (info, near(mine[p]), near(came[p])), [VMEM] * 3, (out, out)),))
        came[p] = swap(send, across(step))

    def whole(p):
        ((mine[p],),) = run("last_sum", piece(add_kernel, (near(mine[p]), near(came[p])), [VMEM] * 2, (held(mine[p].shape, BF16),)), flops=WHOLE)
        came[p] = swap(mine[p], across(bits - 2))

    COST = {("attention", 1): J_A1, ("down", 0): J_D0, ("in", 0): J_I0, ("attention", 0): J_A0, ("down", 1): J_D1, ("in", 1): J_I1}

    def join(p, step, beside=()):
        out = held((2 * mine[p].shape[0], width), BF16)
        joined = piece(partial(join_kernel, step), (info, near(mine[p]), near(came[p])), [VMEM] * 3, (out,))
        *others, (mine[p],) = run("join", *beside, joined, flops=COST.get((p, step), HEAVY), limit=8)
        came[p] = swap(mine[p], across(step - 1) if step else flip(0))
        return others

    dims = {"down": ((1, hidden_width, width),), "in": ((1, width, hidden_width),), "attention": ((1, width, 3 * width), (1, width, width))}
    out_grads = {}

    def stored(p, sides):
        known = out_grads.get(p, ())
        parts = tuple(near(came[p] if theirs else mine[p]) for theirs in sides)
        args = (info,) + parts + tuple(far(g) for g in known)
        size = len(sides) * (2 * width if p == "attention" else rows[p])
        return piece(
            partial(store_kernel, p, sides, len(known)),
            args,
            [VMEM] * (1 + len(sides)) + [ANY] * len(known),
            tuple(pltpu.HBM(d, F32) for d in dims[p]) + (token,),
            (ANY,) * len(dims[p]) + (VMEM,),
            {1 + len(sides) + i: i for i in range(len(known))},
            [pltpu.VMEM((size, width), F32), pltpu.SemaphoreType.DMA((4 * len(sides),))],
        )

    ((theirs,),) = run("down_gradients", products("down", True), flops=LIGHT)
    came["down"] = swap(theirs, flip(0))
    (mine["down"],), (theirs,) = run("ffn_gradients", products("down", False), products("in", True), flops=LIGHT)
    came["in"] = swap(theirs, flip(0))
    split("down", 0)
    ((mine["in"],),) = run("in_gradients", products("in", False), flops=LIGHT)
    split("in", 0)
    args = [info, near(d_resid), qkv_w, out_w] + [near(a) for a in (probs, scales, qkv, proj[0][0], sums)]
    ((last, d_mixed, d_proj, sums),) = run(
        "last_attention_backward",
        piece(
            partial(last_attention_kernel, 0, stages),
            args,
            [VMEM] * len(args),
            (held(block, BF16), held((seq_len, 3 * width), BF16), held((seq_len, width), BF16), held((SMALL, width), F32)),
            aliases={6: 1, 7: 2, 8: 3},
            scratch=[pltpu.VMEM((seq_len, width), BF16)],
        ),
        flops=LIGHT,
    )
    results[0] = last
    results[1] = second_last
    slots[0] = (x, d_mixed) + slots[0][2:]
    proj[0] = (d_proj, d_down)
    (theirs,), (mine["attention"],) = run("attention_gradients", products("attention", True), products("attention", False), flops=LIGHT)
    came["attention"] = swap(theirs, flip(0))
    split("down", 1)
    split("attention", 0)
    ((results[1],),) = run("relay", piece(relay_kernel, (near(results[1]),), [VMEM], (held(block, BF16),)))
    results[1] = move(results[1], [(0, 1)])
    pick = piece(
        pick_kernel, [info] + [near(results[s]) for s in range(stages)], [VMEM] * (1 + stages), (shape((seq_len, width), BF16), token)
    )
    rows_out = piece(
        partial(loss_kernel, stages),
        [info, head_b] + [near(f) for f in finals] + [near(cot_block), near(head_w)],
        [VMEM] * (stages + 4),
        (shape((seq_len, width), BF16), shape(task_ids.shape, F32)),
        scratch=[pltpu.VMEM(block, BF16)],
    )
    moves = [partial(split, step=step) for step in range(1, bits - 1)] + [whole] + [partial(join, step=step) for step in reversed(range(bits - 1))]
    todo = {"in": moves[:-1], "down": moves[1:], "attention": moves[:-1]}
    while any(todo.values()):
        for p, steps in todo.items():
            if steps:
                steps.pop(0)(p)
                if p == "in" and len(steps) == PICK:
                    (hidden_out, losses), (hidden_grad, _) = run("pick_gradient", rows_out, pick)
    (((*out_grads["down"], _)),) = join("in", 0, [stored("down", (False, True))])
    (((*out_grads["in"], _)),) = run("store", stored("in", (False,)), flops=STORE)
    join("attention", 0)
    (*out_grads["in"], _), (*out_grads["attention"], _) = run(
        "store", stored("in", (True,)), stored("attention", (False,)), limit=8, flops=HEAVY
    )
    vectors = tuple(shape((1, n), F32) for n in (2 * width, width, width, width, hidden_width, width, width, width))
    small = piece(
        partial(small_store_kernel, small_start),
        [info, near(mine["attention"]), near(came["attention"])],
        [VMEM] * 3,
        vectors + (shape((class_count, task_count, width), F32), shape((task_count, class_count), F32), token),
    )
    (*out_grads["attention"], _), (*vectors, head_w_grad, head_b_grad, _) = run("store", stored("attention", (True,)), small)
    qv_grad, out_b_grad, gain_one_grad, shift_one_grad, in_b_grad, down_b_grad, gain_two_grad, shift_two_grad = vectors
    return (
        hidden_out[None],
        losses,
        hidden_grad[None],
        out_grads["attention"][0],
        qv_grad,
        out_grads["attention"][1],
        out_b_grad,
        gain_one_grad,
        shift_one_grad,
        out_grads["in"][0],
        in_b_grad,
        out_grads["down"][0],
        down_b_grad,
        gain_two_grad,
        shift_two_grad,
        head_w_grad.transpose(1, 2, 0),
        head_b_grad,
    )


def solution(mesh):
    rows = P(("dp", "pipe"), None, None)
    ids = P(("dp", "pipe"), None)
    big = P("pipe", None, None)
    vec = P("pipe", None)
    return jax.shard_map(
        local,
        mesh=mesh,
        in_specs=(rows, ids, ids, ids, rows, big, vec, big, vec, vec, vec, big, vec, big, vec, vec, vec, P(), P()),
        out_specs=(rows, ids, rows, big, vec, big, vec, vec, vec, big, vec, big, vec, vec, vec, P(), P()),
        check_vma=False,
    )
```
